32 devices in a mesh: groups: 2 (over y), row: 16 (over z, x, core).
Axes of the slice: x: 2, y: 2, z: 4, core: 2. Of those that a mesh axis runs over, the one named last changes fastest.
Arguments:
- decoder: bfloat16 [65536, 4096], P(('groups', 'row')), parts along dimension 0, may hold values from -130 to 130
- quarter: int32 [2], P('groups'), parts along dimension 0, may hold values from 0 to 3
Outputs:
- penalty: float32 [2], P('groups'), parts along dimension 0
- decoder_grad: float32 [65536, 4096], P(('groups', 'row')), parts along dimension 0
The draws below stay inside these ranges and needn't reach their ends.
There are 2 independent parts, one for each index of `groups`. The reference program is written for one: setup_inputs(seed, part) draws one part's arguments, and reference() takes and returns one part's arrays. A program takes and returns all parts, laid end to end along the dimension named above; each array names one. Nothing has to cross between parts.
All inputs are finite; a program needn't handle non-finite values.
Results may differ from the reference program's by a relative error of at most 0.0004.
The reference program's roundings to bfloat16 on the way (of `units`, `chosen` and `weighted`) count: a program that leaves them out, or rounds other values in their place, can miss the bound.
Values may be sent and summed in bfloat16 or wider, within the bound.
No kernel may reach another device: no remote copies, remote signals or barrier semaphores. Data moves between devices by JAX's collectives and lax.ppermute only.
A program may use at most 192 MiB of HBM per device.

```python
import math
import jax
import jax.numpy as jnp
from jax import lax

LATENTS = 32768
DW = 4096
ROWS = 256
QUARTER = 8192


def draw_decoder(key, part):
    key = jax.random.fold_in(key, 11)
    first, second = jax.random.split(key, 2)
    base = jnp.clip(jax.random.normal(first, (LATENTS, DW), jnp.float32), -6.0, 6.0)
    scales = jnp.exp(jax.random.uniform(second, (LATENTS, 1), jnp.float32, 0.0, math.log(10.0)))
    values = base * scales
    return values.astype(jnp.bfloat16)


def setup_inputs(seed: int = 0, part: int = 0) -> dict:
    key_list = jax.random.split(jax.random.key(seed), 3)
    part_splits = jax.random.split(jax.random.fold_in(key_list[2], part), 3)
    decoder = draw_decoder(jax.random.fold_in(jax.random.fold_in(key_list[2], part), 71), part)
    quarter = jax.random.randint(part_splits[1], (1,), 0, 4).astype(jnp.int32)
    return {"decoder": decoder, "quarter": quarter}


def reference(decoder, quarter):
    values = decoder.astype(jnp.float32)
    norms = jnp.sqrt(lax.optimization_barrier(jnp.sum(values * values, axis=1)) + 1e-06)
    directions = values / norms[:, None]
    units = directions.astype(jnp.bfloat16)
    start = (quarter[0] * QUARTER).astype(jnp.int32)
    chosen = lax.dynamic_slice_in_dim(units, start, ROWS, 0)
    cosines = jnp.dot(chosen, units.T, preferred_element_type=jnp.float32)
    row_ids = start + jnp.arange(ROWS, dtype=jnp.int32)
    col_ids = jnp.arange(LATENTS, dtype=jnp.int32)
    inside = (col_ids >= start) & (col_ids < start + ROWS)
    pair_weight = jnp.where(col_ids[None, :] == row_ids[:, None], jnp.float32(0.0), jnp.where(inside[None, :], jnp.float32(0.5), jnp.float32(1.0)))
    products = pair_weight * cosines
    weighted = products.astype(jnp.bfloat16)
    penalty = jnp.sum(products * cosines) * (DW / (ROWS * LATENTS))
    column_part = jnp.dot(weighted.T, chosen, preferred_element_type=jnp.float32)
    row_part = jnp.dot(weighted, units, preferred_element_type=jnp.float32)
    current = lax.dynamic_slice_in_dim(column_part, start, ROWS, 0)
    combined = lax.dynamic_update_slice_in_dim(column_part, current + row_part, start, 0)
    unit_grad = 2.0 * math.sqrt(DW) * combined
    along = lax.optimization_barrier(jnp.sum(unit_grad * directions, axis=1))
    decoder_grad = (unit_grad - along[:, None] * directions) / norms[:, None]
    return (jnp.reshape(penalty, (1,)).astype(jnp.float32), decoder_grad)
```

```python
import functools
import math

import jax
import jax.numpy as jnp
from jax import lax
from jax.experimental import pallas as pl
from jax.experimental.pallas import tpu as pltpu
from jax.sharding import PartitionSpec as P

DW = 4096
ROWS = 256
BLOCK = 256
HALF_CHUNKS = 4
VMEM_LIMIT = 56 * 1024 * 1024
NT = (((1,), (1,)), ((), ()))


def params():
    return pltpu.CompilerParams(vmem_limit_bytes=VMEM_LIMIT)


def unit_block(block):
    values = block.astype(jnp.float32)
    norms = jnp.sqrt(jnp.sum(values * values, axis=1, keepdims=True) + 1e-06)
    inverse = 1.0 / norms
    return (values * inverse).astype(jnp.bfloat16), inverse


def head_kernel(decoder_ref, *chunk_refs):
    units, _ = unit_block(decoder_ref[...])
    step = chunk_refs[0].shape[1]
    for k, ref in enumerate(chunk_refs):
        ref[...] = units[:, k * step : (k + 1) * step]


def units_kernel(decoder_ref, units_ref, inverse_ref):
    units, inverse = unit_block(decoder_ref[...])
    units_ref[...] = units
    inverse_ref[...] = jnp.broadcast_to(inverse, inverse_ref.shape)


def cosine_kernel(delta_ref, *refs):
    count = len(refs) - 4
    chunks = refs[:count]
    units_ref, by_row_ref, by_col_ref, penalty_ref = refs[count:]
    step = chunks[0].shape[1]
    j = pl.program_id(0)
    cosines = jnp.zeros((ROWS, BLOCK), jnp.float32)
    for k in range(count):
        cosines += lax.dot_general(
            chunks[k][...],
            units_ref[:, k * step : (k + 1) * step],
            NT,
            preferred_element_type=jnp.float32,
        )
    rows = lax.broadcasted_iota(jnp.int32, (ROWS, BLOCK), 0)
    cols = lax.broadcasted_iota(jnp.int32, (ROWS, BLOCK), 1)
    cols = cols + (delta_ref[0] + j * BLOCK)
    inside = (cols >= 0) & (cols < ROWS)
    weight = jnp.where(cols == rows, 0.0, jnp.where(inside, 0.5, 1.0))
    products = weight * cosines
    by_row_ref[...] = products.astype(jnp.bfloat16)
    by_col_ref[...] = products.T.astype(jnp.bfloat16)

    @pl.when(j == 0)
    def _():
        penalty_ref[...] = jnp.zeros_like(penalty_ref)

    squares = (products * cosines).reshape(ROWS // 8, 8, BLOCK // 128, 128)
    penalty_ref[...] += jnp.sum(squares, axis=(0, 2))


def row_kernel(by_row_ref, units_ref, out_ref):
    out_ref[...] = jnp.dot(
        by_row_ref[...], units_ref[...], preferred_element_type=jnp.float32
    )


def finish_block(column, decoder_ref, inverse_ref, out_ref):
    inverse = inverse_ref[:, :1]
    values = decoder_ref[...].astype(jnp.float32)
    along = jnp.sum(column[...] * values, axis=1, keepdims=True)
    scale = (2.0 * math.sqrt(DW)) * inverse
    back = scale * (along * inverse * inverse)
    out_ref[...] = scale * column[...] - back * values


def finish_kernel(count, by_col_ref, decoder_ref, inverse_ref, *refs):
    chunks = refs[:count]
    out_ref, column = refs[count:]
    step = chunks[0].shape[1]
    for k in range(count):
        column[:, k * step : (k + 1) * step] = jnp.dot(
            by_col_ref[...], chunks[k][...], preferred_element_type=jnp.float32
        )
    finish_block(column, decoder_ref, inverse_ref, out_ref)


def last_kernel(count, owner_ref, by_col_ref, decoder_ref, inverse_ref, *refs):
    chunks, sums = refs[:count], refs[count : 2 * count]
    out_ref, column = refs[-2:]
    step = chunks[0].shape[1]
    owner = owner_ref[0] == 1
    for k in range(count):
        part = jnp.dot(by_col_ref[...], chunks[k][...], preferred_element_type=jnp.float32)
        column[:, k * step : (k + 1) * step] = part + jnp.where(owner, sums[k][...], 0.0)
    finish_block(column, decoder_ref, inverse_ref, out_ref)


def on_device(decoder, quarter):
    shard, width = decoder.shape
    devices = lax.axis_size("row")
    index = lax.axis_index("row")
    per = devices // 4
    latents = shard * devices
    blocks = shard // BLOCK
    count = 2 * HALF_CHUNKS
    step = width // count
    chosen_quarter = quarter[0]
    start = chosen_quarter * (latents // 4)
    place = index // per
    within = index % per
    here = place == chosen_quarter
    smem = pl.BlockSpec(memory_space=pltpu.SMEM)

    def send(value, pairs):
        return lax.ppermute(value, "row", pairs)

    def hop(level, lanes):
        moves = (((0, 1), (3, 2)), ((1, 2), (2, 1)), ((2, 3), (1, 0)))[level]
        return [(a * per + w, b * per + w) for a, b in moves for w in lanes]

    def each(moves):
        return [(z * per + a, z * per + b) for z in range(4) for a, b in moves]

    own = pl.pallas_call(
        head_kernel,
        grid=(1,),
        in_specs=[pl.BlockSpec((ROWS, width), lambda i: (0, 0))],
        out_specs=[pl.BlockSpec((ROWS, step), lambda i: (0, 0))] * count,
        out_shape=[jax.ShapeDtypeStruct((ROWS, step), jnp.bfloat16)] * count,
        compiler_params=params(),
        name="head_units",
    )(decoder)

    units, inverse = pl.pallas_call(
        units_kernel,
        grid=(blocks,),
        in_specs=[pl.BlockSpec((BLOCK, width), lambda i: (i, 0))],
        out_specs=[
            pl.BlockSpec((BLOCK, width), lambda i: (i, 0)),
            pl.BlockSpec((BLOCK, 128), lambda i: (i, 0)),
        ],
        out_shape=[
            jax.ShapeDtypeStruct((shard, width), jnp.bfloat16),
            jax.ShapeDtypeStruct((shard, 128), jnp.float32),
        ],
        compiler_params=params(),
        cost_estimate=pl.CostEstimate(
            flops=4 * shard * width, bytes_accessed=4 * shard * width, transcendentals=0
        ),
        name="units",
    )(decoder)

    chosen = [None] * count
    for k in range(HALF_CHUNKS):
        across = send(own[k + HALF_CHUNKS], each([(0, 2)]))
        mine = jnp.where(within == 2, across, own[k])
        first = send(mine, hop(0, (0, 2)))
        second = send(jnp.where(here, mine, first), hop(1, (0, 2)))
        third = send(jnp.where(here, mine, second), hop(2, (0, 2)))
        near = jnp.where(place == 1, chosen_quarter == 0, chosen_quarter == 3)
        middle = (place == 1) | (place == 2)
        held = jnp.where(
            here, mine, jnp.where(middle, jnp.where(near, first, second), third)
        )
        other = send(held, each([(0, 2), (2, 0)]))
        core_held = send(held, each([(0, 1), (2, 3)]))
        core_other = send(other, each([(0, 1), (2, 3)]))
        odd = (within % 2) == 1
        low = (within // 2) % 2 == 0
        one = jnp.where(odd, core_held, held)
        two = jnp.where(odd, core_other, other)
        chosen[k] = jnp.where(low, one, two)
        chosen[k + HALF_CHUNKS] = jnp.where(low, two, one)
        far = 4
        while far < per:
            moves = each([(w, w + far) for w in range(far)])
            fresh = (within >= far) & (within < 2 * far)
            for c in (k, k + HALF_CHUNKS):
                chosen[c] = jnp.where(fresh, send(chosen[c], moves), chosen[c])
            far *= 2

    delta = jnp.reshape(index * shard - start, (1,)).astype(jnp.int32)
    whole_chunk = pl.BlockSpec((ROWS, step), lambda i: (0, 0))
    by_row, by_col, local_penalty = pl.pallas_call(
        cosine_kernel,
        grid=(blocks,),
        in_specs=[smem]
        + [whole_chunk] * count
        + [pl.BlockSpec((BLOCK, width), lambda i: (i, 0))],
        out_specs=[
            pl.BlockSpec((ROWS, BLOCK), lambda i: (0, i)),
            pl.BlockSpec((BLOCK, ROWS), lambda i: (i, 0)),
            pl.BlockSpec((8, 128), lambda i: (0, 0)),
        ],
        out_shape=[
            jax.ShapeDtypeStruct((ROWS, shard), jnp.bfloat16),
            jax.ShapeDtypeStruct((shard, ROWS), jnp.bfloat16),
            jax.ShapeDtypeStruct((8, 128), jnp.float32),
        ],
        compiler_params=params(),
        cost_estimate=pl.CostEstimate(
            flops=2 * ROWS * shard * width, bytes_accessed=2 * shard * width, transcendentals=0
        ),
        name="cosines",
    )(delta, *chosen, units)

    penalties = lax.all_gather(local_penalty, "row", axis=0, tiled=True)

    row_parts = []
    for k in range(count):
        row_parts.append(
            pl.pallas_call(
                row_kernel,
                grid=(1,),
                in_specs=[
                    pl.BlockSpec((ROWS, shard), lambda i: (0, 0)),
                    pl.BlockSpec((shard, step), lambda i, k=k: (0, k)),
                ],
                out_specs=pl.BlockSpec((ROWS, step), lambda i: (0, 0)),
                out_shape=jax.ShapeDtypeStruct((ROWS, step), jnp.float32),
                compiler_params=params(),
                cost_estimate=pl.CostEstimate(
                    flops=2 * ROWS * shard * step,
                    bytes_accessed=2 * shard * step,
                    transcendentals=0,
                ),
                name="row_part",
            )(by_row, units)
        )

    sums = [None] * count
    for k in range(HALF_CHUNKS):
        pair = []
        for c in (k, k + HALF_CHUNKS):
            value = row_parts[c]
            far = per // 2
            while far >= 4:
                value = value + send(value, each([(w + far, w) for w in range(far)]))
                far //= 2
            pair.append(value + send(value, each([(1, 0), (3, 2)])))
        low = within == 0
        away = jnp.where(low, pair[1], pair[0])
        held = jnp.where(low, pair[0], pair[1]) + send(away, each([(0, 2), (2, 0)]))
        first = send(held, hop(0, (0, 2)))
        second = send(held + first, hop(1, (0, 2)))
        third = send(held + second, hop(2, (0, 2)))
        total = held + first + second + third
        sums[k] = total
        sums[k + HALF_CHUNKS] = send(total, each([(2, 0)]))

    out_type = jax.ShapeDtypeStruct((shard, width), jnp.float32)
    scratch = [pltpu.VMEM((BLOCK, width), jnp.float32)]

    def block_specs(first_block):
        return [
            pl.BlockSpec((BLOCK, ROWS), lambda i: (i + first_block, 0)),
            pl.BlockSpec((BLOCK, width), lambda i: (i + first_block, 0)),
            pl.BlockSpec((BLOCK, 128), lambda i: (i + first_block, 0)),
        ]

    grad = None
    if blocks > 1:
        grad = pl.pallas_call(
            functools.partial(finish_kernel, count),
            grid=(blocks - 1,),
            in_specs=block_specs(1) + [whole_chunk] * count,
            out_specs=pl.BlockSpec((BLOCK, width), lambda i: (i + 1, 0)),
            out_shape=out_type,
            scratch_shapes=scratch,
            compiler_params=params(),
            cost_estimate=pl.CostEstimate(
                flops=2 * ROWS * shard * width,
                bytes_accessed=6 * shard * width,
                transcendentals=0,
            ),
            name="finish",
        )(by_col, decoder, inverse, *chosen)

    owner = jnp.reshape(here & (within == 0), (1,)).astype(jnp.int32)
    operands = [owner, by_col, decoder, inverse, *chosen, *sums]
    specs = [smem] + block_specs(0) + [whole_chunk] * (2 * count)
    aliases = {}
    body = functools.partial(last_kernel, count)
    if grad is not None:
        aliases = {len(operands): 0}
        operands.append(grad)
        specs.append(pl.BlockSpec(memory_space=pl.ANY))
    decoder_grad = pl.pallas_call(
        body,
        grid=(1,),
        in_specs=specs,
        out_specs=pl.BlockSpec((BLOCK, width), lambda i: (0, 0)),
        out_shape=out_type,
        scratch_shapes=scratch,
        input_output_aliases=aliases,
        compiler_params=params(),
        name="finish_rows",
    )(*operands)

    penalty = jnp.sum(penalties) * (DW / (ROWS * latents))
    return (jnp.reshape(penalty, (1,)), decoder_grad)


def solution(mesh):
    in_specs = (P(("groups", "row"), None), P("groups"))
    out_specs = (P("groups"), P(("groups", "row"), None))
    return jax.shard_map(
        on_device, mesh=mesh, in_specs=in_specs, out_specs=out_specs, check_vma=False
    )
```

```python
import functools
import math

import jax
import jax.numpy as jnp
from jax import lax
from jax.experimental import pallas as pl
from jax.experimental.pallas import tpu as pltpu
from jax.sharding import PartitionSpec as P

DW = 4096
ROWS = 256
BLOCK = 256
WIDE = 512
PAIRS = 2
COUNT = 2 * PAIRS
VMEM_LIMIT = 32 * 1024 * 1024
NT = (((1,), (1,)), ((), ()))


def params():
    return pltpu.CompilerParams(vmem_limit_bytes=VMEM_LIMIT)


def cost(flops, moved):
    return pl.CostEstimate(flops=flops, bytes_accessed=moved, transcendentals=0)


def strip_inverse(ref, rows):
    width = ref.shape[1]
    total = None
    for t in range(0, width, 128):
        v = ref[rows, t : t + 128].astype(jnp.float32)
        total = v * v if total is None else total + v * v
    return 1.0 / jnp.sqrt(jnp.sum(total, axis=1, keepdims=True) + 1e-06)


def head_kernel(decoder_ref, *chunk_refs):
    step = chunk_refs[0].shape[1]
    rows = slice(0, decoder_ref.shape[0])
    inverse = strip_inverse(decoder_ref, rows)
    for k, ref in enumerate(chunk_refs):
        for t in range(0, step, 128):
            v = decoder_ref[rows, k * step + t : k * step + t + 128].astype(jnp.float32)
            ref[rows, t : t + 128] = (v * inverse).astype(jnp.bfloat16)


def units_kernel(decoder_ref, units_ref, inverse_ref):
    strip = 64

    def body(s, carry):
        rows = pl.ds(pl.multiple_of(s * strip, strip), strip)
        inverse = strip_inverse(decoder_ref, rows)
        inverse_ref[rows, :] = jnp.broadcast_to(inverse, (strip, 128))
        for t in range(0, decoder_ref.shape[1], 128):
            v = decoder_ref[rows, t : t + 128].astype(jnp.float32)
            units_ref[rows, t : t + 128] = (v * inverse).astype(jnp.bfloat16)
        return carry

    lax.fori_loop(0, decoder_ref.shape[0] // strip, body, 0)


def pair_cosines(units_ref, low_ref, high_ref):
    step = low_ref.shape[1]
    low = lax.dot_general(
        units_ref[:, :step], low_ref[...], NT, preferred_element_type=jnp.float32
    )
    high = lax.dot_general(
        units_ref[:, step:], high_ref[...], NT, preferred_element_type=jnp.float32
    )
    return low + high


def partial_kernel(units_ref, low_ref, high_ref, out_ref):
    out_ref[...] = pair_cosines(units_ref, low_ref, high_ref)


def weight_kernel(
    delta_ref, units_ref, low_ref, high_ref, partial_ref, col_ref, row_ref, along_ref, penalty_ref
):
    size = units_ref.shape[0]
    j = pl.program_id(0)
    cosines = partial_ref[...] + pair_cosines(units_ref, low_ref, high_ref)
    latents = lax.broadcasted_iota(jnp.int32, (size, ROWS), 0) + (delta_ref[0] + j * size)
    rows = lax.broadcasted_iota(jnp.int32, (size, ROWS), 1)
    inside = (latents >= 0) & (latents < ROWS)
    weight = jnp.where(latents == rows, 0.0, jnp.where(inside, 0.5, 1.0))
    products = weight * cosines
    weighted = products.astype(jnp.bfloat16)
    col_ref[...] = weighted
    row_ref[...] = products.T.astype(jnp.bfloat16)
    along = jnp.sum(weighted.astype(jnp.float32) * cosines, axis=1, keepdims=True)
    along_ref[...] = jnp.broadcast_to(along, along_ref.shape)

    @pl.when(j == 0)
    def _():
        penalty_ref[...] = jnp.zeros_like(penalty_ref)

    squares = products * cosines
    squares = squares[:, :128] + squares[:, 128:]
    penalty_ref[...] += jnp.sum(squares.reshape(size // 8, 8, 128), axis=0)


def row_kernel(row_ref, units_ref, out_ref):
    out_ref[...] = jnp.dot(row_ref[...], units_ref[...], preferred_element_type=jnp.float32)


def finish_kernel(col_ref, decoder_ref, inverse_ref, along_ref, *refs):
    chunks, out_ref = refs[:COUNT], refs[-1]
    step = chunks[0].shape[1]
    inverse = inverse_ref[:, :1]
    scale = (2.0 * math.sqrt(DW)) * inverse
    back = scale * (along_ref[:, :1] * inverse)
    for k in range(COUNT):
        span = slice(k * step, (k + 1) * step)
        part = jnp.dot(col_ref[...], chunks[k][...], preferred_element_type=jnp.float32)
        out_ref[:, span] = scale * part - back * decoder_ref[:, span].astype(jnp.float32)


def last_kernel(owner_ref, col_ref, decoder_ref, inverse_ref, *refs):
    chunks, sums = refs[:COUNT], refs[COUNT : 2 * COUNT]
    out_ref, column = refs[-2:]
    step = chunks[0].shape[1]
    owner = owner_ref[0] == 1
    total = jnp.zeros((col_ref.shape[0], 128), jnp.float32)
    for k in range(COUNT):
        span = slice(k * step, (k + 1) * step)
        part = jnp.dot(col_ref[...], chunks[k][...], preferred_element_type=jnp.float32)
        part = part + jnp.where(owner, sums[k][...], 0.0)
        column[:, span] = part
        along = part * decoder_ref[:, span].astype(jnp.float32)
        for t in range(0, step, 128):
            total = total + along[:, t : t + 128]
    inverse = inverse_ref[:, :1]
    scale = (2.0 * math.sqrt(DW)) * inverse
    back = scale * (jnp.sum(total, axis=1, keepdims=True) * inverse * inverse)
    for k in range(COUNT):
        span = slice(k * step, (k + 1) * step)
        out_ref[:, span] = scale * column[:, span] - back * decoder_ref[:, span].astype(
            jnp.float32
        )


def on_device(decoder, quarter):
    shard, width = decoder.shape
    devices = lax.axis_size("row")
    index = lax.axis_index("row")
    per = devices // 4
    latents = shard * devices
    blocks = shard // BLOCK
    wide = min(WIDE, shard)
    step = width // COUNT
    chosen_quarter = quarter[0]
    start = chosen_quarter * (latents // 4)
    place = index // per
    within = index % per
    here = place == chosen_quarter
    even_chip = (within // 2) % 2 == 0
    odd_core = (within % 2) == 1
    smem = pl.BlockSpec(memory_space=pltpu.SMEM)

    def send(value, pairs):
        return lax.ppermute(value, "row", pairs)

    def hop(level):
        moves = (((0, 1), (3, 2)), ((1, 2), (2, 1)), ((2, 3), (1, 0)))[level]
        return [(a * per + w, b * per + w) for a, b in moves for w in (0, 2)]

    def each(moves):
        return [(z * per + a, z * per + b) for z in range(4) for a, b in moves]

    own = pl.pallas_call(
        head_kernel,
        grid=(4,),
        in_specs=[pl.BlockSpec((ROWS // 4, width), lambda i: (i, 0))],
        out_specs=[pl.BlockSpec((ROWS // 4, step), lambda i: (i, 0))] * COUNT,
        out_shape=[jax.ShapeDtypeStruct((ROWS, step), jnp.bfloat16)] * COUNT,
        compiler_params=params(),
        cost_estimate=cost(4 * ROWS * width, 4 * ROWS * width),
        name="head_units",
    )(decoder)

    units, inverse = pl.pallas_call(
        units_kernel,
        grid=(blocks,),
        in_specs=[pl.BlockSpec((BLOCK, width), lambda i: (i, 0))],
        out_specs=[
            pl.BlockSpec((BLOCK, width), lambda i: (i, 0)),
            pl.BlockSpec((BLOCK, 128), lambda i: (i, 0)),
        ],
        out_shape=[
            jax.ShapeDtypeStruct((shard, width), jnp.bfloat16),
            jax.ShapeDtypeStruct((shard, 128), jnp.float32),
        ],
        compiler_params=params(),
        cost_estimate=cost(4 * shard * width, 4 * shard * width),
        name="units",
    )(decoder)

    near = jnp.where(place == 1, chosen_quarter == 0, chosen_quarter == 3)
    middle = (place == 1) | (place == 2)
    takes = (within == 2) & (inverse[0, 0] > 0)
    mine, first, second, third, held = ([None] * PAIRS for _ in range(5))
    for k in range(PAIRS):
        across = send(own[2 * k + 1], each([(0, 2)]))
        mine[k] = jnp.where(takes, across, own[2 * k])
        first[k] = send(mine[k], hop(0))
        second[k] = send(jnp.where(here, mine[k], first[k]), hop(1))
        third[k] = send(jnp.where(here, mine[k], second[k]), hop(2))
        inner = jnp.where(near, first[k], second[k])
        held[k] = jnp.where(here, mine[k], jnp.where(middle, inner, third[k]))
    chosen = []
    for k in range(PAIRS):
        other = send(held[k], each([(0, 2), (2, 0)]))
        core_held = send(held[k], each([(0, 1), (2, 3)]))
        core_other = send(other, each([(0, 1), (2, 3)]))
        one = jnp.where(odd_core, core_held, held[k])
        two = jnp.where(odd_core, core_other, other)
        pair = [jnp.where(even_chip, one, two), jnp.where(even_chip, two, one)]
        far = 4
        while far < per:
            moves = each([(w, w + far) for w in range(far)])
            fresh = (within >= far) & (within < 2 * far)
            pair = [jnp.where(fresh, send(value, moves), value) for value in pair]
            far *= 2
        chosen += pair

    delta = jnp.reshape(index * shard - start, (1,)).astype(jnp.int32)
    whole_chunk = pl.BlockSpec((ROWS, step), lambda i: (0, 0))
    half_flops = ROWS * shard * width
    partial = None
    for k in range(PAIRS):
        unit_spec = pl.BlockSpec((wide, 2 * step), lambda i, k=k: (i, k))
        wide_spec = pl.BlockSpec((wide, ROWS), lambda i: (i, 0))
        if k < PAIRS - 1:
            partial = pl.pallas_call(
                partial_kernel,
                grid=(shard // wide,),
                in_specs=[unit_spec, whole_chunk, whole_chunk],
                out_specs=wide_spec,
                out_shape=jax.ShapeDtypeStruct((shard, ROWS), jnp.float32),
                compiler_params=params(),
                cost_estimate=cost(half_flops, shard * width),
                name="part_cosines",
            )(units, chosen[2 * k], chosen[2 * k + 1])
            continue
        by_col, by_row, along, local_penalty = pl.pallas_call(
            weight_kernel,
            grid=(shard // wide,),
            in_specs=[smem, unit_spec, whole_chunk, whole_chunk, wide_spec],
            out_specs=[
                wide_spec,
                pl.BlockSpec((ROWS, wide), lambda i: (0, i)),
                pl.BlockSpec((wide, 128), lambda i: (i, 0)),
                pl.BlockSpec((8, 128), lambda i: (0, 0)),
            ],
            out_shape=[
                jax.ShapeDtypeStruct((shard, ROWS), jnp.bfloat16),
                jax.ShapeDtypeStruct((ROWS, shard), jnp.bfloat16),
                jax.ShapeDtypeStruct((shard, 128), jnp.float32),
                jax.ShapeDtypeStruct((8, 128), jnp.float32),
            ],
            compiler_params=params(),
            cost_estimate=cost(half_flops, shard * width),
            name="weights",
        )(delta, units, chosen[2 * k], chosen[2 * k + 1], partial)

    sums = [None] * COUNT
    for k in range(PAIRS):
        value = pl.pallas_call(
            row_kernel,
            grid=(4,),
            in_specs=[
                pl.BlockSpec((ROWS, shard), lambda i: (0, 0)),
                pl.BlockSpec((shard, step // 2), lambda i, k=k: (0, 4 * k + i)),
            ],
            out_specs=pl.BlockSpec((ROWS, step // 2), lambda i: (0, i)),
            out_shape=jax.ShapeDtypeStruct((ROWS, 2 * step), jnp.float32),
            compiler_params=params(),
            cost_estimate=cost(half_flops, shard * width),
            name="row_part",
        )(by_row, units)
        far = per // 2
        while far >= 4:
            value = value + send(value, each([(w + far, w) for w in range(far)]))
            far //= 2
        value = value + send(value, each([(1, 0), (3, 2)]))
        low, high = value[:, :step], value[:, step:]
        away = jnp.where(even_chip, high, low)
        kept = jnp.where(even_chip, low, high)
        kept = kept + send(away, each([(0, 2), (2, 0)]))
        first_sum = send(kept, hop(0))
        second_sum = send(kept + first_sum, hop(1))
        third_sum = send(kept + second_sum, hop(2))
        total = kept + first_sum + second_sum + third_sum
        sums[2 * k] = total
        sums[2 * k + 1] = send(total, each([(2, 0)]))

    penalties = local_penalty
    far = 1
    while far < devices:
        swap = [(i, i ^ far) for i in range(devices)]
        penalties = penalties + send(penalties, swap)
        far *= 2
    penalty = jnp.sum(penalties) * (DW / (ROWS * latents))

    out_type = jax.ShapeDtypeStruct((shard, width), jnp.float32)
    any_spec = pl.BlockSpec(memory_space=pl.ANY)
    grad = None
    bounds = [1, 1 + (blocks - 1) // 2, blocks] if blocks > 2 else [1, blocks]
    for low, high in zip(bounds[:-1], bounds[1:]):
        if high == low:
            continue
        operands = [by_col, decoder, inverse, along, *chosen]
        specs = [
            pl.BlockSpec((BLOCK, ROWS), lambda i, low=low: (i + low, 0)),
            pl.BlockSpec((BLOCK, width), lambda i, low=low: (i + low, 0)),
            pl.BlockSpec((BLOCK, 128), lambda i, low=low: (i + low, 0)),
            pl.BlockSpec((BLOCK, 128), lambda i, low=low: (i + low, 0)),
        ] + [whole_chunk] * COUNT
        aliases = {}
        if grad is not None:
            aliases = {len(operands): 0}
            operands.append(grad)
            specs.append(any_spec)
        rows = (high - low) * BLOCK
        grad = pl.pallas_call(
            finish_kernel,
            grid=(high - low,),
            in_specs=specs,
            out_specs=pl.BlockSpec((BLOCK, width), lambda i, low=low: (i + low, 0)),
            out_shape=out_type,
            input_output_aliases=aliases,
            compiler_params=params(),
            cost_estimate=cost(2 * ROWS * rows * width, 6 * rows * width),
            name="finish",
        )(*operands)

    owner = jnp.reshape(here & (within == 0), (1,)).astype(jnp.int32)
    narrow = BLOCK // 2
    operands = [owner, by_col, decoder, inverse, *chosen, *sums]
    specs = [
        smem,
        pl.BlockSpec((narrow, ROWS), lambda i: (i, 0)),
        pl.BlockSpec((narrow, width), lambda i: (i, 0)),
        pl.BlockSpec((narrow, 128), lambda i: (i, 0)),
    ]
    specs += [whole_chunk] * COUNT
    specs += [pl.BlockSpec((narrow, step), lambda i: (i, 0))] * COUNT
    aliases = {}
    if grad is not None:
        aliases = {len(operands): 0}
        operands.append(grad)
        specs.append(any_spec)
    decoder_grad = pl.pallas_call(
        last_kernel,
        grid=(2,),
        in_specs=specs,
        out_specs=pl.BlockSpec((narrow, width), lambda i: (i, 0)),
        out_shape=out_type,
        scratch_shapes=[pltpu.VMEM((narrow, width), jnp.float32)],
        input_output_aliases=aliases,
        compiler_params=params(),
        name="finish_rows",
    )(*operands)

    return (jnp.reshape(penalty, (1,)), decoder_grad)


def solution(mesh):
    in_specs = (P(("groups", "row"), None), P("groups"))
    out_specs = (P("groups"), P(("groups", "row"), None))
    return jax.shard_map(
        on_device, mesh=mesh, in_specs=in_specs, out_specs=out_specs, check_vma=False
    )
```

```python
import functools
import math

import jax
import jax.numpy as jnp
from jax import lax
from jax.experimental import pallas as pl
from jax.experimental.pallas import tpu as pltpu
from jax.sharding import PartitionSpec as P

DW = 4096
ROWS = 256
BLOCK = 256
WIDE = 512
PAIRS = 2
COUNT = 2 * PAIRS
VMEM_LIMIT = 48 * 1024 * 1024
NT = (((1,), (1,)), ((), ()))


def params():
    return pltpu.CompilerParams(vmem_limit_bytes=VMEM_LIMIT)


def cost(flops, moved):
    return pl.CostEstimate(flops=flops, bytes_accessed=moved, transcendentals=0)


def strip_inverse(ref, rows):
    width = ref.shape[1]
    total = None
    for t in range(0, width, 128):
        v = ref[rows, t : t + 128].astype(jnp.float32)
        total = v * v if total is None else total + v * v
    return 1.0 / jnp.sqrt(jnp.sum(total, axis=1, keepdims=True) + 1e-06)


def head_kernel(decoder_ref, *chunk_refs):
    step = chunk_refs[0].shape[1]
    rows = slice(0, decoder_ref.shape[0])
    inverse = strip_inverse(decoder_ref, rows)
    for k, ref in enumerate(chunk_refs):
        for t in range(0, step, 128):
            v = decoder_ref[rows, k * step + t : k * step + t + 128].astype(jnp.float32)
            ref[rows, t : t + 128] = (v * inverse).astype(jnp.bfloat16)


def units_kernel(decoder_ref, units_ref, inverse_ref):
    strip = 64

    def body(s, carry):
        rows = pl.ds(pl.multiple_of(s * strip, strip), strip)
        inverse = strip_inverse(decoder_ref, rows)
        inverse_ref[rows, :] = jnp.broadcast_to(inverse, (strip, 128))
        for t in range(0, decoder_ref.shape[1], 128):
            v = decoder_ref[rows, t : t + 128].astype(jnp.float32)
            units_ref[rows, t : t + 128] = (v * inverse).astype(jnp.bfloat16)
        return carry

    lax.fori_loop(0, decoder_ref.shape[0] // strip, body, 0)


def pair_cosines(units_ref, low_ref, high_ref):
    step = low_ref.shape[1]
    low = lax.dot_general(
        units_ref[:, :step], low_ref[...], NT, preferred_element_type=jnp.float32
    )
    high = lax.dot_general(
        units_ref[:, step:], high_ref[...], NT, preferred_element_type=jnp.float32
    )
    return low + high


def partial_kernel(units_ref, low_ref, high_ref, out_ref):
    out_ref[...] = pair_cosines(units_ref, low_ref, high_ref)


def weight_kernel(
    delta_ref, units_ref, low_ref, high_ref, partial_ref, col_ref, row_ref, along_ref, penalty_ref
):
    size = units_ref.shape[0]
    j = pl.program_id(0)
    cosines = partial_ref[...] + pair_cosines(units_ref, low_ref, high_ref)
    latents = lax.broadcasted_iota(jnp.int32, (size, ROWS), 0) + (delta_ref[0] + j * size)
    rows = lax.broadcasted_iota(jnp.int32, (size, ROWS), 1)
    inside = (latents >= 0) & (latents < ROWS)
    weight = jnp.where(latents == rows, 0.0, jnp.where(inside, 0.5, 1.0))
    products = weight * cosines
    weighted = products.astype(jnp.bfloat16)
    col_ref[...] = weighted
    row_ref[...] = products.T.astype(jnp.bfloat16)
    along = jnp.sum(weighted.astype(jnp.float32) * cosines, axis=1, keepdims=True)
    along_ref[...] = jnp.broadcast_to(along, along_ref.shape)

    @pl.when(j == 0)
    def _():
        penalty_ref[...] = jnp.zeros_like(penalty_ref)

    squares = products * cosines
    squares = squares[:, :128] + squares[:, 128:]
    penalty_ref[...] += jnp.sum(squares.reshape(size // 8, 8, 128), axis=0)


def row_kernel(row_ref, units_ref, out_ref):
    out_ref[...] = jnp.dot(row_ref[...], units_ref[...], preferred_element_type=jnp.float32)


def finish_kernel(col_ref, decoder_ref, inverse_ref, along_ref, *refs):
    chunks = refs[:COUNT]
    out_ref, mark_ref = refs[-2:]
    step = chunks[0].shape[1]
    inverse = inverse_ref[:, :1]
    scale = (2.0 * math.sqrt(DW)) * inverse
    back = scale * (along_ref[:, :1] * inverse)
    for k in range(COUNT):
        span = slice(k * step, (k + 1) * step)
        part = jnp.dot(col_ref[...], chunks[k][...], preferred_element_type=jnp.float32)
        out_ref[:, span] = scale * part - back * decoder_ref[:, span].astype(jnp.float32)
    mark_ref[...] = jnp.zeros_like(mark_ref)


STEPS = 32000.0


def encode(value, msg_ref):
    size = value.shape[1]
    top = jnp.max(jnp.abs(value), axis=1, keepdims=True)
    power = jnp.ceil(jnp.log2(jnp.maximum(top, 1e-35)) * 8.0)
    ratio = value * jnp.exp2(power * -0.125)
    coded = ratio * lax.rsqrt(jnp.maximum(jnp.abs(ratio), 1e-30))
    coded = jnp.round(coded * STEPS).astype(jnp.int32)
    msg_ref[:, :size] = coded.astype(jnp.int16)
    power = jnp.broadcast_to(power.astype(jnp.int32), (value.shape[0], 128))
    msg_ref[:, size:] = power.astype(jnp.int16)


def decode(msg_ref):
    size = msg_ref.shape[1] - 128
    power = msg_ref[:, size:].astype(jnp.int32).astype(jnp.float32)[:, :1]
    coded = msg_ref[:, :size].astype(jnp.int32).astype(jnp.float32)
    scale = jnp.exp2(power * 0.125) * (1.0 / (STEPS * STEPS))
    return coded * jnp.abs(coded) * scale


def split_kernel(even_ref, mine_ref, theirs_ref, *refs):
    kept_ref, msg_ref = refs[-2:]
    step = kept_ref.shape[1]
    low, high = slice(0, step), slice(step, 2 * step)

    @pl.when(even_ref[0] == 1)
    def _():
        kept_ref[...] = mine_ref[:, low] + theirs_ref[:, low]
        encode(mine_ref[:, high] + theirs_ref[:, high], msg_ref)

    @pl.when(even_ref[0] == 0)
    def _():
        kept_ref[...] = mine_ref[:, high] + theirs_ref[:, high]
        encode(mine_ref[:, low] + theirs_ref[:, low], msg_ref)


def merge_kernel(arrived, keep, kept_ref, *refs):
    value = kept_ref[...]
    for msg_ref in refs[:arrived]:
        value = value + decode(msg_ref)
    if keep:
        refs[-2][...] = value
    encode(value, refs[-1])


def last_kernel(owner_ref, col_ref, decoder_ref, inverse_ref, *refs):
    chunks, sums = refs[:COUNT], refs[COUNT : 2 * COUNT]
    out_ref, column = refs[-2:]
    step = chunks[0].shape[1]
    owner = owner_ref[0] == 1
    total = jnp.zeros((col_ref.shape[0], 128), jnp.float32)
    for k in range(COUNT):
        span = slice(k * step, (k + 1) * step)
        part = jnp.dot(col_ref[...], chunks[k][...], preferred_element_type=jnp.float32)
        row_sum = decode(sums[k]) if k % 2 else sums[k][...]
        part = part + jnp.where(owner, row_sum, 0.0)
        column[:, span] = part
        along = part * decoder_ref[:, span].astype(jnp.float32)
        for t in range(0, step, 128):
            total = total + along[:, t : t + 128]
    inverse = inverse_ref[:, :1]
    scale = (2.0 * math.sqrt(DW)) * inverse
    back = scale * (jnp.sum(total, axis=1, keepdims=True) * inverse * inverse)
    for k in range(COUNT):
        span = slice(k * step, (k + 1) * step)
        out_ref[:, span] = scale * column[:, span] - back * decoder_ref[:, span].astype(
            jnp.float32
        )


def on_device(decoder, quarter):
    shard, width = decoder.shape
    devices = lax.axis_size("row")
    index = lax.axis_index("row")
    per = devices // 4
    latents = shard * devices
    blocks = shard // BLOCK
    wide = min(WIDE, shard)
    step = width // COUNT
    chosen_quarter = quarter[0]
    start = chosen_quarter * (latents // 4)
    place = index // per
    within = index % per
    here = place == chosen_quarter
    even_chip = (within // 2) % 2 == 0
    odd_core = (within % 2) == 1
    smem = pl.BlockSpec(memory_space=pltpu.SMEM)

    def send(value, pairs):
        return lax.ppermute(value, "row", pairs)

    def hop(level):
        moves = (((0, 1), (3, 2)), ((1, 2), (2, 1)), ((2, 3), (1, 0)))[level]
        return [(a * per + w, b * per + w) for a, b in moves for w in (0, 2)]

    def each(moves):
        return [(z * per + a, z * per + b) for z in range(4) for a, b in moves]

    own = pl.pallas_call(
        head_kernel,
        grid=(4,),
        in_specs=[pl.BlockSpec((ROWS // 4, width), lambda i: (i, 0))],
        out_specs=[pl.BlockSpec((ROWS // 4, step), lambda i: (i, 0))] * COUNT,
        out_shape=[jax.ShapeDtypeStruct((ROWS, step), jnp.bfloat16)] * COUNT,
        compiler_params=params(),
        cost_estimate=cost(4 * ROWS * width, 4 * ROWS * width),
        name="head_units",
    )(decoder)

    units, inverse = pl.pallas_call(
        units_kernel,
        grid=(blocks,),
        in_specs=[pl.BlockSpec((BLOCK, width), lambda i: (i, 0))],
        out_specs=[
            pl.BlockSpec((BLOCK, width), lambda i: (i, 0)),
            pl.BlockSpec((BLOCK, 128), lambda i: (i, 0)),
        ],
        out_shape=[
            jax.ShapeDtypeStruct((shard, width), jnp.bfloat16),
            jax.ShapeDtypeStruct((shard, 128), jnp.float32),
        ],
        compiler_params=params(),
        cost_estimate=cost(4 * shard * width, 4 * shard * width),
        name="units",
    )(decoder)

    near = jnp.where(place == 1, chosen_quarter == 0, chosen_quarter == 3)
    middle = (place == 1) | (place == 2)
    takes = (within == 2) & (inverse[0, 0] > 0)
    mine, first, second, third, held = ([None] * PAIRS for _ in range(5))
    for k in range(PAIRS):
        across = send(own[2 * k + 1], each([(0, 2)]))
        mine[k] = jnp.where(takes, across, own[2 * k])
        first[k] = send(mine[k], hop(0))
        second[k] = send(jnp.where(here, mine[k], first[k]), hop(1))
        third[k] = send(jnp.where(here, mine[k], second[k]), hop(2))
        inner = jnp.where(near, first[k], second[k])
        held[k] = jnp.where(here, mine[k], jnp.where(middle, inner, third[k]))
    chosen = []
    for k in range(PAIRS):
        other = send(held[k], each([(0, 2), (2, 0)]))
        core_held = send(held[k], each([(0, 1), (2, 3)]))
        core_other = send(other, each([(0, 1), (2, 3)]))
        one = jnp.where(odd_core, core_held, held[k])
        two = jnp.where(odd_core, core_other, other)
        pair = [jnp.where(even_chip, one, two), jnp.where(even_chip, two, one)]
        far = 4
        while far < per:
            moves = each([(w, w + far) for w in range(far)])
            fresh = (within >= far) & (within < 2 * far)
            pair = [jnp.where(fresh, send(value, moves), value) for value in pair]
            far *= 2
        chosen += pair

    delta = jnp.reshape(index * shard - start, (1,)).astype(jnp.int32)
    whole_chunk = pl.BlockSpec((ROWS, step), lambda i: (0, 0))
    half_flops = ROWS * shard * width
    partial = None
    for k in range(PAIRS):
        unit_spec = pl.BlockSpec((wide, 2 * step), lambda i, k=k: (i, k))
        wide_spec = pl.BlockSpec((wide, ROWS), lambda i: (i, 0))
        if k < PAIRS - 1:
            partial = pl.pallas_call(
                partial_kernel,
                grid=(shard // wide,),
                in_specs=[unit_spec, whole_chunk, whole_chunk],
                out_specs=wide_spec,
                out_shape=jax.ShapeDtypeStruct((shard, ROWS), jnp.float32),
                compiler_params=params(),
                cost_estimate=cost(half_flops, shard * width),
                name="part_cosines",
            )(units, chosen[2 * k], chosen[2 * k + 1])
            continue
        by_col, by_row, along, local_penalty = pl.pallas_call(
            weight_kernel,
            grid=(shard // wide,),
            in_specs=[smem, unit_spec, whole_chunk, whole_chunk, wide_spec],
            out_specs=[
                wide_spec,
                pl.BlockSpec((ROWS, wide), lambda i: (0, i)),
                pl.BlockSpec((wide, 128), lambda i: (i, 0)),
                pl.BlockSpec((8, 128), lambda i: (0, 0)),
            ],
            out_shape=[
                jax.ShapeDtypeStruct((shard, ROWS), jnp.bfloat16),
                jax.ShapeDtypeStruct((ROWS, shard), jnp.bfloat16),
                jax.ShapeDtypeStruct((shard, 128), jnp.float32),
                jax.ShapeDtypeStruct((8, 128), jnp.float32),
            ],
            compiler_params=params(),
            cost_estimate=cost(half_flops, shard * width),
            name="weights",
        )(delta, units, chosen[2 * k], chosen[2 * k + 1], partial)

    penalties = [local_penalty]
    far = 1
    while far < devices:
        swap = [(i, i ^ far) for i in range(devices)]
        penalties.append(penalties[-1] + send(penalties[-1], swap))
        far *= 2
    penalty = jnp.sum(penalties[-1]) * (DW / (ROWS * latents))

    out_type = jax.ShapeDtypeStruct((shard, width), jnp.float32)
    mark_type = jax.ShapeDtypeStruct((8, 128), jnp.float32)
    mark_spec = pl.BlockSpec((8, 128), lambda i: (0, 0))
    any_spec = pl.BlockSpec(memory_space=pl.ANY)
    grad = None
    marks = []
    bounds = [1 + (blocks - 1) * p // 3 for p in range(4)]
    for low, high in zip(bounds[:-1], bounds[1:]):
        if high == low:
            continue
        operands = [by_col, decoder, inverse, along, *chosen]
        specs = [
            pl.BlockSpec((BLOCK, ROWS), lambda i, low=low: (i + low, 0)),
            pl.BlockSpec((BLOCK, width), lambda i, low=low: (i + low, 0)),
            pl.BlockSpec((BLOCK, 128), lambda i, low=low: (i + low, 0)),
            pl.BlockSpec((BLOCK, 128), lambda i, low=low: (i + low, 0)),
        ] + [whole_chunk] * COUNT
        aliases = {}
        if grad is not None:
            aliases = {len(operands): 0}
            operands.append(grad)
            specs.append(any_spec)
        rows = (high - low) * BLOCK
        grad, mark = pl.pallas_call(
            finish_kernel,
            grid=(high - low,),
            in_specs=specs,
            out_specs=[pl.BlockSpec((BLOCK, width), lambda i, low=low: (i + low, 0)), mark_spec],
            out_shape=[out_type, mark_type],
            input_output_aliases=aliases,
            compiler_params=params(),
            cost_estimate=cost(2 * ROWS * rows * width, 6 * rows * width),
            name="finish",
        )(*operands)
        marks.append(mark)

    quarter_rows = ROWS // 4
    kept_spec = pl.BlockSpec((quarter_rows, step), lambda i: (i, 0))
    msg_spec = pl.BlockSpec((quarter_rows, step + 128), lambda i: (i, 0))
    both_spec = pl.BlockSpec((quarter_rows, 2 * step), lambda i: (i, 0))
    kept_type = jax.ShapeDtypeStruct((ROWS, step), jnp.float32)
    msg_type = jax.ShapeDtypeStruct((ROWS, step + 128), jnp.int16)
    even_flag = jnp.reshape(even_chip, (1,)).astype(jnp.int32)
    merge_cost = cost(20 * ROWS * step, 12 * ROWS * step)

    def after(k, level):
        if k:
            return []
        return penalties[level + 1 : level + 2] + (marks[level - 1 : level] if level else [])

    def merge(kept, arrived, keep, ties):
        result = pl.pallas_call(
            functools.partial(merge_kernel, len(arrived), keep),
            grid=(4,),
            in_specs=[kept_spec] + [msg_spec] * len(arrived) + [any_spec] * len(ties),
            out_specs=[kept_spec, msg_spec] if keep else [msg_spec],
            out_shape=[kept_type, msg_type] if keep else [msg_type],
            compiler_params=params(),
            cost_estimate=merge_cost,
            name="merge",
        )(kept, *arrived, *ties)
        return result if keep else result[0]

    mine_row, kept, msg = ([None] * PAIRS for _ in range(3))
    one_hop, two_hop, three_hop = ([None] * PAIRS for _ in range(3))
    for k in range(PAIRS):
        value = pl.pallas_call(
            row_kernel,
            grid=(4,),
            in_specs=[
                pl.BlockSpec((ROWS, shard), lambda i: (0, 0)),
                pl.BlockSpec((shard, step // 2), lambda i, k=k: (0, 4 * k + i)),
            ],
            out_specs=pl.BlockSpec((ROWS, step // 2), lambda i: (0, i)),
            out_shape=jax.ShapeDtypeStruct((ROWS, 2 * step), jnp.float32),
            compiler_params=params(),
            cost_estimate=cost(half_flops, shard * width),
            name="row_part",
        )(by_row, units)
        far = per // 2
        while far >= 4:
            value = value + send(value, each([(w + far, w) for w in range(far)]))
            far //= 2
        mine_row[k] = value
    for k in range(PAIRS):
        theirs = send(mine_row[k], each([(1, 0), (3, 2)]))
        ties = after(k, 0)
        kept[k], msg[k] = pl.pallas_call(
            split_kernel,
            grid=(4,),
            in_specs=[smem, both_spec, both_spec] + [any_spec] * len(ties),
            out_specs=[kept_spec, msg_spec],
            out_shape=[kept_type, msg_type],
            compiler_params=params(),
            cost_estimate=merge_cost,
            name="split",
        )(even_flag, mine_row[k], theirs, *ties)
    for k in range(PAIRS):
        across = send(msg[k], each([(0, 2), (2, 0)]))
        kept[k], msg[k] = merge(kept[k], [across], True, after(k, 1))
    for k in range(PAIRS):
        one_hop[k] = send(msg[k], hop(0))
        msg[k] = merge(kept[k], [one_hop[k]], False, after(k, 2))
    for k in range(PAIRS):
        two_hop[k] = send(msg[k], hop(1))
        msg[k] = merge(kept[k], [two_hop[k]], False, after(k, 3))
    sums = []
    for k in range(PAIRS):
        three_hop[k] = send(msg[k], hop(2))
        total, coded = merge(kept[k], [one_hop[k], two_hop[k], three_hop[k]], True, [])
        sums += [total, send(coded, each([(2, 0)]))]

    owner = jnp.reshape(here & (within == 0), (1,)).astype(jnp.int32)
    narrow = BLOCK // 2
    operands = [owner, by_col, decoder, inverse, *chosen, *sums]
    specs = [
        smem,
        pl.BlockSpec((narrow, ROWS), lambda i: (i, 0)),
        pl.BlockSpec((narrow, width), lambda i: (i, 0)),
        pl.BlockSpec((narrow, 128), lambda i: (i, 0)),
    ]
    specs += [whole_chunk] * COUNT
    specs += [
        pl.BlockSpec((narrow, step), lambda i: (i, 0)),
        pl.BlockSpec((narrow, step + 128), lambda i: (i, 0)),
    ] * PAIRS
    aliases = {}
    if grad is not None:
        aliases = {len(operands): 0}
        operands.append(grad)
        specs.append(any_spec)
    decoder_grad = pl.pallas_call(
        last_kernel,
        grid=(2,),
        in_specs=specs,
        out_specs=pl.BlockSpec((narrow, width), lambda i: (i, 0)),
        out_shape=out_type,
        scratch_shapes=[pltpu.VMEM((narrow, width), jnp.float32)],
        input_output_aliases=aliases,
        compiler_params=params(),
        name="finish_rows",
    )(*operands)

    return (jnp.reshape(penalty, (1,)), decoder_grad)


def solution(mesh):
    in_specs = (P(("groups", "row"), None), P("groups"))
    out_specs = (P("groups"), P(("groups", "row"), None))
    return jax.shard_map(
        on_device, mesh=mesh, in_specs=in_specs, out_specs=out_specs, check_vma=False
    )
```

```python
import functools
import math

import jax
import jax.numpy as jnp
from jax import lax
from jax.experimental import pallas as pl
from jax.experimental.pallas import tpu as pltpu
from jax.sharding import PartitionSpec as P

DW = 4096
ROWS = 256
BLOCK = 256
WIDE = 512
PAIRS = 2
COUNT = 2 * PAIRS
VMEM_LIMIT = 48 * 1024 * 1024
NT = (((1,), (1,)), ((), ()))


def params():
    return pltpu.CompilerParams(vmem_limit_bytes=VMEM_LIMIT)


def cost(flops, moved):
    return pl.CostEstimate(flops=flops, bytes_accessed=moved, transcendentals=0)


def strip_inverse(ref, rows):
    width = ref.shape[1]
    total = None
    for t in range(0, width, 128):
        v = ref[rows, t : t + 128].astype(jnp.float32)
        total = v * v if total is None else total + v * v
    return 1.0 / jnp.sqrt(jnp.sum(total, axis=1, keepdims=True) + 1e-06)


def head_kernel(decoder_ref, *chunk_refs):
    step = chunk_refs[0].shape[1]
    rows = slice(0, decoder_ref.shape[0])
    inverse = strip_inverse(decoder_ref, rows)
    piece = step // 2
    for k in range(PAIRS):
        for p in range(4):
            ref, base = chunk_refs[2 * k + p % 2], (4 * k + p) * piece
            for t in range(0, piece, 128):
                v = decoder_ref[rows, base + t : base + t + 128].astype(jnp.float32)
                to = (p // 2) * piece + t
                ref[rows, to : to + 128] = (v * inverse).astype(jnp.bfloat16)


def units_kernel(decoder_ref, *refs):
    units_ref, inverse_ref = refs[-2:]
    strip = 64

    def body(s, carry):
        rows = pl.ds(pl.multiple_of(s * strip, strip), strip)
        inverse = strip_inverse(decoder_ref, rows)
        inverse_ref[rows, :] = jnp.broadcast_to(inverse, (strip, 128))
        for t in range(0, decoder_ref.shape[1], 128):
            v = decoder_ref[rows, t : t + 128].astype(jnp.float32)
            units_ref[rows, t : t + 128] = (v * inverse).astype(jnp.bfloat16)
        return carry

    lax.fori_loop(0, decoder_ref.shape[0] // strip, body, 0)


def pair_cosines(units_ref, low_ref, high_ref):
    step = low_ref.shape[1]
    low = lax.dot_general(
        units_ref[:, :step], low_ref[...], NT, preferred_element_type=jnp.float32
    )
    high = lax.dot_general(
        units_ref[:, step:], high_ref[...], NT, preferred_element_type=jnp.float32
    )
    return low + high


def partial_kernel(units_ref, low_ref, high_ref, out_ref):
    out_ref[...] = pair_cosines(units_ref, low_ref, high_ref)


def weight_kernel(
    delta_ref, units_ref, low_ref, high_ref, partial_ref, col_ref, row_ref, along_ref, penalty_ref
):
    size = units_ref.shape[0]
    j = pl.program_id(0)
    cosines = partial_ref[...] + pair_cosines(units_ref, low_ref, high_ref)
    latents = lax.broadcasted_iota(jnp.int32, (size, ROWS), 0) + (delta_ref[0] + j * size)
    rows = lax.broadcasted_iota(jnp.int32, (size, ROWS), 1)
    inside = (latents >= 0) & (latents < ROWS)
    weight = jnp.where(latents == rows, 0.0, jnp.where(inside, 0.5, 1.0))
    products = weight * cosines
    weighted = products.astype(jnp.bfloat16)
    col_ref[...] = weighted
    row_ref[...] = products.T.astype(jnp.bfloat16)
    along = jnp.sum(weighted.astype(jnp.float32) * cosines, axis=1, keepdims=True)
    along_ref[...] = jnp.broadcast_to(along, along_ref.shape)

    @pl.when(j == 0)
    def _():
        penalty_ref[...] = jnp.zeros_like(penalty_ref)

    squares = products * cosines
    squares = squares[:, :128] + squares[:, 128:]
    penalty_ref[...] += jnp.sum(squares.reshape(size // 8, 8, 128), axis=0)


def row_kernel(side_ref, row_ref, penalty_ref, units_ref, *refs):
    out_ref = refs[-1]
    out_ref[:ROWS, :] = jnp.dot(
        row_ref[...], units_ref[...], preferred_element_type=jnp.float32
    )
    out_ref[ROWS:, :] = jnp.concatenate([penalty_ref[...]] * (out_ref.shape[1] // 128), axis=1)


def finish_kernel(col_ref, decoder_ref, inverse_ref, along_ref, *refs):
    chunks = refs[:COUNT]
    out_ref, mark_ref = refs[-2:]
    step = chunks[0].shape[1]
    inverse = inverse_ref[:, :1]
    scale = (2.0 * math.sqrt(DW)) * inverse
    back = scale * (along_ref[:, :1] * inverse)
    for k in range(COUNT):
        span = slice(k * step, (k + 1) * step)
        part = jnp.dot(col_ref[...], chunks[k][...], preferred_element_type=jnp.float32)
        out_ref[:, span] = scale * part - back * decoder_ref[:, span].astype(jnp.float32)
    mark_ref[...] = jnp.zeros_like(mark_ref)


STEPS = 32000.0
CODED_ROWS = ROWS + 16
PENALTY_STEPS = float(1 << 23)


def pack(coded):
    half = coded.shape[1] // 2
    return (coded[:, :half] << 16) | (coded[:, half:] & 0xFFFF)


def unpack(words):
    both = jnp.concatenate([words >> 16, (words << 16) >> 16], axis=1)
    return both.astype(jnp.float32)


def encode(value, penalty, msg_ref):
    top = jnp.max(jnp.abs(value), axis=0, keepdims=True)
    power = jnp.ceil(jnp.log2(jnp.maximum(top, 1e-35)) * 8.0)
    ratio = value * jnp.exp2(power * -0.125)
    coded = ratio * lax.rsqrt(jnp.maximum(jnp.abs(ratio), 1e-30))
    msg_ref[:ROWS, :] = pack(jnp.round(coded * STEPS).astype(jnp.int32))
    power = pack(power.astype(jnp.int32))
    msg_ref[ROWS : ROWS + 8, :] = jnp.broadcast_to(power, (8, power.shape[1]))
    top = jnp.max(jnp.max(penalty, axis=1, keepdims=True), axis=0, keepdims=True)
    power = jnp.ceil(jnp.log2(jnp.maximum(top, 1e-35)))
    coded = jnp.round(penalty * (jnp.exp2(-power) * PENALTY_STEPS)).astype(jnp.int32)
    msg_ref[ROWS + 8 :, :128] = coded
    msg_ref[ROWS + 8 :, 128:] = jnp.broadcast_to(power.astype(jnp.int32), (8, 128))


def decode(words, powers):
    coded = unpack(words)
    scale = jnp.exp2(unpack(powers)[:1, :] * 0.125) * (1.0 / (STEPS * STEPS))
    return coded * jnp.abs(coded) * scale


def decode_at(msg_ref, base):
    value = decode(msg_ref[base : base + ROWS, :], msg_ref[base + ROWS : base + ROWS + 8, :])
    tail = slice(base + ROWS + 8, base + CODED_ROWS)
    power = msg_ref[tail, 128:].astype(jnp.float32)
    penalty = msg_ref[tail, :128].astype(jnp.float32) * (jnp.exp2(power) / PENALTY_STEPS)
    return value, penalty


def split_kernel(odd_ref, mine_ref, theirs_ref, kept_ref, penalty_ref, msg_ref):
    piece = kept_ref.shape[1]
    penalty = mine_ref[ROWS:, :128] + theirs_ref[ROWS:, :128]
    penalty_ref[...] = penalty
    low, high = slice(0, piece), slice(piece, 2 * piece)

    def divide(keep, away):
        kept_ref[...] = mine_ref[:ROWS, keep] + theirs_ref[:ROWS, keep]
        encode(mine_ref[:ROWS, away] + theirs_ref[:ROWS, away], penalty, msg_ref)

    @pl.when(odd_ref[0] == 0)
    def _():
        divide(low, high)

    @pl.when(odd_ref[0] == 1)
    def _():
        divide(high, low)


def merge_kernel(kept_ref, penalty_ref, arrived_ref, msg_ref):
    value, penalty = decode_at(arrived_ref, 0)
    encode(kept_ref[...] + value, penalty_ref[...] + penalty, msg_ref)


def total_kernel(gathered_ref, *refs):
    total_ref, penalty_ref, msg_ref = refs[-3:]
    value, penalty = decode_at(gathered_ref, 0)
    for z in range(1, 4):
        more, more_penalty = decode_at(gathered_ref, z * CODED_ROWS)
        value, penalty = value + more, penalty + more_penalty
    total_ref[...] = value
    penalty_ref[...] = penalty
    encode(value, penalty, msg_ref)


def last_kernel(owner_ref, col_ref, decoder_ref, inverse_ref, *refs):
    chunks, sums = refs[:COUNT], refs[COUNT : COUNT + 7 * PAIRS]
    out_ref, column = refs[-2:]
    step = chunks[0].shape[1]
    piece = step // 2
    owner = owner_ref[0] == 1
    total = jnp.zeros((col_ref.shape[0], 128), jnp.float32)
    for k in range(COUNT):
        span = slice(k * step, (k + 1) * step)
        part = jnp.dot(col_ref[...], chunks[k][...], preferred_element_type=jnp.float32)
        own, *coded = sums[7 * (k // 2) : 7 * (k // 2) + 7]
        pieces = [own[...]] + [
            decode(coded[2 * p][...], coded[2 * p + 1][...]) for p in range(3)
        ]
        row_sum = jnp.concatenate(pieces[2 * (k % 2) : 2 * (k % 2) + 2], axis=1)
        part = part + jnp.where(owner, row_sum, 0.0)
        column[:, span] = part
        along = part * decoder_ref[:, span].astype(jnp.float32)
        for t in range(0, step, 128):
            total = total + along[:, t : t + 128]
    inverse = inverse_ref[:, :1]
    scale = (2.0 * math.sqrt(DW)) * inverse
    back = scale * (jnp.sum(total, axis=1, keepdims=True) * inverse * inverse)
    for k in range(COUNT):
        span = slice(k * step, (k + 1) * step)
        out_ref[:, span] = scale * column[:, span] - back * decoder_ref[:, span].astype(
            jnp.float32
        )


def on_device(decoder, quarter):
    shard, width = decoder.shape
    devices = lax.axis_size("row")
    index = lax.axis_index("row")
    per = devices // 4
    latents = shard * devices
    blocks = shard // BLOCK
    wide = min(WIDE, shard)
    step = width // COUNT
    chosen_quarter = quarter[0]
    start = chosen_quarter * (latents // 4)
    place = index // per
    within = index % per
    here = place == chosen_quarter
    even_chip = (within // 2) % 2 == 0
    odd_core = (within % 2) == 1
    smem = pl.BlockSpec(memory_space=pltpu.SMEM)

    def send(value, pairs):
        return lax.ppermute(value, "row", pairs)

    def each(moves):
        return [(z * per + a, z * per + b) for z in range(4) for a, b in moves]

    own = pl.pallas_call(
        head_kernel,
        grid=(4,),
        in_specs=[pl.BlockSpec((ROWS // 4, width), lambda i: (i, 0))],
        out_specs=[pl.BlockSpec((ROWS // 4, step), lambda i: (i, 0))] * COUNT,
        out_shape=[jax.ShapeDtypeStruct((ROWS, step), jnp.bfloat16)] * COUNT,
        compiler_params=params(),
        cost_estimate=cost(4 * ROWS * width, 4 * ROWS * width),
        name="head_units",
    )(decoder)

    any_spec = pl.BlockSpec(memory_space=pl.ANY)
    planes = [[z * per + w for z in range(4)] for w in range(per)]
    across_x = each([(0, 2), (2, 0), (1, 3), (3, 1)])
    across_core = each([(0, 1), (1, 0), (2, 3), (3, 2)])

    def gather(value):
        return lax.all_gather(value, "row", axis=0, tiled=True, axis_index_groups=planes)

    piece = step // 2
    pieces = []
    for k in range(PAIRS):
        across = send(own[2 * k + 1], each([(0, 2)]))
        mine = jnp.where(within == 2, across, own[2 * k])
        moved = send(mine[:, piece:], each([(0, 1), (2, 3)]))
        pieces.append(jnp.where(odd_core, moved, mine[:, :piece]))

    units = inverse = None
    ready = []
    bounds = [0, blocks // 2, blocks]
    for part, (low, high) in enumerate(zip(bounds[:-1], bounds[1:])):
        if high == low:
            continue
        operands = [decoder, pieces[min(part, PAIRS - 1)]]
        specs = [pl.BlockSpec((BLOCK, width), lambda i, low=low: (i + low, 0)), any_spec]
        aliases = {}
        if units is not None:
            aliases = {2: 0, 3: 1}
            operands += [units, inverse]
            specs += [any_spec, any_spec]
        units, inverse = pl.pallas_call(
            units_kernel,
            grid=(high - low,),
            in_specs=specs,
            out_specs=[
                pl.BlockSpec((BLOCK, width), lambda i, low=low: (i + low, 0)),
                pl.BlockSpec((BLOCK, 128), lambda i, low=low: (i + low, 0)),
            ],
            out_shape=[
                jax.ShapeDtypeStruct((shard, width), jnp.bfloat16),
                jax.ShapeDtypeStruct((shard, 128), jnp.float32),
            ],
            input_output_aliases=aliases,
            compiler_params=params(),
            cost_estimate=cost(4 * BLOCK * width, 4 * (high - low) * BLOCK * width),
            name="units",
        )(*operands)
        ready.append((inverse[low * BLOCK, 0] < 0).astype(jnp.int32))

    chosen = []
    for k in range(PAIRS):
        first_row = chosen_quarter * ROWS + ready[min(k, len(ready) - 1)]
        found = lax.dynamic_slice_in_dim(gather(pieces[k]), first_row, ROWS, 0)
        other = send(found, across_x)
        both = jnp.concatenate(
            [jnp.where(even_chip, found, other), jnp.where(even_chip, other, found)], axis=1
        )
        theirs = send(both, across_core)
        pair = [jnp.where(odd_core, theirs, both), jnp.where(odd_core, both, theirs)]
        far = 4
        while far < per:
            moves = each([(w, w + far) for w in range(far)])
            fresh = (within >= far) & (within < 2 * far)
            pair = [jnp.where(fresh, send(value, moves), value) for value in pair]
            far *= 2
        chosen += pair

    delta = jnp.reshape(index * shard - start, (1,)).astype(jnp.int32)
    whole_chunk = pl.BlockSpec((ROWS, step), lambda i: (0, 0))
    half_flops = ROWS * shard * width
    partial = None
    for k in range(PAIRS):
        unit_spec = pl.BlockSpec((wide, 2 * step), lambda i, k=k: (i, k))
        wide_spec = pl.BlockSpec((wide, ROWS), lambda i: (i, 0))
        if k < PAIRS - 1:
            partial = pl.pallas_call(
                partial_kernel,
                grid=(shard // wide,),
                in_specs=[unit_spec, whole_chunk, whole_chunk],
                out_specs=wide_spec,
                out_shape=jax.ShapeDtypeStruct((shard, ROWS), jnp.float32),
                compiler_params=params(),
                cost_estimate=cost(half_flops, shard * width),
                name="part_cosines",
            )(units, chosen[2 * k], chosen[2 * k + 1])
            continue
        by_col, by_row, along, local_penalty = pl.pallas_call(
            weight_kernel,
            grid=(shard // wide,),
            in_specs=[smem, unit_spec, whole_chunk, whole_chunk, wide_spec],
            out_specs=[
                wide_spec,
                pl.BlockSpec((ROWS, wide), lambda i: (0, i)),
                pl.BlockSpec((wide, 128), lambda i: (i, 0)),
                pl.BlockSpec((8, 128), lambda i: (0, 0)),
            ],
            out_shape=[
                jax.ShapeDtypeStruct((shard, ROWS), jnp.bfloat16),
                jax.ShapeDtypeStruct((ROWS, shard), jnp.bfloat16),
                jax.ShapeDtypeStruct((shard, 128), jnp.float32),
                jax.ShapeDtypeStruct((8, 128), jnp.float32),
            ],
            compiler_params=params(),
            cost_estimate=cost(half_flops, shard * width),
            name="weights",
        )(delta, units, chosen[2 * k], chosen[2 * k + 1], partial)

    core_side = within % 2
    plane_x = jnp.reshape((within // 2) % 2, (1,)).astype(jnp.int32)
    tall = ROWS + 8
    coded_type = jax.ShapeDtypeStruct((CODED_ROWS, piece // 2), jnp.int32)
    piece_type = jax.ShapeDtypeStruct((ROWS, piece), jnp.float32)
    tile_type = jax.ShapeDtypeStruct((8, 128), jnp.float32)
    vmem = pl.BlockSpec(memory_space=pltpu.VMEM)
    merge_cost = cost(20 * ROWS * piece, 12 * ROWS * piece)

    def row_part(k, side):
        return pl.pallas_call(
            row_kernel,
            grid_spec=pltpu.PrefetchScalarGridSpec(
                num_scalar_prefetch=1,
                grid=(2,),
                in_specs=[
                    pl.BlockSpec((ROWS, shard), lambda i, s: (0, 0)),
                    pl.BlockSpec((8, 128), lambda i, s: (0, 0)),
                    pl.BlockSpec((shard, piece), lambda i, s: (0, 4 * k + 2 * s[0] + i)),
                ],
                out_specs=pl.BlockSpec((tall, piece), lambda i, s: (0, i)),
            ),
            out_shape=jax.ShapeDtypeStruct((tall, step), jnp.float32),
            compiler_params=params(),
            cost_estimate=cost(half_flops // 2, shard * width // 2),
            name="row_part",
        )(jnp.reshape(side, (1,)).astype(jnp.int32), by_row, local_penalty, units)

    coded = []
    for k in range(PAIRS):
        away, near = row_part(k, 1 - core_side), row_part(k, core_side)
        far = per // 2
        while far >= 4:
            moves = each([(w + far, w) for w in range(far)])
            away, near = away + send(away, moves), near + send(near, moves)
            far //= 2
        kept, tile, msg = pl.pallas_call(
            split_kernel,
            in_specs=[smem, vmem, vmem],
            out_specs=[vmem, vmem, vmem],
            out_shape=[piece_type, tile_type, coded_type],
            compiler_params=params(),
            cost_estimate=merge_cost,
            name="split",
        )(plane_x, near, send(away, across_core))
        coded.append(
            pl.pallas_call(
                merge_kernel,
                in_specs=[vmem, vmem, vmem],
                out_specs=vmem,
                out_shape=coded_type,
                compiler_params=params(),
                cost_estimate=merge_cost,
                name="merge",
            )(kept, tile, send(msg, across_x))
        )

    out_type = jax.ShapeDtypeStruct((shard, width), jnp.float32)
    mark_type = jax.ShapeDtypeStruct((8, 128), jnp.float32)
    mark_spec = pl.BlockSpec((8, 128), lambda i: (0, 0))
    grad = None
    marks = []
    bounds = [1 + (blocks - 1) * p // 3 for p in range(4)]
    for part, (low, high) in enumerate(zip(bounds[:-1], bounds[1:])):
        if high == low:
            continue
        operands = [by_col, decoder, inverse, along, *chosen]
        specs = [
            pl.BlockSpec((BLOCK, ROWS), lambda i, low=low: (i + low, 0)),
            pl.BlockSpec((BLOCK, width), lambda i, low=low: (i + low, 0)),
            pl.BlockSpec((BLOCK, 128), lambda i, low=low: (i + low, 0)),
            pl.BlockSpec((BLOCK, 128), lambda i, low=low: (i + low, 0)),
        ] + [whole_chunk] * COUNT
        operands.append(coded[min(part, PAIRS - 1)])
        specs.append(any_spec)
        aliases = {}
        if grad is not None:
            aliases = {len(operands): 0}
            operands.append(grad)
            specs.append(any_spec)
        rows = (high - low) * BLOCK
        grad, mark = pl.pallas_call(
            finish_kernel,
            grid=(high - low,),
            in_specs=specs,
            out_specs=[pl.BlockSpec((BLOCK, width), lambda i, low=low: (i + low, 0)), mark_spec],
            out_shape=[out_type, mark_type],
            input_output_aliases=aliases,
            compiler_params=params(),
            cost_estimate=cost(2 * ROWS * rows * width, 6 * rows * width),
            name="finish",
        )(*operands)
        marks.append(mark)

    sums, row_specs = [], []
    narrow = BLOCK // 2
    for k in range(PAIRS):
        ties = marks[:2] if k == 0 else marks[2:]
        total, tile, msg = pl.pallas_call(
            total_kernel,
            in_specs=[vmem] + [any_spec] * len(ties),
            out_specs=[vmem, vmem, vmem],
            out_shape=[piece_type, tile_type, coded_type],
            compiler_params=params(),
            cost_estimate=merge_cost,
            name="total",
        )(gather(coded[k]), *ties)
        sums.append(total)
        row_specs.append(pl.BlockSpec((narrow, piece), lambda i: (i, 0)))
        for source in (2, 1, 3):
            arrived = send(msg, each([(source, 0)]))
            sums += [arrived, arrived]
            row_specs += [
                pl.BlockSpec((narrow, piece // 2), lambda i: (i, 0)),
                pl.BlockSpec((8, piece // 2), lambda i: (ROWS // 8, 0)),
            ]
        if k == 0:
            far = 4
            while far < per:
                moves = each([(w, w + far) for w in range(far)])
                fresh = (within >= far) & (within < 2 * far)
                tile = jnp.where(fresh, send(tile, moves), tile)
                far *= 2
            penalty = jnp.sum(tile) * (DW / (ROWS * latents))

    owner = jnp.reshape(here & (within == 0), (1,)).astype(jnp.int32)
    operands = [owner, by_col, decoder, inverse, *chosen, *sums]
    specs = [
        smem,
        pl.BlockSpec((narrow, ROWS), lambda i: (i, 0)),
        pl.BlockSpec((narrow, width), lambda i: (i, 0)),
        pl.BlockSpec((narrow, 128), lambda i: (i, 0)),
    ]
    specs += [whole_chunk] * COUNT
    specs += row_specs
    aliases = {}
    if grad is not None:
        aliases = {len(operands): 0}
        operands.append(grad)
        specs.append(any_spec)
    decoder_grad = pl.pallas_call(
        last_kernel,
        grid=(2,),
        in_specs=specs,
        out_specs=pl.BlockSpec((narrow, width), lambda i: (i, 0)),
        out_shape=out_type,
        scratch_shapes=[pltpu.VMEM((narrow, width), jnp.float32)],
        input_output_aliases=aliases,
        compiler_params=params(),
        name="finish_rows",
    )(*operands)

    return (jnp.reshape(penalty, (1,)), decoder_grad)


def solution(mesh):
    in_specs = (P(("groups", "row"), None), P("groups"))
    out_specs = (P("groups"), P(("groups", "row"), None))
    return jax.shard_map(
        on_device, mesh=mesh, in_specs=in_specs, out_specs=out_specs, check_vma=False
    )
```

```python
import functools
import math

import jax
import jax.numpy as jnp
from jax import lax
from jax.experimental import pallas as pl
from jax.experimental.pallas import tpu as pltpu
from jax.sharding import PartitionSpec as P

DW = 4096
ROWS = 256
BLOCK = 256
WIDE = 512
PAIRS = 2
COUNT = 2 * PAIRS
VMEM_LIMIT = 48 * 1024 * 1024
NT = (((1,), (1,)), ((), ()))


def params():
    return pltpu.CompilerParams(vmem_limit_bytes=VMEM_LIMIT)


def cost(flops, moved):
    return pl.CostEstimate(flops=flops, bytes_accessed=moved, transcendentals=0)


def strip_inverse(ref, rows):
    width = ref.shape[1]
    total = None
    for t in range(0, width, 128):
        v = ref[rows, t : t + 128].astype(jnp.float32)
        total = v * v if total is None else total + v * v
    return 1.0 / jnp.sqrt(jnp.sum(total, axis=1, keepdims=True) + 1e-06)


def head_kernel(decoder_ref, *chunk_refs):
    step = chunk_refs[0].shape[1]
    rows = slice(0, decoder_ref.shape[0])
    inverse = strip_inverse(decoder_ref, rows)
    for k, ref in enumerate(chunk_refs):
        for t in range(0, step, 128):
            v = decoder_ref[rows, k * step + t : k * step + t + 128].astype(jnp.float32)
            ref[rows, t : t + 128] = (v * inverse).astype(jnp.bfloat16)


def units_kernel(decoder_ref, *refs):
    units_ref, inverse_ref = refs[-2:]
    strip = 64

    for base in range(0, decoder_ref.shape[0], strip):
        rows = slice(base, base + strip)
        inverse = strip_inverse(decoder_ref, rows)
        inverse_ref[rows, :] = jnp.broadcast_to(inverse, (strip, 128))
        for t in range(0, decoder_ref.shape[1], 128):
            v = decoder_ref[rows, t : t + 128].astype(jnp.float32)
            units_ref[rows, t : t + 128] = (v * inverse).astype(jnp.bfloat16)


def pair_cosines(units_ref, low_ref, high_ref):
    step = low_ref.shape[1]
    low = lax.dot_general(
        units_ref[:, :step], low_ref[...], NT, preferred_element_type=jnp.float32
    )
    high = lax.dot_general(
        units_ref[:, step:], high_ref[...], NT, preferred_element_type=jnp.float32
    )
    return low + high


def partial_kernel(units_ref, low_ref, high_ref, out_ref):
    out_ref[...] = pair_cosines(units_ref, low_ref, high_ref)


def weight_kernel(
    delta_ref, units_ref, low_ref, high_ref, partial_ref, col_ref, row_ref, along_ref, penalty_ref
):
    size = units_ref.shape[0]
    j = pl.program_id(0)
    cosines = partial_ref[...] + pair_cosines(units_ref, low_ref, high_ref)
    latents = lax.broadcasted_iota(jnp.int32, (size, ROWS), 0) + (delta_ref[0] + j * size)
    rows = lax.broadcasted_iota(jnp.int32, (size, ROWS), 1)
    inside = (latents >= 0) & (latents < ROWS)
    weight = jnp.where(latents == rows, 0.0, jnp.where(inside, 0.5, 1.0))
    products = weight * cosines
    weighted = products.astype(jnp.bfloat16)
    col_ref[...] = weighted
    row_ref[...] = products.T.astype(jnp.bfloat16)
    along = jnp.sum(weighted.astype(jnp.float32) * cosines, axis=1, keepdims=True)
    along_ref[...] = jnp.broadcast_to(along, along_ref.shape)

    @pl.when(j == 0)
    def _():
        penalty_ref[...] = jnp.zeros_like(penalty_ref)

    squares = products * cosines
    squares = squares[:, :128] + squares[:, 128:]
    penalty_ref[...] += jnp.sum(squares.reshape(size // 8, 8, 128), axis=0)


def row_kernel(side_ref, row_ref, penalty_ref, units_ref, *refs):
    out_ref = refs[-1]
    out_ref[:ROWS, :] = jnp.dot(
        row_ref[...], units_ref[...], preferred_element_type=jnp.float32
    )
    out_ref[ROWS:, :] = jnp.concatenate([penalty_ref[...]] * (out_ref.shape[1] // 128), axis=1)


def finish_kernel(col_ref, decoder_ref, inverse_ref, along_ref, *refs):
    chunks = refs[:COUNT]
    out_ref, mark_ref = refs[-2:]
    step = chunks[0].shape[1]
    inverse = inverse_ref[:, :1]
    scale = (2.0 * math.sqrt(DW)) * inverse
    back = scale * (along_ref[:, :1] * inverse)
    for k in range(COUNT):
        span = slice(k * step, (k + 1) * step)
        part = jnp.dot(col_ref[...], chunks[k][...], preferred_element_type=jnp.float32)
        out_ref[:, span] = scale * part - back * decoder_ref[:, span].astype(jnp.float32)
    mark_ref[...] = jnp.zeros_like(mark_ref)


STEPS = 32000.0
CODED_ROWS = ROWS + 16
PENALTY_STEPS = float(1 << 23)


def pack(coded):
    half = coded.shape[1] // 2
    return (coded[:, :half] << 16) | (coded[:, half:] & 0xFFFF)


def unpack(words):
    both = jnp.concatenate([words >> 16, (words << 16) >> 16], axis=1)
    return both.astype(jnp.float32)


def encode(value, penalty, msg_ref):
    top = jnp.max(jnp.abs(value), axis=0, keepdims=True)
    power = jnp.ceil(jnp.log2(jnp.maximum(top, 1e-35)) * 8.0)
    ratio = value * jnp.exp2(power * -0.125)
    coded = ratio * lax.rsqrt(jnp.maximum(jnp.abs(ratio), 1e-30))
    msg_ref[:ROWS, :] = pack(jnp.round(coded * STEPS).astype(jnp.int32))
    power = pack(power.astype(jnp.int32))
    msg_ref[ROWS : ROWS + 8, :] = jnp.broadcast_to(power, (8, power.shape[1]))
    top = jnp.max(jnp.max(penalty, axis=1, keepdims=True), axis=0, keepdims=True)
    power = jnp.ceil(jnp.log2(jnp.maximum(top, 1e-35)))
    coded = jnp.round(penalty * (jnp.exp2(-power) * PENALTY_STEPS)).astype(jnp.int32)
    msg_ref[ROWS + 8 :, :128] = coded
    msg_ref[ROWS + 8 :, 128:] = jnp.broadcast_to(power.astype(jnp.int32), (8, 128))


def decode(words, powers):
    coded = unpack(words)
    scale = jnp.exp2(unpack(powers)[:1, :] * 0.125) * (1.0 / (STEPS * STEPS))
    return coded * jnp.abs(coded) * scale


def decode_at(msg_ref):
    value = decode(msg_ref[:ROWS, :], msg_ref[ROWS : ROWS + 8, :])
    power = msg_ref[ROWS + 8 :, 128:].astype(jnp.float32)
    penalty = msg_ref[ROWS + 8 :, :128].astype(jnp.float32) * (jnp.exp2(power) / PENALTY_STEPS)
    return value, penalty


def split_kernel(odd_ref, mine_ref, theirs_ref, kept_ref, penalty_ref, msg_ref):
    piece = kept_ref.shape[1]
    penalty = mine_ref[ROWS:, :128] + theirs_ref[ROWS:, :128]
    penalty_ref[...] = penalty
    low, high = slice(0, piece), slice(piece, 2 * piece)

    def divide(keep, away):
        kept_ref[...] = mine_ref[:ROWS, keep] + theirs_ref[:ROWS, keep]
        encode(mine_ref[:ROWS, away] + theirs_ref[:ROWS, away], penalty, msg_ref)

    @pl.when(odd_ref[0] == 0)
    def _():
        divide(low, high)

    @pl.when(odd_ref[0] == 1)
    def _():
        divide(high, low)


def merge_kernel(arrived, keep, kept_ref, penalty_ref, *refs):
    value, penalty = kept_ref[...], penalty_ref[...]
    for msg_ref in refs[:arrived]:
        more, more_penalty = decode_at(msg_ref)
        value, penalty = value + more, penalty + more_penalty
    if keep:
        refs[-3][...] = value
        refs[-2][...] = penalty
    encode(value, penalty, refs[-1])


def last_kernel(owner_ref, col_ref, decoder_ref, inverse_ref, *refs):
    chunks, sums = refs[:COUNT], refs[COUNT : COUNT + 7 * PAIRS]
    out_ref, column = refs[-2:]
    step = chunks[0].shape[1]
    piece = step // 2
    owner = owner_ref[0] == 1
    total = jnp.zeros((col_ref.shape[0], 128), jnp.float32)
    for k in range(COUNT):
        span = slice(k * step, (k + 1) * step)
        part = jnp.dot(col_ref[...], chunks[k][...], preferred_element_type=jnp.float32)
        own, *coded = sums[7 * (k // 2) : 7 * (k // 2) + 7]
        pieces = [own[...]] + [
            decode(coded[2 * p][...], coded[2 * p + 1][...]) for p in range(3)
        ]
        row_sum = jnp.concatenate(pieces[2 * (k % 2) : 2 * (k % 2) + 2], axis=1)
        part = part + jnp.where(owner, row_sum, 0.0)
        column[:, span] = part
        along = part * decoder_ref[:, span].astype(jnp.float32)
        for t in range(0, step, 128):
            total = total + along[:, t : t + 128]
    inverse = inverse_ref[:, :1]
    scale = (2.0 * math.sqrt(DW)) * inverse
    back = scale * (jnp.sum(total, axis=1, keepdims=True) * inverse * inverse)
    for k in range(COUNT):
        span = slice(k * step, (k + 1) * step)
        out_ref[:, span] = scale * column[:, span] - back * decoder_ref[:, span].astype(
            jnp.float32
        )


def on_device(decoder, quarter):
    shard, width = decoder.shape
    devices = lax.axis_size("row")
    index = lax.axis_index("row")
    per = devices // 4
    latents = shard * devices
    blocks = shard // BLOCK
    wide = min(WIDE, shard)
    step = width // COUNT
    chosen_quarter = quarter[0]
    start = chosen_quarter * (latents // 4)
    place = index // per
    within = index % per
    here = place == chosen_quarter
    even_chip = (within // 2) % 2 == 0
    odd_core = (within % 2) == 1
    smem = pl.BlockSpec(memory_space=pltpu.SMEM)

    def send(value, pairs):
        return lax.ppermute(value, "row", pairs)

    def each(moves):
        return [(z * per + a, z * per + b) for z in range(4) for a, b in moves]

    own = pl.pallas_call(
        head_kernel,
        grid=(4,),
        in_specs=[pl.BlockSpec((ROWS // 4, width), lambda i: (i, 0))],
        out_specs=[pl.BlockSpec((ROWS // 4, step), lambda i: (i, 0))] * COUNT,
        out_shape=[jax.ShapeDtypeStruct((ROWS, step), jnp.bfloat16)] * COUNT,
        compiler_params=params(),
        cost_estimate=cost(4 * ROWS * width, 4 * ROWS * width),
        name="head_units",
    )(decoder)

    any_spec = pl.BlockSpec(memory_space=pl.ANY)
    across_x = each([(0, 2), (2, 0), (1, 3), (3, 1)])
    across_core = each([(0, 1), (1, 0), (2, 3), (3, 2)])
    piece = step // 2

    def hop(level, lanes):
        moves = (((0, 1), (3, 2)), ((1, 2), (2, 1)), ((2, 3), (1, 0)))[level]
        return [(a * per + w, b * per + w) for a, b in moves for w in lanes]

    unit_bounds = [0, blocks // 4, 5 * blocks // 8, blocks]
    made = [None, None]

    def make_units(part, tie):
        low, high = unit_bounds[part], unit_bounds[part + 1]
        if high == low:
            return True
        operands = [decoder, tie]
        specs = [pl.BlockSpec((BLOCK, width), lambda i: (i + low, 0)), any_spec]
        aliases = {}
        if made[0] is not None:
            aliases = {2: 0, 3: 1}
            operands += made
            specs += [any_spec, any_spec]
        made[:] = pl.pallas_call(
            units_kernel,
            grid=(high - low,),
            in_specs=specs,
            out_specs=[
                pl.BlockSpec((BLOCK, width), lambda i: (i + low, 0)),
                pl.BlockSpec((BLOCK, 128), lambda i: (i + low, 0)),
            ],
            out_shape=[
                jax.ShapeDtypeStruct((shard, width), jnp.bfloat16),
                jax.ShapeDtypeStruct((shard, 128), jnp.float32),
            ],
            input_output_aliases=aliases,
            compiler_params=params(),
            cost_estimate=cost(4 * BLOCK * width, 4 * (high - low) * BLOCK * width),
            name="units",
        )(*operands)
        return made[1][low * BLOCK, 0] > 0

    near = jnp.where(place == 1, chosen_quarter == 0, chosen_quarter == 3)
    middle = (place == 1) | (place == 2)
    mine, first, second, third, held = ([None] * PAIRS for _ in range(5))
    across = [send(own[2 * k + 1], each([(0, 2)])) for k in range(PAIRS)]
    done = make_units(0, own[0])
    for k in range(PAIRS):
        takes = (within == 2) & done if k == 0 else within == 2
        mine[k] = jnp.where(takes, across[k], own[2 * k])
    for k in range(PAIRS):
        first[k] = send(mine[k], hop(0, (0, 2)))
    done = make_units(1, mine[PAIRS - 1])
    going = [None] * PAIRS
    for k in range(PAIRS):
        keeps = here & done if k == 0 else here
        going[k] = jnp.where(keeps, mine[k], first[k])
        second[k] = send(going[k], hop(1, (0, 2)))
    for k in range(PAIRS):
        going[k] = jnp.where(here, mine[k], second[k])
        third[k] = send(going[k], hop(2, (0, 2)))
    done = make_units(2, going[PAIRS - 1])
    units, inverse = made
    for k in range(PAIRS):
        inner = jnp.where(near, first[k], second[k])
        keeps = here & done if k == 0 else here
        held[k] = jnp.where(keeps, mine[k], jnp.where(middle, inner, third[k]))
    chosen = []
    for k in range(PAIRS):
        other = send(held[k], each([(0, 2), (2, 0)]))
        core_held = send(held[k], each([(0, 1), (2, 3)]))
        core_other = send(other, each([(0, 1), (2, 3)]))
        one = jnp.where(odd_core, core_held, held[k])
        two = jnp.where(odd_core, core_other, other)
        pair = [jnp.where(even_chip, one, two), jnp.where(even_chip, two, one)]
        far = 4
        while far < per:
            moves = each([(w, w + far) for w in range(far)])
            fresh = (within >= far) & (within < 2 * far)
            pair = [jnp.where(fresh, send(value, moves), value) for value in pair]
            far *= 2
        chosen += pair

    delta = jnp.reshape(index * shard - start, (1,)).astype(jnp.int32)
    whole_chunk = pl.BlockSpec((ROWS, step), lambda i: (0, 0))
    half_flops = ROWS * shard * width
    partial = None
    for k in range(PAIRS):
        unit_spec = pl.BlockSpec((wide, 2 * step), lambda i, k=k: (i, k))
        wide_spec = pl.BlockSpec((wide, ROWS), lambda i: (i, 0))
        if k < PAIRS - 1:
            partial = pl.pallas_call(
                partial_kernel,
                grid=(shard // wide,),
                in_specs=[unit_spec, whole_chunk, whole_chunk],
                out_specs=wide_spec,
                out_shape=jax.ShapeDtypeStruct((shard, ROWS), jnp.float32),
                compiler_params=params(),
                cost_estimate=cost(half_flops, shard * width),
                name="part_cosines",
            )(units, chosen[2 * k], chosen[2 * k + 1])
            continue
        by_col, by_row, along, local_penalty = pl.pallas_call(
            weight_kernel,
            grid=(shard // wide,),
            in_specs=[smem, unit_spec, whole_chunk, whole_chunk, wide_spec],
            out_specs=[
                wide_spec,
                pl.BlockSpec((ROWS, wide), lambda i: (0, i)),
                pl.BlockSpec((wide, 128), lambda i: (i, 0)),
                pl.BlockSpec((8, 128), lambda i: (0, 0)),
            ],
            out_shape=[
                jax.ShapeDtypeStruct((shard, ROWS), jnp.bfloat16),
                jax.ShapeDtypeStruct((ROWS, shard), jnp.bfloat16),
                jax.ShapeDtypeStruct((shard, 128), jnp.float32),
                jax.ShapeDtypeStruct((8, 128), jnp.float32),
            ],
            compiler_params=params(),
            cost_estimate=cost(half_flops, shard * width),
            name="weights",
        )(delta, units, chosen[2 * k], chosen[2 * k + 1], partial)

    core_side = within % 2
    plane_x = jnp.reshape((within // 2) % 2, (1,)).astype(jnp.int32)
    tall = ROWS + 8
    coded_type = jax.ShapeDtypeStruct((CODED_ROWS, piece // 2), jnp.int32)
    piece_type = jax.ShapeDtypeStruct((ROWS, piece), jnp.float32)
    tile_type = jax.ShapeDtypeStruct((8, 128), jnp.float32)
    vmem = pl.BlockSpec(memory_space=pltpu.VMEM)
    merge_cost = cost(20 * ROWS * piece, 12 * ROWS * piece)

    def row_part(k, side):
        return pl.pallas_call(
            row_kernel,
            grid_spec=pltpu.PrefetchScalarGridSpec(
                num_scalar_prefetch=1,
                grid=(2,),
                in_specs=[
                    pl.BlockSpec((ROWS, shard), lambda i, s: (0, 0)),
                    pl.BlockSpec((8, 128), lambda i, s: (0, 0)),
                    pl.BlockSpec((shard, piece), lambda i, s: (0, 4 * k + 2 * s[0] + i)),
                ],
                out_specs=pl.BlockSpec((tall, piece), lambda i, s: (0, i)),
            ),
            out_shape=jax.ShapeDtypeStruct((tall, step), jnp.float32),
            compiler_params=params(),
            cost_estimate=cost(half_flops // 2, shard * width // 2),
            name="row_part",
        )(jnp.reshape(side, (1,)).astype(jnp.int32), by_row, local_penalty, units)

    def merge(kept, arrived, keep, ties=()):
        tiles = [piece_type, tile_type, coded_type] if keep else [coded_type]
        result = pl.pallas_call(
            functools.partial(merge_kernel, len(arrived), keep),
            in_specs=[vmem] * (2 + len(arrived)) + [any_spec] * len(ties),
            out_specs=[vmem] * len(tiles),
            out_shape=tiles,
            compiler_params=params(),
            cost_estimate=merge_cost,
            name="merge",
        )(*kept, *arrived, *ties)
        return (tuple(result[:2]), result[2]) if keep else result[0]

    kept, msg = [None] * PAIRS, [None] * PAIRS
    for k in range(PAIRS):
        away, near = row_part(k, 1 - core_side), row_part(k, core_side)
        far = per // 2
        while far >= 4:
            moves = each([(w + far, w) for w in range(far)])
            away, near = away + send(away, moves), near + send(near, moves)
            far //= 2
        rest, tile, msg[k] = pl.pallas_call(
            split_kernel,
            in_specs=[smem, vmem, vmem],
            out_specs=[vmem, vmem, vmem],
            out_shape=[piece_type, tile_type, coded_type],
            compiler_params=params(),
            cost_estimate=merge_cost,
            name="split",
        )(plane_x, near, send(away, across_core))
        kept[k] = (rest, tile)

    out_type = jax.ShapeDtypeStruct((shard, width), jnp.float32)
    mark_type = jax.ShapeDtypeStruct((8, 128), jnp.float32)
    mark_spec = pl.BlockSpec((8, 128), lambda i: (0, 0))
    bounds = [1 + -(-(blocks - 1) * p // 4) for p in range(5)]
    grad = None

    def finish(part, tie):
        nonlocal grad
        low, high = bounds[part], bounds[part + 1]
        if high == low:
            return []
        operands = [by_col, decoder, inverse, along, *chosen]
        specs = [
            pl.BlockSpec((BLOCK, ROWS), lambda i: (i + low, 0)),
            pl.BlockSpec((BLOCK, width), lambda i: (i + low, 0)),
            pl.BlockSpec((BLOCK, 128), lambda i: (i + low, 0)),
            pl.BlockSpec((BLOCK, 128), lambda i: (i + low, 0)),
        ] + [whole_chunk] * COUNT
        operands.append(tie)
        specs.append(any_spec)
        aliases = {}
        if grad is not None:
            aliases = {len(operands): 0}
            operands.append(grad)
            specs.append(any_spec)
        rows = (high - low) * BLOCK
        grad, mark = pl.pallas_call(
            finish_kernel,
            grid=(high - low,),
            in_specs=specs,
            out_specs=[pl.BlockSpec((BLOCK, width), lambda i: (i + low, 0)), mark_spec],
            out_shape=[out_type, mark_type],
            input_output_aliases=aliases,
            compiler_params=params(),
            cost_estimate=cost(2 * ROWS * rows * width, 6 * rows * width),
            name="finish",
        )(*operands)
        return [mark]

    lanes = range(4)
    across = [send(msg[k], across_x) for k in range(PAIRS)]
    ties = finish(0, msg[PAIRS - 1])
    for k in range(PAIRS):
        kept[k], msg[k] = merge(kept[k], [across[k]], True, () if k else ties)
    arrivals = [[] for _ in range(PAIRS)]
    for level in range(3):
        for k in range(PAIRS):
            arrivals[k].append(send(msg[k], hop(level, lanes)))
        ties = finish(level + 1, msg[PAIRS - 1])
        for k in range(PAIRS):
            tied = () if k else ties
            if level < 2:
                msg[k] = merge(kept[k], arrivals[k][-1:], False, tied)
            else:
                kept[k], msg[k] = merge(kept[k], arrivals[k], True, tied)

    tile = kept[0][1]
    far = 4
    while far < per:
        moves = each([(w, w + far) for w in range(far)])
        fresh = (within >= far) & (within < 2 * far)
        tile = jnp.where(fresh, send(tile, moves), tile)
        far *= 2
    penalty = jnp.sum(tile) * (DW / (ROWS * latents))

    sums, row_specs = [], []
    narrow = BLOCK // 2
    for k in range(PAIRS):
        sums.append(kept[k][0])
        row_specs.append(pl.BlockSpec((narrow, piece), lambda i: (i, 0)))
        for source in (2, 1, 3):
            arrived = send(msg[k], each([(source, 0)]))
            sums += [arrived, arrived]
            row_specs += [
                pl.BlockSpec((narrow, piece // 2), lambda i: (i, 0)),
                pl.BlockSpec((8, piece // 2), lambda i: (ROWS // 8, 0)),
            ]

    owner = jnp.reshape(here & (within == 0), (1,)).astype(jnp.int32)
    operands = [owner, by_col, decoder, inverse, *chosen, *sums]
    specs = [
        smem,
        pl.BlockSpec((narrow, ROWS), lambda i: (i, 0)),
        pl.BlockSpec((narrow, width), lambda i: (i, 0)),
        pl.BlockSpec((narrow, 128), lambda i: (i, 0)),
    ]
    specs += [whole_chunk] * COUNT
    specs += row_specs
    aliases = {}
    if grad is not None:
        aliases = {len(operands): 0}
        operands.append(grad)
        specs.append(any_spec)
    decoder_grad = pl.pallas_call(
        last_kernel,
        grid=(2,),
        in_specs=specs,
        out_specs=pl.BlockSpec((narrow, width), lambda i: (i, 0)),
        out_shape=out_type,
        scratch_shapes=[pltpu.VMEM((narrow, width), jnp.float32)],
        input_output_aliases=aliases,
        compiler_params=params(),
        name="finish_rows",
    )(*operands)

    return (jnp.reshape(penalty, (1,)), decoder_grad)


def solution(mesh):
    in_specs = (P(("groups", "row"), None), P("groups"))
    out_specs = (P("groups"), P(("groups", "row"), None))
    return jax.shard_map(
        on_device, mesh=mesh, in_specs=in_specs, out_specs=out_specs, check_vma=False
    )
```

```python
import functools
import math

import jax
import jax.numpy as jnp
from jax import lax
from jax.experimental import pallas as pl
from jax.experimental.pallas import tpu as pltpu
from jax.sharding import PartitionSpec as P

DW = 4096
ROWS = 256
BLOCK = 256
WIDE = 512
PAIRS = 2
COUNT = 2 * PAIRS
MIB = 1024 * 1024
NT = (((1,), (1,)), ((), ()))


def params(mib):
    return pltpu.CompilerParams(vmem_limit_bytes=mib * MIB)


def cost(flops, moved):
    return pl.CostEstimate(flops=flops, bytes_accessed=moved, transcendentals=0)


def strip_inverse(ref, rows):
    width = ref.shape[1]
    total = None
    for t in range(0, width, 128):
        v = ref[rows, t : t + 128].astype(jnp.float32)
        total = v * v if total is None else total + v * v
    return 1.0 / jnp.sqrt(jnp.sum(total, axis=1, keepdims=True) + 1e-06)


def head_kernel(decoder_ref, *refs):
    chunk_refs, (held, sems) = refs[:COUNT], refs[COUNT:]
    step = chunk_refs[0].shape[1]
    strip = ROWS // 4

    def fetch(j):
        rows = pl.ds(j * strip, strip)
        return pltpu.make_async_copy(decoder_ref.at[rows, :], held.at[rows, :], sems.at[j])

    for j in range(4):
        fetch(j).start()
    for j in range(4):
        fetch(j).wait()
        rows = slice(j * strip, (j + 1) * strip)
        inverse = strip_inverse(held, rows)
        for k, ref in enumerate(chunk_refs):
            for t in range(0, step, 128):
                v = held[rows, k * step + t : k * step + t + 128].astype(jnp.float32)
                ref[rows, t : t + 128] = (v * inverse).astype(jnp.bfloat16)


def units_kernel(low, count, decoder_ref, *refs):
    units_ref, inverse_ref, held, sems = refs[-4:]
    strip = 64

    def fetch(j):
        return pltpu.make_async_copy(
            decoder_ref.at[pl.ds((low + j) * BLOCK, BLOCK), :], held.at[j % 2], sems.at[j % 2]
        )

    fetch(0).start()
    for j in range(count):
        if j + 1 < count:
            fetch(j + 1).start()
        fetch(j).wait()
        block = held.at[j % 2]
        for base in range(0, BLOCK, strip):
            rows = slice(base, base + strip)
            to = slice((low + j) * BLOCK + base, (low + j) * BLOCK + base + strip)
            inverse = strip_inverse(block, rows)
            inverse_ref[to, :] = jnp.broadcast_to(inverse, (strip, 128))
            for t in range(0, block.shape[1], 128):
                v = block[rows, t : t + 128].astype(jnp.float32)
                units_ref[to, t : t + 128] = (v * inverse).astype(jnp.bfloat16)


def pair_cosines(k, units_ref, rows, low_ref, high_ref):
    step = low_ref.shape[1]
    base = 2 * k * step
    low = lax.dot_general(
        units_ref[rows, base : base + step],
        low_ref[...],
        NT,
        preferred_element_type=jnp.float32,
    )
    high = lax.dot_general(
        units_ref[rows, base + step : base + 2 * step],
        high_ref[...],
        NT,
        preferred_element_type=jnp.float32,
    )
    return low + high


def partial_kernel(k, units_ref, low_ref, high_ref, out_ref):
    size = min(WIDE, units_ref.shape[0])

    def body(j, carry):
        rows = pl.ds(pl.multiple_of(j * size, size), size)
        out_ref[rows, :] = pair_cosines(k, units_ref, rows, low_ref, high_ref)
        return carry

    lax.fori_loop(0, units_ref.shape[0] // size, body, 0)


def weight_kernel(
    k,
    delta_ref,
    units_ref,
    low_ref,
    high_ref,
    partial_ref,
    col_ref,
    row_ref,
    along_ref,
    penalty_ref,
):
    size = min(WIDE, units_ref.shape[0])
    penalty_ref[...] = jnp.zeros_like(penalty_ref)

    def body(j, carry):
        span = pl.ds(pl.multiple_of(j * size, size), size)
        cosines = partial_ref[span, :] + pair_cosines(k, units_ref, span, low_ref, high_ref)
        latents = lax.broadcasted_iota(jnp.int32, (size, ROWS), 0) + (delta_ref[0] + j * size)
        rows = lax.broadcasted_iota(jnp.int32, (size, ROWS), 1)
        inside = (latents >= 0) & (latents < ROWS)
        weight = jnp.where(latents == rows, 0.0, jnp.where(inside, 0.5, 1.0))
        products = weight * cosines
        weighted = products.astype(jnp.bfloat16)
        col_ref[span, :] = weighted
        row_ref[:, span] = products.T.astype(jnp.bfloat16)
        along = jnp.sum(weighted.astype(jnp.float32) * cosines, axis=1, keepdims=True)
        along_ref[span, :] = jnp.broadcast_to(along, (size, 128))
        squares = products * cosines
        squares = squares[:, :128] + squares[:, 128:]
        penalty_ref[...] += jnp.sum(squares.reshape(size // 8, 8, 128), axis=0)
        return carry

    lax.fori_loop(0, units_ref.shape[0] // size, body, 0)


def row_kernel(k, side_ref, row_ref, penalty_ref, units_ref, out_ref):
    tile = out_ref.shape[1] // 2
    first = (2 * k + side_ref[0]) * out_ref.shape[1]
    for i in range(2):
        span = pl.ds(pl.multiple_of(first + i * tile, tile), tile)
        out_ref[:ROWS, i * tile : (i + 1) * tile] = jnp.dot(
            row_ref[...], units_ref[:, span], preferred_element_type=jnp.float32
        )
    out_ref[ROWS:, :] = jnp.concatenate([penalty_ref[...]] * (out_ref.shape[1] // 128), axis=1)


def next_block(low, decoder_ref, held, sems):
    i, size = pl.program_id(0), held.shape[1]

    def fetch(j):
        rows = pl.ds(pl.multiple_of((low + j) * size, size), size)
        slot = lax.rem(j, 2)
        return pltpu.make_async_copy(decoder_ref.at[rows, :], held.at[slot], sems.at[slot])

    @pl.when(i == 0)
    def _():
        fetch(i).start()

    @pl.when(i + 1 < pl.num_programs(0))
    def _():
        fetch(i + 1).start()

    fetch(i).wait()
    return held.at[lax.rem(i, 2)]


def finish_kernel(low, pinned_ref, col_ref, inverse_ref, along_ref, *refs):
    chunks = refs[:COUNT]
    out_ref, mark_ref, held, sems = refs[-4:]
    decoder_ref = next_block(low, pinned_ref, held, sems)
    step = chunks[0].shape[1]
    inverse = inverse_ref[:, :1]
    scale = (2.0 * math.sqrt(DW)) * inverse
    back = scale * (along_ref[:, :1] * inverse)
    for k in range(COUNT):
        span = slice(k * step, (k + 1) * step)
        part = jnp.dot(col_ref[...], chunks[k][...], preferred_element_type=jnp.float32)
        out_ref[:, span] = scale * part - back * decoder_ref[:, span].astype(jnp.float32)
    mark_ref[...] = jnp.zeros_like(mark_ref)


STEPS = 32000.0
CODED_ROWS = ROWS + 16
PENALTY_STEPS = float(1 << 23)


def pack(coded):
    half = coded.shape[1] // 2
    return (coded[:, :half] << 16) | (coded[:, half:] & 0xFFFF)


def unpack(words):
    both = jnp.concatenate([words >> 16, (words << 16) >> 16], axis=1)
    return both.astype(jnp.float32)


def encode(value, penalty, msg_ref):
    top = jnp.max(jnp.abs(value), axis=0, keepdims=True)
    power = jnp.ceil(jnp.log2(jnp.maximum(top, 1e-35)) * 8.0)
    ratio = value * jnp.exp2(power * -0.125)
    coded = ratio * lax.rsqrt(jnp.maximum(jnp.abs(ratio), 1e-30))
    msg_ref[:ROWS, :] = pack(jnp.round(coded * STEPS).astype(jnp.int32))
    power = pack(power.astype(jnp.int32))
    msg_ref[ROWS : ROWS + 8, :] = jnp.broadcast_to(power, (8, power.shape[1]))
    top = jnp.max(jnp.max(penalty, axis=1, keepdims=True), axis=0, keepdims=True)
    power = jnp.ceil(jnp.log2(jnp.maximum(top, 1e-35)))
    coded = jnp.round(penalty * (jnp.exp2(-power) * PENALTY_STEPS)).astype(jnp.int32)
    msg_ref[ROWS + 8 :, :128] = coded
    msg_ref[ROWS + 8 :, 128:] = jnp.broadcast_to(power.astype(jnp.int32), (8, 128))


def decode(words, powers):
    coded = unpack(words)
    scale = jnp.exp2(unpack(powers)[:1, :] * 0.125) * (1.0 / (STEPS * STEPS))
    return coded * jnp.abs(coded) * scale


def decode_at(msg_ref):
    value = decode(msg_ref[:ROWS, :], msg_ref[ROWS : ROWS + 8, :])
    power = msg_ref[ROWS + 8 :, 128:].astype(jnp.float32)
    penalty = msg_ref[ROWS + 8 :, :128].astype(jnp.float32) * (jnp.exp2(power) / PENALTY_STEPS)
    return value, penalty


def split_kernel(odd_ref, mine_ref, theirs_ref, kept_ref, penalty_ref, msg_ref):
    piece = kept_ref.shape[1]
    penalty = mine_ref[ROWS:, :128] + theirs_ref[ROWS:, :128]
    penalty_ref[...] = penalty
    low, high = slice(0, piece), slice(piece, 2 * piece)

    def divide(keep, away):
        kept_ref[...] = mine_ref[:ROWS, keep] + theirs_ref[:ROWS, keep]
        encode(mine_ref[:ROWS, away] + theirs_ref[:ROWS, away], penalty, msg_ref)

    @pl.when(odd_ref[0] == 0)
    def _():
        divide(low, high)

    @pl.when(odd_ref[0] == 1)
    def _():
        divide(high, low)


def merge_kernel(arrived, keep, kept_ref, penalty_ref, *refs):
    value, penalty = kept_ref[...], penalty_ref[...]
    for msg_ref in refs[:arrived]:
        more, more_penalty = decode_at(msg_ref)
        value, penalty = value + more, penalty + more_penalty
    if keep:
        refs[-3][...] = value
        refs[-2][...] = penalty
    encode(value, penalty, refs[-1])


def last_kernel(owner_ref, pinned_ref, col_ref, inverse_ref, *refs):
    chunks, sums = refs[:COUNT], refs[COUNT : COUNT + 7 * PAIRS]
    out_ref, column, held, sems = refs[-4:]
    decoder_ref = next_block(0, pinned_ref, held, sems)
    step = chunks[0].shape[1]
    piece = step // 2
    owner = owner_ref[0] == 1
    total = jnp.zeros((col_ref.shape[0], 128), jnp.float32)
    for k in range(COUNT):
        span = slice(k * step, (k + 1) * step)
        part = jnp.dot(col_ref[...], chunks[k][...], preferred_element_type=jnp.float32)
        own, *coded = sums[7 * (k // 2) : 7 * (k // 2) + 7]
        pieces = [own[...]] + [
            decode(coded[2 * p][...], coded[2 * p + 1][...]) for p in range(3)
        ]
        row_sum = jnp.concatenate(pieces[2 * (k % 2) : 2 * (k % 2) + 2], axis=1)
        part = part + jnp.where(owner, row_sum, 0.0)
        column[:, span] = part
        along = part * decoder_ref[:, span].astype(jnp.float32)
        for t in range(0, step, 128):
            total = total + along[:, t : t + 128]
    inverse = inverse_ref[:, :1]
    scale = (2.0 * math.sqrt(DW)) * inverse
    back = scale * (jnp.sum(total, axis=1, keepdims=True) * inverse * inverse)
    for k in range(COUNT):
        span = slice(k * step, (k + 1) * step)
        out_ref[:, span] = scale * column[:, span] - back * decoder_ref[:, span].astype(
            jnp.float32
        )


def on_device(decoder, quarter):
    shard, width = decoder.shape
    devices = lax.axis_size("row")
    index = lax.axis_index("row")
    per = devices // 4
    latents = shard * devices
    blocks = shard // BLOCK
    step = width // COUNT
    chosen_quarter = quarter[0]
    start = chosen_quarter * (latents // 4)
    place = index // per
    within = index % per
    here = place == chosen_quarter
    even_chip = (within // 2) % 2 == 0
    odd_core = (within % 2) == 1
    smem = pl.BlockSpec(memory_space=pltpu.SMEM)

    def send(value, pairs):
        return lax.ppermute(value, "row", pairs)

    def each(moves):
        return [(z * per + a, z * per + b) for z in range(4) for a, b in moves]

    pinned = pl.BlockSpec(memory_space=pl.ANY)
    vmem = pl.BlockSpec(memory_space=pltpu.VMEM)
    own = pl.pallas_call(
        head_kernel,
        in_specs=[pinned],
        out_specs=[vmem] * COUNT,
        out_shape=[jax.ShapeDtypeStruct((ROWS, step), jnp.bfloat16)] * COUNT,
        scratch_shapes=[
            pltpu.VMEM((ROWS, width), jnp.bfloat16),
            pltpu.SemaphoreType.DMA((4,)),
        ],
        compiler_params=params(50),
        cost_estimate=cost(4 * ROWS * width, 4 * ROWS * width),
        name="head_units",
    )(decoder)

    any_spec = pl.BlockSpec(memory_space=pl.ANY)
    across_x = each([(0, 2), (2, 0), (1, 3), (3, 1)])
    across_core = each([(0, 1), (1, 0), (2, 3), (3, 2)])
    piece = step // 2

    def hop(level, lanes):
        moves = (((0, 1), (3, 2)), ((1, 2), (2, 1)), ((2, 3), (1, 0)))[level]
        return [(a * per + w, b * per + w) for a, b in moves for w in lanes]

    unit_bounds = [0, blocks // 4, 5 * blocks // 8, blocks]
    made = [None, None]

    def make_units(part, tie):
        low, high = unit_bounds[part], unit_bounds[part + 1]
        if high == low:
            return True
        operands = [decoder, tie]
        specs = [pinned, any_spec]
        aliases = {}
        if made[0] is not None:
            aliases = {2: 0, 3: 1}
            operands += made
            specs += [vmem, vmem]
        made[:] = pl.pallas_call(
            functools.partial(units_kernel, low, high - low),
            in_specs=specs,
            out_specs=[vmem, vmem],
            out_shape=[
                jax.ShapeDtypeStruct((shard, width), jnp.bfloat16),
                jax.ShapeDtypeStruct((shard, 128), jnp.float32),
            ],
            scratch_shapes=[
                pltpu.VMEM((2, BLOCK, width), jnp.bfloat16),
                pltpu.SemaphoreType.DMA((2,)),
            ],
            input_output_aliases=aliases,
            compiler_params=params(24),
            cost_estimate=cost(4 * BLOCK * width, 4 * (high - low) * BLOCK * width),
            name="units",
        )(*operands)
        return made[1][low * BLOCK, 0] > 0

    near = jnp.where(place == 1, chosen_quarter == 0, chosen_quarter == 3)
    middle = (place == 1) | (place == 2)
    mine, first, second, third, held = ([None] * PAIRS for _ in range(5))
    across = [send(own[2 * k + 1], each([(0, 2)])) for k in range(PAIRS)]
    done = make_units(0, own[0])
    for k in range(PAIRS):
        takes = (within == 2) & done if k == 0 else within == 2
        mine[k] = jnp.where(takes, across[k], own[2 * k])
    for k in range(PAIRS):
        first[k] = send(mine[k], hop(0, (0, 2)))
    done = make_units(1, mine[PAIRS - 1])
    going = [None] * PAIRS
    for k in range(PAIRS):
        keeps = here & done if k == 0 else here
        going[k] = jnp.where(keeps, mine[k], first[k])
        second[k] = send(going[k], hop(1, (0, 2)))
    for k in range(PAIRS):
        going[k] = jnp.where(here, mine[k], second[k])
        third[k] = send(going[k], hop(2, (0, 2)))
    done = make_units(2, going[PAIRS - 1])
    units, inverse = made
    for k in range(PAIRS):
        inner = jnp.where(near, first[k], second[k])
        keeps = here & done if k == 0 else here
        held[k] = jnp.where(keeps, mine[k], jnp.where(middle, inner, third[k]))
    chosen = []
    for k in range(PAIRS):
        other = send(held[k], each([(0, 2), (2, 0)]))
        core_held = send(held[k], each([(0, 1), (2, 3)]))
        core_other = send(other, each([(0, 1), (2, 3)]))
        one = jnp.where(odd_core, core_held, held[k])
        two = jnp.where(odd_core, core_other, other)
        pair = [jnp.where(even_chip, one, two), jnp.where(even_chip, two, one)]
        far = 4
        while far < per:
            moves = each([(w, w + far) for w in range(far)])
            fresh = (within >= far) & (within < 2 * far)
            pair = [jnp.where(fresh, send(value, moves), value) for value in pair]
            far *= 2
        chosen += pair

    delta = jnp.reshape(index * shard - start, (1,)).astype(jnp.int32)
    whole_chunk = pl.BlockSpec((ROWS, step), lambda i: (0, 0))
    half_flops = ROWS * shard * width
    partial = pl.pallas_call(
        functools.partial(partial_kernel, 0),
        in_specs=[vmem] * 3,
        out_specs=vmem,
        out_shape=jax.ShapeDtypeStruct((shard, ROWS), jnp.float32),
        compiler_params=params(24),
        cost_estimate=cost(half_flops, shard * width),
        name="part_cosines",
    )(units, chosen[0], chosen[1])
    by_col, by_row, along, local_penalty = pl.pallas_call(
        functools.partial(weight_kernel, 1),
        in_specs=[smem] + [vmem] * 4,
        out_specs=[vmem] * 4,
        out_shape=[
            jax.ShapeDtypeStruct((shard, ROWS), jnp.bfloat16),
            jax.ShapeDtypeStruct((ROWS, shard), jnp.bfloat16),
            jax.ShapeDtypeStruct((shard, 128), jnp.float32),
            jax.ShapeDtypeStruct((8, 128), jnp.float32),
        ],
        compiler_params=params(24),
        cost_estimate=cost(half_flops, shard * width),
        name="weights",
    )(delta, units, chosen[2], chosen[3], partial)

    core_side = within % 2
    plane_x = jnp.reshape((within // 2) % 2, (1,)).astype(jnp.int32)
    tall = ROWS + 8
    coded_type = jax.ShapeDtypeStruct((CODED_ROWS, piece // 2), jnp.int32)
    piece_type = jax.ShapeDtypeStruct((ROWS, piece), jnp.float32)
    tile_type = jax.ShapeDtypeStruct((8, 128), jnp.float32)
    merge_cost = cost(20 * ROWS * piece, 12 * ROWS * piece)

    def row_part(k, side):
        return pl.pallas_call(
            functools.partial(row_kernel, k),
            in_specs=[smem, vmem, vmem, vmem],
            out_specs=vmem,
            out_shape=jax.ShapeDtypeStruct((tall, step), jnp.float32),
            compiler_params=params(24),
            cost_estimate=cost(half_flops // 2, shard * width // 2),
            name="row_part",
        )(jnp.reshape(side, (1,)).astype(jnp.int32), by_row, local_penalty, units)

    def merge(kept, arrived, keep, ties=()):
        tiles = [piece_type, tile_type, coded_type] if keep else [coded_type]
        result = pl.pallas_call(
            functools.partial(merge_kernel, len(arrived), keep),
            in_specs=[vmem] * (2 + len(arrived)) + [any_spec] * len(ties),
            out_specs=[vmem] * len(tiles),
            out_shape=tiles,
            compiler_params=params(24),
            cost_estimate=merge_cost,
            name="merge",
        )(*kept, *arrived, *ties)
        return (tuple(result[:2]), result[2]) if keep else result[0]

    kept, msg = [None] * PAIRS, [None] * PAIRS
    for k in range(PAIRS):
        away, near = row_part(k, 1 - core_side), row_part(k, core_side)
        far = per // 2
        while far >= 4:
            moves = each([(w + far, w) for w in range(far)])
            away, near = away + send(away, moves), near + send(near, moves)
            far //= 2
        rest, tile, msg[k] = pl.pallas_call(
            split_kernel,
            in_specs=[smem, vmem, vmem],
            out_specs=[vmem, vmem, vmem],
            out_shape=[piece_type, tile_type, coded_type],
            compiler_params=params(24),
            cost_estimate=merge_cost,
            name="split",
        )(plane_x, near, send(away, across_core))
        kept[k] = (rest, tile)

    out_type = jax.ShapeDtypeStruct((shard, width), jnp.float32)
    mark_type = jax.ShapeDtypeStruct((8, 128), jnp.float32)
    mark_spec = pl.BlockSpec((8, 128), lambda i: (0, 0))
    bounds = [1 + -(-(blocks - 1) * p // 4) for p in range(5)]
    grad = None

    def finish(part, tie):
        nonlocal grad
        low, high = bounds[part], bounds[part + 1]
        if high == low:
            return []
        operands = [decoder, by_col, inverse, along, *chosen]
        specs = [
            pinned,
            pl.BlockSpec((BLOCK, ROWS), lambda i: (i + low, 0)),
            pl.BlockSpec((BLOCK, 128), lambda i: (i + low, 0)),
            pl.BlockSpec((BLOCK, 128), lambda i: (i + low, 0)),
        ] + [whole_chunk] * COUNT
        operands.append(tie)
        specs.append(any_spec)
        aliases = {}
        if grad is not None:
            aliases = {len(operands): 0}
            operands.append(grad)
            specs.append(any_spec)
        rows = (high - low) * BLOCK
        grad, mark = pl.pallas_call(
            functools.partial(finish_kernel, low),
            grid=(high - low,),
            in_specs=specs,
            out_specs=[pl.BlockSpec((BLOCK, width), lambda i: (i + low, 0)), mark_spec],
            out_shape=[out_type, mark_type],
            scratch_shapes=[
                pltpu.VMEM((2, BLOCK, width), jnp.bfloat16),
                pltpu.SemaphoreType.DMA((2,)),
            ],
            input_output_aliases=aliases,
            compiler_params=params(50),
            cost_estimate=cost(2 * ROWS * rows * width, 6 * rows * width),
            name="finish",
        )(*operands)
        return [mark]

    lanes = range(4)
    across = [send(msg[k], across_x) for k in range(PAIRS)]
    ties = finish(0, msg[PAIRS - 1])
    for k in range(PAIRS):
        kept[k], msg[k] = merge(kept[k], [across[k]], True, () if k else ties)
    arrivals = [[] for _ in range(PAIRS)]
    for level in range(3):
        for k in range(PAIRS):
            arrivals[k].append(send(msg[k], hop(level, lanes)))
        ties = finish(level + 1, msg[PAIRS - 1])
        for k in range(PAIRS):
            tied = () if k else ties
            if level < 2:
                msg[k] = merge(kept[k], arrivals[k][-1:], False, tied)
            else:
                kept[k], msg[k] = merge(kept[k], arrivals[k], True, tied)

    tile = kept[0][1]
    far = 4
    while far < per:
        moves = each([(w, w + far) for w in range(far)])
        fresh = (within >= far) & (within < 2 * far)
        tile = jnp.where(fresh, send(tile, moves), tile)
        far *= 2
    penalty = jnp.sum(tile) * (DW / (ROWS * latents))

    sums, row_specs = [], []
    narrow = BLOCK // 2
    for k in range(PAIRS):
        sums.append(kept[k][0])
        row_specs.append(pl.BlockSpec((narrow, piece), lambda i: (i, 0)))
        for source in (2, 1, 3):
            arrived = send(msg[k], each([(source, 0)]))
            sums += [arrived, arrived]
            row_specs += [
                pl.BlockSpec((narrow, piece // 2), lambda i: (i, 0)),
                pl.BlockSpec((8, piece // 2), lambda i: (ROWS // 8, 0)),
            ]

    owner = jnp.reshape(here & (within == 0), (1,)).astype(jnp.int32)
    operands = [owner, decoder, by_col, inverse, *chosen, *sums]
    specs = [
        smem,
        pinned,
        pl.BlockSpec((narrow, ROWS), lambda i: (i, 0)),
        pl.BlockSpec((narrow, 128), lambda i: (i, 0)),
    ]
    specs += [whole_chunk] * COUNT
    specs += row_specs
    aliases = {}
    if grad is not None:
        aliases = {len(operands): 0}
        operands.append(grad)
        specs.append(any_spec)
    decoder_grad = pl.pallas_call(
        last_kernel,
        grid=(2,),
        in_specs=specs,
        out_specs=pl.BlockSpec((narrow, width), lambda i: (i, 0)),
        out_shape=out_type,
        scratch_shapes=[
            pltpu.VMEM((narrow, width), jnp.float32),
            pltpu.VMEM((2, narrow, width), jnp.bfloat16),
            pltpu.SemaphoreType.DMA((2,)),
        ],
        input_output_aliases=aliases,
        compiler_params=params(50),
        name="finish_rows",
    )(*operands)

    return (jnp.reshape(penalty, (1,)), decoder_grad)


def solution(mesh):
    in_specs = (P(("groups", "row"), None), P("groups"))
    out_specs = (P("groups"), P(("groups", "row"), None))
    return jax.shard_map(
        on_device, mesh=mesh, in_specs=in_specs, out_specs=out_specs, check_vma=False
    )
```

```python
import functools
import math

import jax
import jax.numpy as jnp
from jax import lax
from jax.experimental import pallas as pl
from jax.experimental.pallas import tpu as pltpu
from jax.sharding import PartitionSpec as P

DW = 4096
ROWS = 256
BLOCK = 256
WIDE = 512
PAIRS = 2
COUNT = 2 * PAIRS
MIB = 1024 * 1024
NT = (((1,), (1,)), ((), ()))


def params(mib):
    return pltpu.CompilerParams(vmem_limit_bytes=mib * MIB)


def cost(flops, moved):
    return pl.CostEstimate(flops=flops, bytes_accessed=moved, transcendentals=0)


def strip_inverse(ref, rows):
    width = ref.shape[1]
    total = None
    for t in range(0, width, 128):
        v = ref[rows, t : t + 128].astype(jnp.float32)
        total = v * v if total is None else total + v * v
    return 1.0 / jnp.sqrt(jnp.sum(total, axis=1, keepdims=True) + 1e-06)


def head_kernel(flags_ref, decoder_ref, *refs):
    chunk_refs, (held, sems) = refs[:COUNT], refs[COUNT:]
    step = chunk_refs[0].shape[1]
    strip = ROWS // 4

    def fetch(j):
        rows = pl.ds(j * strip, strip)
        return pltpu.make_async_copy(decoder_ref.at[rows, :], held.at[rows, :], sems.at[j])

    for j in range(4):
        fetch(j).start()
    for j in range(4):
        fetch(j).wait()
        rows = slice(j * strip, (j + 1) * strip)
        inverse = strip_inverse(held, rows)
        for k, ref in enumerate(chunk_refs):
            for t in range(0, step, 128):
                v = held[rows, k * step + t : k * step + t + 128].astype(jnp.float32)
                ref[rows, t : t + 128] = (v * inverse).astype(jnp.bfloat16)


def units_kernel(low, count, decoder_ref, *refs):
    units_ref, inverse_ref, held, sems = refs[-4:]
    strip = 64

    def fetch(j):
        return pltpu.make_async_copy(
            decoder_ref.at[pl.ds((low + j) * BLOCK, BLOCK), :], held.at[j % 2], sems.at[j % 2]
        )

    fetch(0).start()
    for j in range(count):
        if j + 1 < count:
            fetch(j + 1).start()
        fetch(j).wait()
        block = held.at[j % 2]
        for base in range(0, BLOCK, strip):
            rows = slice(base, base + strip)
            to = slice(j * BLOCK + base, j * BLOCK + base + strip)
            inverse = strip_inverse(block, rows)
            inverse_ref[to, :] = jnp.broadcast_to(inverse, (strip, 128))
            for t in range(0, block.shape[1], 128):
                v = block[rows, t : t + 128].astype(jnp.float32)
                units_ref[to, t : t + 128] = (v * inverse).astype(jnp.bfloat16)


def pair_cosines(k, units_ref, rows, low_ref, high_ref):
    step = low_ref.shape[1]
    base = 2 * k * step
    low = lax.dot_general(
        units_ref[rows, base : base + step],
        low_ref[...],
        NT,
        preferred_element_type=jnp.float32,
    )
    high = lax.dot_general(
        units_ref[rows, base + step : base + 2 * step],
        high_ref[...],
        NT,
        preferred_element_type=jnp.float32,
    )
    return low + high


def pick_kernel(slots, count, flags_ref, *refs):
    for slot, out_ref in zip(slots, refs[-len(slots) :]):
        for c in range(count):

            @pl.when(flags_ref[slot] == c)
            def _(out_ref=out_ref, c=c):
                out_ref[...] = refs[c][...]


def partial_kernel(k, parts, low_ref, high_ref, *refs):
    out_ref = refs[-1]
    base = 0
    for units_ref in refs[:parts]:
        count = units_ref.shape[0]
        size = min(WIDE, count)

        def body(j, carry, units_ref=units_ref, size=size, base=base):
            rows = pl.ds(pl.multiple_of(j * size, size), size)
            to = pl.ds(pl.multiple_of(base + j * size, size), size)
            out_ref[to, :] = pair_cosines(k, units_ref, rows, low_ref, high_ref)
            return carry

        lax.fori_loop(0, count // size, body, 0)
        base += count


def weight_kernel(k, parts, delta_ref, low_ref, high_ref, partial_ref, *refs):
    col_ref, row_ref, factor_ref, penalty_ref = refs[-4:]
    penalty_ref[...] = jnp.zeros_like(penalty_ref)
    base = 0
    for units_ref, inverse_ref in zip(refs[:parts], refs[parts : 2 * parts]):
        count = units_ref.shape[0]
        size = min(WIDE, count)

        def body(j, carry, units_ref=units_ref, inverse_ref=inverse_ref, size=size, base=base):
            here = pl.ds(pl.multiple_of(j * size, size), size)
            first = base + j * size
            span = pl.ds(pl.multiple_of(first, size), size)
            cosines = partial_ref[span, :] + pair_cosines(k, units_ref, here, low_ref, high_ref)
            latents = lax.broadcasted_iota(jnp.int32, (size, ROWS), 0) + (delta_ref[0] + first)
            rows = lax.broadcasted_iota(jnp.int32, (size, ROWS), 1)
            inside = (latents >= 0) & (latents < ROWS)
            weight = jnp.where(latents == rows, 0.0, jnp.where(inside, 0.5, 1.0))
            products = weight * cosines
            weighted = products.astype(jnp.bfloat16)
            col_ref[span, :] = weighted
            row_ref[:, span] = products.T.astype(jnp.bfloat16)
            along = jnp.sum(weighted.astype(jnp.float32) * cosines, axis=1, keepdims=True)
            inverse = inverse_ref[here, :]
            lanes = lax.broadcasted_iota(jnp.int32, (size, 128), 1)
            factor_ref[span, :] = jnp.where(lanes < 64, inverse, along * inverse)
            squares = products * cosines
            squares = squares[:, :128] + squares[:, 128:]
            penalty_ref[...] += jnp.sum(squares.reshape(size // 8, 8, 128), axis=0)
            return carry

        lax.fori_loop(0, count // size, body, 0)
        base += count


def row_kernel(k, parts, side_ref, row_ref, penalty_ref, *refs):
    out_ref = refs[-1]
    tile = out_ref.shape[1] // 2
    first = (2 * k + side_ref[0]) * out_ref.shape[1]
    for i in range(2):
        span = pl.ds(pl.multiple_of(first + i * tile, tile), tile)
        total, base = None, 0
        for units_ref in refs[:parts]:
            count = units_ref.shape[0]
            part = jnp.dot(
                row_ref[:, base : base + count],
                units_ref[:, span],
                preferred_element_type=jnp.float32,
            )
            total = part if total is None else total + part
            base += count
        out_ref[:ROWS, i * tile : (i + 1) * tile] = total
    out_ref[ROWS:, :] = jnp.concatenate([penalty_ref[...]] * (out_ref.shape[1] // 128), axis=1)


def finish_kernel(col_ref, decoder_ref, factor_ref, *refs):
    chunks = refs[:COUNT]
    out_ref, mark_ref = refs[-2:]
    step = chunks[0].shape[1]
    scale = (2.0 * math.sqrt(DW)) * factor_ref[:, :1]
    back = scale * factor_ref[:, 64:65]
    for k in range(COUNT):
        span = slice(k * step, (k + 1) * step)
        part = jnp.dot(col_ref[...], chunks[k][...], preferred_element_type=jnp.float32)
        out_ref[:, span] = scale * part - back * decoder_ref[:, span].astype(jnp.float32)
    mark_ref[...] = jnp.zeros_like(mark_ref)


STEPS = 32000.0
CODED_ROWS = ROWS + 16
PENALTY_STEPS = float(1 << 23)


def pack(coded):
    half = coded.shape[1] // 2
    return (coded[:, :half] << 16) | (coded[:, half:] & 0xFFFF)


def unpack(words):
    both = jnp.concatenate([words >> 16, (words << 16) >> 16], axis=1)
    return both.astype(jnp.float32)


def encode(value, penalty, msg_ref):
    top = jnp.max(jnp.abs(value), axis=0, keepdims=True)
    power = jnp.ceil(jnp.log2(jnp.maximum(top, 1e-35)) * 8.0)
    ratio = value * jnp.exp2(power * -0.125)
    coded = ratio * lax.rsqrt(jnp.maximum(jnp.abs(ratio), 1e-30))
    msg_ref[:ROWS, :] = pack(jnp.round(coded * STEPS).astype(jnp.int32))
    power = pack(power.astype(jnp.int32))
    msg_ref[ROWS : ROWS + 8, :] = jnp.broadcast_to(power, (8, power.shape[1]))
    top = jnp.max(jnp.max(penalty, axis=1, keepdims=True), axis=0, keepdims=True)
    power = jnp.ceil(jnp.log2(jnp.maximum(top, 1e-35)))
    coded = jnp.round(penalty * (jnp.exp2(-power) * PENALTY_STEPS)).astype(jnp.int32)
    msg_ref[ROWS + 8 :, :128] = coded
    msg_ref[ROWS + 8 :, 128:] = jnp.broadcast_to(power.astype(jnp.int32), (8, 128))


def decode(words, powers):
    coded = unpack(words)
    scale = jnp.exp2(unpack(powers)[:1, :] * 0.125) * (1.0 / (STEPS * STEPS))
    return coded * jnp.abs(coded) * scale


def decode_at(msg_ref):
    value = decode(msg_ref[:ROWS, :], msg_ref[ROWS : ROWS + 8, :])
    power = msg_ref[ROWS + 8 :, 128:].astype(jnp.float32)
    penalty = msg_ref[ROWS + 8 :, :128].astype(jnp.float32) * (jnp.exp2(power) / PENALTY_STEPS)
    return value, penalty


def split_kernel(odd_ref, mine_ref, theirs_ref, kept_ref, penalty_ref, msg_ref):
    piece = kept_ref.shape[1]
    penalty = mine_ref[ROWS:, :128] + theirs_ref[ROWS:, :128]
    penalty_ref[...] = penalty
    low, high = slice(0, piece), slice(piece, 2 * piece)

    def divide(keep, away):
        kept_ref[...] = mine_ref[:ROWS, keep] + theirs_ref[:ROWS, keep]
        encode(mine_ref[:ROWS, away] + theirs_ref[:ROWS, away], penalty, msg_ref)

    @pl.when(odd_ref[0] == 0)
    def _():
        divide(low, high)

    @pl.when(odd_ref[0] == 1)
    def _():
        divide(high, low)


def merge_kernel(arrived, keep, kept_ref, penalty_ref, *refs):
    value, penalty = kept_ref[...], penalty_ref[...]
    for msg_ref in refs[:arrived]:
        more, more_penalty = decode_at(msg_ref)
        value, penalty = value + more, penalty + more_penalty
    if keep:
        refs[-3][...] = value
        refs[-2][...] = penalty
    encode(value, penalty, refs[-1])


def last_kernel(share, owner_ref, col_ref, decoder_ref, factor_ref, tile_ref, *refs):
    chunks, sums = refs[:COUNT], refs[COUNT : COUNT + 7 * PAIRS]
    out_ref, penalty_ref, column = refs[-3:]
    penalty_ref[0] = jnp.sum(tile_ref[...]) * share
    step = chunks[0].shape[1]
    piece = step // 2
    owner = owner_ref[0] == 1
    total = jnp.zeros((col_ref.shape[0], 128), jnp.float32)
    for k in range(COUNT):
        span = slice(k * step, (k + 1) * step)
        part = jnp.dot(col_ref[...], chunks[k][...], preferred_element_type=jnp.float32)
        own, *coded = sums[7 * (k // 2) : 7 * (k // 2) + 7]
        pieces = [own[...]] + [
            decode(coded[2 * p][...], coded[2 * p + 1][...]) for p in range(3)
        ]
        row_sum = jnp.concatenate(pieces[2 * (k % 2) : 2 * (k % 2) + 2], axis=1)
        part = part + jnp.where(owner, row_sum, 0.0)
        column[:, span] = part
        along = part * decoder_ref[:, span].astype(jnp.float32)
        for t in range(0, step, 128):
            total = total + along[:, t : t + 128]
    inverse = factor_ref[:, :1]
    scale = (2.0 * math.sqrt(DW)) * inverse
    back = scale * (jnp.sum(total, axis=1, keepdims=True) * inverse * inverse)
    for k in range(COUNT):
        span = slice(k * step, (k + 1) * step)
        out_ref[:, span] = scale * column[:, span] - back * decoder_ref[:, span].astype(
            jnp.float32
        )


def on_device(decoder, quarter):
    shard, width = decoder.shape
    devices = lax.axis_size("row")
    index = lax.axis_index("row")
    per = devices // 4
    latents = shard * devices
    blocks = shard // BLOCK
    step = width // COUNT
    chosen_quarter = quarter[0]
    start = chosen_quarter * (latents // 4)
    place = index // per
    within = index % per
    here = place == chosen_quarter
    even_chip = (within // 2) % 2 == 0
    smem = pl.BlockSpec(memory_space=pltpu.SMEM)

    def send(value, pairs):
        return lax.ppermute(value, "row", pairs)

    def each(moves):
        return [(z * per + a, z * per + b) for z in range(4) for a, b in moves]

    near = jnp.where(place == 1, chosen_quarter == 0, chosen_quarter == 3)
    middle = (place == 1) | (place == 2)
    reached = jnp.where(here, 0, jnp.where(middle, jnp.where(near, 1, 2), 3))
    core_index = within % 2
    fresh = [(within >= 4 << n) & (within < 8 << n) for n in range((per // 4).bit_length() - 1)]
    TAKES, WAITS, REACHED, LOW, HIGH, FRESH = range(6)
    flags = jnp.stack(
        [
            jnp.where(within == 2, 1, 0),
            jnp.where(here, 0, 1),
            reached,
            jnp.where(even_chip, 0, 2) + core_index,
            jnp.where(even_chip, 2, 0) + core_index,
        ]
        + [jnp.where(value, 1, 0) for value in fresh]
    ).astype(jnp.int32)

    pinned = pl.BlockSpec(memory_space=pl.ANY)
    any_spec = pinned
    vmem = pl.BlockSpec(memory_space=pltpu.VMEM)
    chunk_type = jax.ShapeDtypeStruct((ROWS, step), jnp.bfloat16)
    own = pl.pallas_call(
        head_kernel,
        in_specs=[smem, pinned],
        out_specs=[vmem] * COUNT,
        out_shape=[chunk_type] * COUNT,
        scratch_shapes=[
            pltpu.VMEM((ROWS, width), jnp.bfloat16),
            pltpu.SemaphoreType.DMA((4,)),
        ],
        compiler_params=params(50),
        cost_estimate=cost(4 * ROWS * width, 4 * ROWS * width),
        name="head_units",
    )(flags, decoder)

    across_x = each([(0, 2), (2, 0), (1, 3), (3, 1)])
    across_core = each([(0, 1), (1, 0), (2, 3), (3, 2)])
    piece = step // 2

    def hop(level, lanes):
        moves = (((0, 1), (3, 2)), ((1, 2), (2, 1)), ((2, 3), (1, 0)))[level]
        return [(a * per + w, b * per + w) for a, b in moves for w in lanes]

    def pick(slots, candidates, ties=()):
        return pl.pallas_call(
            functools.partial(pick_kernel, slots, len(candidates)),
            in_specs=[smem] + [vmem] * len(candidates) + [any_spec] * len(ties),
            out_specs=[vmem] * len(slots),
            out_shape=[chunk_type] * len(slots),
            compiler_params=params(12),
            cost_estimate=cost(ROWS * step, 4 * ROWS * step),
            name="pick",
        )(flags, *candidates, *ties)

    unit_bounds = [0, blocks // 4, blocks // 2, blocks]
    units, inverses = [], []

    def make_units(part, tie):
        low, high = unit_bounds[part], unit_bounds[part + 1]
        if high == low:
            return []
        rows = (high - low) * BLOCK
        made = pl.pallas_call(
            functools.partial(units_kernel, low, high - low),
            in_specs=[pinned, any_spec],
            out_specs=[vmem, vmem],
            out_shape=[
                jax.ShapeDtypeStruct((rows, width), jnp.bfloat16),
                jax.ShapeDtypeStruct((rows, 128), jnp.float32),
            ],
            scratch_shapes=[
                pltpu.VMEM((2, BLOCK, width), jnp.bfloat16),
                pltpu.SemaphoreType.DMA((2,)),
            ],
            compiler_params=params((46, 44, 34)[part]),
            cost_estimate=cost(4 * rows * width, 4 * rows * width),
            name="units",
        )(decoder, tie)
        units.append(made[0])
        inverses.append(made[1])
        return [made[1]]

    mine, first, second, third, held = ([None] * PAIRS for _ in range(5))
    across = [send(own[2 * k + 1], each([(0, 2)])) for k in range(PAIRS)]
    done = make_units(0, own[0])
    for k in range(PAIRS):
        [mine[k]] = pick([TAKES], [own[2 * k], across[k]], () if k else done)
        first[k] = send(mine[k], hop(0, (0, 2)))
    done = make_units(1, mine[PAIRS - 1])
    for k in range(PAIRS):
        [going] = pick([WAITS], [mine[k], first[k]], () if k else done)
        second[k] = send(going, hop(1, (0, 2)))
    for k in range(PAIRS):
        [going] = pick([WAITS], [mine[k], second[k]])
        third[k] = send(going, hop(2, (0, 2)))
    for k in range(PAIRS):
        [held[k]] = pick([REACHED], [mine[k], first[k], second[k], third[k]])
    done = make_units(2, held[PAIRS - 1])
    chosen = []
    for k in range(PAIRS):
        other = send(held[k], each([(0, 2), (2, 0)]))
        core_held = send(held[k], each([(0, 1), (2, 3)]))
        core_other = send(other, each([(0, 1), (2, 3)]))
        pair = pick(
            [LOW, HIGH], [held[k], core_held, other, core_other], () if k else done
        )
        for n in range(len(fresh)):
            moves = each([(w, w + (4 << n)) for w in range(4 << n)])
            pair = [pick([FRESH + n], [value, send(value, moves)])[0] for value in pair]
        chosen += pair

    delta = jnp.reshape(index * shard - start, (1,)).astype(jnp.int32)
    whole_chunk = pl.BlockSpec((ROWS, step), lambda i: (0, 0))
    half_flops = ROWS * shard * width
    parts = len(units)
    partial = pl.pallas_call(
        functools.partial(partial_kernel, 0, parts),
        in_specs=[vmem] * (2 + parts),
        out_specs=vmem,
        out_shape=jax.ShapeDtypeStruct((shard, ROWS), jnp.float32),
        compiler_params=params(16),
        cost_estimate=cost(half_flops, shard * width),
        name="part_cosines",
    )(chosen[0], chosen[1], *units)
    by_col, by_row, factors, local_penalty = pl.pallas_call(
        functools.partial(weight_kernel, 1, parts),
        in_specs=[smem] + [vmem] * (3 + 2 * parts),
        out_specs=[vmem] * 4,
        out_shape=[
            jax.ShapeDtypeStruct((shard, ROWS), jnp.bfloat16),
            jax.ShapeDtypeStruct((ROWS, shard), jnp.bfloat16),
            jax.ShapeDtypeStruct((shard, 128), jnp.float32),
            jax.ShapeDtypeStruct((8, 128), jnp.float32),
        ],
        compiler_params=params(16),
        cost_estimate=cost(half_flops, shard * width),
        name="weights",
    )(delta, chosen[2], chosen[3], partial, *units, *inverses)

    core_side = within % 2
    plane_x = jnp.reshape((within // 2) % 2, (1,)).astype(jnp.int32)
    tall = ROWS + 8
    coded_type = jax.ShapeDtypeStruct((CODED_ROWS, piece // 2), jnp.int32)
    piece_type = jax.ShapeDtypeStruct((ROWS, piece), jnp.float32)
    tile_type = jax.ShapeDtypeStruct((8, 128), jnp.float32)
    merge_cost = cost(20 * ROWS * piece, 12 * ROWS * piece)

    def row_part(k, side):
        return pl.pallas_call(
            functools.partial(row_kernel, k, parts),
            in_specs=[smem] + [vmem] * (2 + parts),
            out_specs=vmem,
            out_shape=jax.ShapeDtypeStruct((tall, step), jnp.float32),
            compiler_params=params(24),
            cost_estimate=cost(half_flops // 2, shard * width // 2),
            name="row_part",
        )(jnp.reshape(side, (1,)).astype(jnp.int32), by_row, local_penalty, *units)

    def merge(kept, arrived, keep, ties=()):
        tiles = [piece_type, tile_type, coded_type] if keep else [coded_type]
        result = pl.pallas_call(
            functools.partial(merge_kernel, len(arrived), keep),
            in_specs=[vmem] * (2 + len(arrived)) + [any_spec] * len(ties),
            out_specs=[vmem] * len(tiles),
            out_shape=tiles,
            compiler_params=params(24),
            cost_estimate=merge_cost,
            name="merge",
        )(*kept, *arrived, *ties)
        return (tuple(result[:2]), result[2]) if keep else result[0]

    kept, msg = [None] * PAIRS, [None] * PAIRS
    for k in range(PAIRS):
        away, near = row_part(k, 1 - core_side), row_part(k, core_side)
        far = per // 2
        while far >= 4:
            moves = each([(w + far, w) for w in range(far)])
            away, near = away + send(away, moves), near + send(near, moves)
            far //= 2
        rest, tile, msg[k] = pl.pallas_call(
            split_kernel,
            in_specs=[smem, vmem, vmem],
            out_specs=[vmem, vmem, vmem],
            out_shape=[piece_type, tile_type, coded_type],
            compiler_params=params(24),
            cost_estimate=merge_cost,
            name="split",
        )(plane_x, near, send(away, across_core))
        kept[k] = (rest, tile)

    out_type = jax.ShapeDtypeStruct((shard, width), jnp.float32)
    mark_type = jax.ShapeDtypeStruct((8, 128), jnp.float32)
    mark_spec = pl.BlockSpec((8, 128), lambda i: (0, 0))
    bounds = [1 + -(-(blocks - 1) * p // 4) for p in range(5)]
    grad = None

    def finish(part, tie):
        nonlocal grad
        low, high = bounds[part], bounds[part + 1]
        if high == low:
            return []
        operands = [by_col, decoder, factors, *chosen]
        specs = [
            pl.BlockSpec((BLOCK, ROWS), lambda i: (i + low, 0)),
            pl.BlockSpec((BLOCK, width), lambda i: (i + low, 0)),
            pl.BlockSpec((BLOCK, 128), lambda i: (i + low, 0)),
        ] + [whole_chunk] * COUNT
        operands.append(tie)
        specs.append(any_spec)
        aliases = {}
        if grad is not None:
            aliases = {len(operands): 0}
            operands.append(grad)
            specs.append(any_spec)
        rows = (high - low) * BLOCK
        grad, mark = pl.pallas_call(
            finish_kernel,
            grid=(high - low,),
            in_specs=specs,
            out_specs=[pl.BlockSpec((BLOCK, width), lambda i: (i + low, 0)), mark_spec],
            out_shape=[out_type, mark_type],
            input_output_aliases=aliases,
            compiler_params=params(50),
            cost_estimate=cost(2 * ROWS * rows * width, 6 * rows * width),
            name="finish",
        )(*operands)
        return [mark]

    lanes = range(4)
    across = [send(msg[k], across_x) for k in range(PAIRS)]
    ties = finish(0, msg[PAIRS - 1])
    for k in range(PAIRS):
        kept[k], msg[k] = merge(kept[k], [across[k]], True, () if k else ties)
    arrivals = [[] for _ in range(PAIRS)]
    for level in range(3):
        for k in range(PAIRS):
            arrivals[k].append(send(msg[k], hop(level, lanes)))
        ties = finish(level + 1, msg[PAIRS - 1])
        for k in range(PAIRS):
            tied = () if k else ties
            if level < 2:
                msg[k] = merge(kept[k], arrivals[k][-1:], False, tied)
            else:
                kept[k], msg[k] = merge(kept[k], arrivals[k], True, tied)

    tile = kept[0][1]
    far = 4
    while far < per:
        moves = each([(w, w + far) for w in range(far)])
        fresh = (within >= far) & (within < 2 * far)
        tile = jnp.where(fresh, send(tile, moves), tile)
        far *= 2

    sums, row_specs = [], []
    narrow = BLOCK // 2
    for k in range(PAIRS):
        sums.append(kept[k][0])
        row_specs.append(pl.BlockSpec((narrow, piece), lambda i: (i, 0)))
        for source in (2, 1, 3):
            arrived = send(msg[k], each([(source, 0)]))
            sums += [arrived, arrived]
            row_specs += [
                pl.BlockSpec((narrow, piece // 2), lambda i: (i, 0)),
                pl.BlockSpec((8, piece // 2), lambda i: (ROWS // 8, 0)),
            ]

    owner = jnp.reshape(here & (within == 0), (1,)).astype(jnp.int32)
    operands = [owner, by_col, decoder, factors, tile, *chosen, *sums]
    specs = [
        smem,
        pl.BlockSpec((narrow, ROWS), lambda i: (i, 0)),
        pl.BlockSpec((narrow, width), lambda i: (i, 0)),
        pl.BlockSpec((narrow, 128), lambda i: (i, 0)),
        pl.BlockSpec((8, 128), lambda i: (0, 0)),
    ]
    specs += [whole_chunk] * COUNT
    specs += row_specs
    aliases = {}
    if grad is not None:
        aliases = {len(operands): 0}
        operands.append(grad)
        specs.append(any_spec)
    decoder_grad, penalty = pl.pallas_call(
        functools.partial(last_kernel, DW / (ROWS * latents)),
        grid=(2,),
        in_specs=specs,
        out_specs=[pl.BlockSpec((narrow, width), lambda i: (i, 0)), smem],
        out_shape=[out_type, jax.ShapeDtypeStruct((1,), jnp.float32)],
        scratch_shapes=[pltpu.VMEM((narrow, width), jnp.float32)],
        input_output_aliases=aliases,
        compiler_params=params(50),
        name="finish_rows",
    )(*operands)

    return (penalty, decoder_grad)


def solution(mesh):
    in_specs = (P(("groups", "row"), None), P("groups"))
    out_specs = (P("groups"), P(("groups", "row"), None))
    return jax.shard_map(
        on_device, mesh=mesh, in_specs=in_specs, out_specs=out_specs, check_vma=False
    )
```

```python
import functools
import math

import jax
import jax.numpy as jnp
from jax import lax
from jax.experimental import pallas as pl
from jax.experimental.pallas import tpu as pltpu
from jax.sharding import PartitionSpec as P

DW = 4096
ROWS = 256
BLOCK = 256
WIDE = 512
PAIRS = 2
COUNT = 2 * PAIRS
MIB = 1024 * 1024
NT = (((1,), (1,)), ((), ()))


def params(mib):
    return pltpu.CompilerParams(vmem_limit_bytes=mib * MIB)


def cost(flops, moved):
    return pl.CostEstimate(flops=flops, bytes_accessed=moved, transcendentals=0)


def strip_inverse(ref, rows):
    width = ref.shape[1]
    total = None
    for t in range(0, width, 128):
        v = ref[rows, t : t + 128].astype(jnp.float32)
        total = v * v if total is None else total + v * v
    return 1.0 / jnp.sqrt(jnp.sum(total, axis=1, keepdims=True) + 1e-06)


def head_kernel(flags_ref, decoder_ref, *refs):
    chunk_refs, (held, sems) = refs[:COUNT], refs[COUNT:]
    step = chunk_refs[0].shape[1]
    strip = ROWS // 4

    def fetch(j):
        rows = pl.ds(j * strip, strip)
        return pltpu.make_async_copy(decoder_ref.at[rows, :], held.at[rows, :], sems.at[j])

    for j in range(4):
        fetch(j).start()
    for j in range(4):
        fetch(j).wait()
        rows = slice(j * strip, (j + 1) * strip)
        inverse = strip_inverse(held, rows)
        for k, ref in enumerate(chunk_refs):
            for t in range(0, step, 128):
                v = held[rows, k * step + t : k * step + t + 128].astype(jnp.float32)
                ref[rows, t : t + 128] = (v * inverse).astype(jnp.bfloat16)


def units_kernel(low, count, decoder_ref, *refs):
    units_ref, inverse_ref, held, sems = refs[-4:]
    strip = 64

    def fetch(j):
        return pltpu.make_async_copy(
            decoder_ref.at[pl.ds((low + j) * BLOCK, BLOCK), :], held.at[j % 2], sems.at[j % 2]
        )

    fetch(0).start()
    for j in range(count):
        if j + 1 < count:
            fetch(j + 1).start()
        fetch(j).wait()
        block = held.at[j % 2]
        for base in range(0, BLOCK, strip):
            rows = slice(base, base + strip)
            to = slice(j * BLOCK + base, j * BLOCK + base + strip)
            inverse = strip_inverse(block, rows)
            inverse_ref[to, :] = jnp.broadcast_to(inverse, (strip, 128))
            for t in range(0, block.shape[1], 128):
                v = block[rows, t : t + 128].astype(jnp.float32)
                units_ref[to, t : t + 128] = (v * inverse).astype(jnp.bfloat16)


def pair_cosines(k, units_ref, rows, low_ref, high_ref):
    step = low_ref.shape[1]
    base = 2 * k * step
    low = lax.dot_general(
        units_ref[rows, base : base + step],
        low_ref[...],
        NT,
        preferred_element_type=jnp.float32,
    )
    high = lax.dot_general(
        units_ref[rows, base + step : base + 2 * step],
        high_ref[...],
        NT,
        preferred_element_type=jnp.float32,
    )
    return low + high


def pick_kernel(slots, count, flags_ref, *refs):
    out_refs, sems = refs[-len(slots) - 1 : -1], refs[-1]
    for n, (slot, out_ref) in enumerate(zip(slots, out_refs)):
        for c in range(count):

            @pl.when(flags_ref[slot] == c)
            def _(out_ref=out_ref, c=c, n=n):
                pltpu.make_async_copy(refs[c], out_ref, sems.at[n]).start()

    for n, out_ref in enumerate(out_refs):
        pltpu.make_async_copy(refs[0], out_ref, sems.at[n]).wait()


def partial_kernel(k, parts, low_ref, high_ref, *refs):
    out_ref = refs[-1]
    base = 0
    for units_ref in refs[:parts]:
        count = units_ref.shape[0]
        size = min(WIDE, count)

        def body(j, carry, units_ref=units_ref, size=size, base=base):
            rows = pl.ds(pl.multiple_of(j * size, size), size)
            to = pl.ds(pl.multiple_of(base + j * size, size), size)
            out_ref[to, :] = pair_cosines(k, units_ref, rows, low_ref, high_ref)
            return carry

        lax.fori_loop(0, count // size, body, 0)
        base += count


def weight_kernel(k, parts, delta_ref, low_ref, high_ref, partial_ref, *refs):
    col_ref, row_ref, factor_ref, penalty_ref = refs[-4:]
    penalty_ref[...] = jnp.zeros_like(penalty_ref)
    base = 0
    for units_ref, inverse_ref in zip(refs[:parts], refs[parts : 2 * parts]):
        count = units_ref.shape[0]
        size = min(WIDE, count)

        def body(j, carry, units_ref=units_ref, inverse_ref=inverse_ref, size=size, base=base):
            here = pl.ds(pl.multiple_of(j * size, size), size)
            first = base + j * size
            span = pl.ds(pl.multiple_of(first, size), size)
            cosines = partial_ref[span, :] + pair_cosines(k, units_ref, here, low_ref, high_ref)
            latents = lax.broadcasted_iota(jnp.int32, (size, ROWS), 0) + (delta_ref[0] + first)
            rows = lax.broadcasted_iota(jnp.int32, (size, ROWS), 1)
            inside = (latents >= 0) & (latents < ROWS)
            weight = jnp.where(latents == rows, 0.0, jnp.where(inside, 0.5, 1.0))
            products = weight * cosines
            weighted = products.astype(jnp.bfloat16)
            col_ref[span, :] = weighted
            row_ref[:, span] = products.T.astype(jnp.bfloat16)
            along = jnp.sum(weighted.astype(jnp.float32) * cosines, axis=1, keepdims=True)
            inverse = inverse_ref[here, :]
            lanes = lax.broadcasted_iota(jnp.int32, (size, 128), 1)
            factor_ref[span, :] = jnp.where(lanes < 64, inverse, along * inverse)
            squares = products * cosines
            squares = squares[:, :128] + squares[:, 128:]
            penalty_ref[...] += jnp.sum(squares.reshape(size // 8, 8, 128), axis=0)
            return carry

        lax.fori_loop(0, count // size, body, 0)
        base += count


def row_kernel(k, parts, side_ref, row_ref, penalty_ref, *refs):
    out_ref = refs[-1]
    tile = out_ref.shape[1] // 2
    first = (2 * k + side_ref[0]) * out_ref.shape[1]
    for i in range(2):
        span = pl.ds(pl.multiple_of(first + i * tile, tile), tile)
        total, base = None, 0
        for units_ref in refs[:parts]:
            count = units_ref.shape[0]
            part = jnp.dot(
                row_ref[:, base : base + count],
                units_ref[:, span],
                preferred_element_type=jnp.float32,
            )
            total = part if total is None else total + part
            base += count
        out_ref[:ROWS, i * tile : (i + 1) * tile] = total
    out_ref[ROWS:, :] = jnp.concatenate([penalty_ref[...]] * (out_ref.shape[1] // 128), axis=1)


def finish_kernel(col_ref, decoder_ref, factor_ref, *refs):
    chunks = refs[:COUNT]
    out_ref, mark_ref = refs[-2:]
    step = chunks[0].shape[1]
    scale = (2.0 * math.sqrt(DW)) * factor_ref[:, :1]
    back = scale * factor_ref[:, 64:65]
    for k in range(COUNT):
        span = slice(k * step, (k + 1) * step)
        part = jnp.dot(col_ref[...], chunks[k][...], preferred_element_type=jnp.float32)
        out_ref[:, span] = scale * part - back * decoder_ref[:, span].astype(jnp.float32)
    mark_ref[...] = jnp.zeros_like(mark_ref)


STEPS = 32000.0
CODED_ROWS = ROWS + 16
PENALTY_STEPS = float(1 << 23)


def pack(coded):
    half = coded.shape[1] // 2
    return (coded[:, :half] << 16) | (coded[:, half:] & 0xFFFF)


def unpack(words):
    both = jnp.concatenate([words >> 16, (words << 16) >> 16], axis=1)
    return both.astype(jnp.float32)


def encode(value, penalty, msg_ref):
    top = jnp.max(jnp.abs(value), axis=0, keepdims=True)
    power = jnp.ceil(jnp.log2(jnp.maximum(top, 1e-35)) * 8.0)
    ratio = value * jnp.exp2(power * -0.125)
    coded = ratio * lax.rsqrt(jnp.maximum(jnp.abs(ratio), 1e-30))
    msg_ref[:ROWS, :] = pack(jnp.round(coded * STEPS).astype(jnp.int32))
    power = pack(power.astype(jnp.int32))
    msg_ref[ROWS : ROWS + 8, :] = jnp.broadcast_to(power, (8, power.shape[1]))
    top = jnp.max(jnp.max(penalty, axis=1, keepdims=True), axis=0, keepdims=True)
    power = jnp.ceil(jnp.log2(jnp.maximum(top, 1e-35)))
    coded = jnp.round(penalty * (jnp.exp2(-power) * PENALTY_STEPS)).astype(jnp.int32)
    msg_ref[ROWS + 8 :, :128] = coded
    msg_ref[ROWS + 8 :, 128:] = jnp.broadcast_to(power.astype(jnp.int32), (8, 128))


def decode(words, powers):
    coded = unpack(words)
    scale = jnp.exp2(unpack(powers)[:1, :] * 0.125) * (1.0 / (STEPS * STEPS))
    return coded * jnp.abs(coded) * scale


def decode_at(msg_ref):
    value = decode(msg_ref[:ROWS, :], msg_ref[ROWS : ROWS + 8, :])
    power = msg_ref[ROWS + 8 :, 128:].astype(jnp.float32)
    penalty = msg_ref[ROWS + 8 :, :128].astype(jnp.float32) * (jnp.exp2(power) / PENALTY_STEPS)
    return value, penalty


def split_kernel(odd_ref, mine_ref, theirs_ref, kept_ref, penalty_ref, msg_ref):
    piece = kept_ref.shape[1]
    penalty = mine_ref[ROWS:, :128] + theirs_ref[ROWS:, :128]
    penalty_ref[...] = penalty
    low, high = slice(0, piece), slice(piece, 2 * piece)

    def divide(keep, away):
        kept_ref[...] = mine_ref[:ROWS, keep] + theirs_ref[:ROWS, keep]
        encode(mine_ref[:ROWS, away] + theirs_ref[:ROWS, away], penalty, msg_ref)

    @pl.when(odd_ref[0] == 0)
    def _():
        divide(low, high)

    @pl.when(odd_ref[0] == 1)
    def _():
        divide(high, low)


def merge_kernel(arrived, keep, kept_ref, penalty_ref, *refs):
    value, penalty = kept_ref[...], penalty_ref[...]
    for msg_ref in refs[:arrived]:
        more, more_penalty = decode_at(msg_ref)
        value, penalty = value + more, penalty + more_penalty
    if keep:
        refs[-3][...] = value
        refs[-2][...] = penalty
    encode(value, penalty, refs[-1])


def last_kernel(share, owner_ref, col_ref, decoder_ref, factor_ref, tile_ref, *refs):
    chunks, sums = refs[:COUNT], refs[COUNT : COUNT + 7 * PAIRS]
    out_ref, penalty_ref, column = refs[-3:]
    penalty_ref[0] = jnp.sum(tile_ref[...]) * share
    step = chunks[0].shape[1]
    piece = step // 2
    owner = owner_ref[0] == 1
    total = jnp.zeros((col_ref.shape[0], 128), jnp.float32)
    for k in range(COUNT):
        span = slice(k * step, (k + 1) * step)
        part = jnp.dot(col_ref[...], chunks[k][...], preferred_element_type=jnp.float32)
        own, *coded = sums[7 * (k // 2) : 7 * (k // 2) + 7]
        pieces = [own[...]] + [
            decode(coded[2 * p][...], coded[2 * p + 1][...]) for p in range(3)
        ]
        row_sum = jnp.concatenate(pieces[2 * (k % 2) : 2 * (k % 2) + 2], axis=1)
        part = part + jnp.where(owner, row_sum, 0.0)
        column[:, span] = part
        along = part * decoder_ref[:, span].astype(jnp.float32)
        for t in range(0, step, 128):
            total = total + along[:, t : t + 128]
    inverse = factor_ref[:, :1]
    scale = (2.0 * math.sqrt(DW)) * inverse
    back = scale * (jnp.sum(total, axis=1, keepdims=True) * inverse * inverse)
    for k in range(COUNT):
        span = slice(k * step, (k + 1) * step)
        out_ref[:, span] = scale * column[:, span] - back * decoder_ref[:, span].astype(
            jnp.float32
        )


def on_device(decoder, quarter):
    shard, width = decoder.shape
    devices = lax.axis_size("row")
    index = lax.axis_index("row")
    per = devices // 4
    latents = shard * devices
    blocks = shard // BLOCK
    step = width // COUNT
    chosen_quarter = quarter[0]
    start = chosen_quarter * (latents // 4)
    place = index // per
    within = index % per
    here = place == chosen_quarter
    even_chip = (within // 2) % 2 == 0
    smem = pl.BlockSpec(memory_space=pltpu.SMEM)

    def send(value, pairs):
        return lax.ppermute(value, "row", pairs)

    def each(moves):
        return [(z * per + a, z * per + b) for z in range(4) for a, b in moves]

    near = jnp.where(place == 1, chosen_quarter == 0, chosen_quarter == 3)
    middle = (place == 1) | (place == 2)
    reached = jnp.where(here, 0, jnp.where(middle, jnp.where(near, 1, 2), 3))
    core_index = within % 2
    fresh = [(within >= 4 << n) & (within < 8 << n) for n in range((per // 4).bit_length() - 1)]
    TAKES, WAITS, REACHED, LOW, HIGH, FRESH = range(6)
    flags = jnp.stack(
        [
            jnp.where(within == 2, 1, 0),
            jnp.where(here, 0, 1),
            reached,
            jnp.where(even_chip, 0, 2) + core_index,
            jnp.where(even_chip, 2, 0) + core_index,
        ]
        + [jnp.where(value, 1, 0) for value in fresh]
    ).astype(jnp.int32)

    pinned = pl.BlockSpec(memory_space=pl.ANY)
    any_spec = pinned
    vmem = pl.BlockSpec(memory_space=pltpu.VMEM)
    chunk_type = jax.ShapeDtypeStruct((ROWS, step), jnp.bfloat16)
    own = pl.pallas_call(
        head_kernel,
        in_specs=[smem, pinned],
        out_specs=[vmem] * COUNT,
        out_shape=[chunk_type] * COUNT,
        scratch_shapes=[
            pltpu.VMEM((ROWS, width), jnp.bfloat16),
            pltpu.SemaphoreType.DMA((4,)),
        ],
        compiler_params=params(50),
        cost_estimate=cost(4 * ROWS * width, 4 * ROWS * width),
        name="head_units",
    )(flags, decoder)

    across_x = each([(0, 2), (2, 0), (1, 3), (3, 1)])
    across_core = each([(0, 1), (1, 0), (2, 3), (3, 2)])
    piece = step // 2

    def hop(level, lanes):
        moves = (((0, 1), (3, 2)), ((1, 2), (2, 1)), ((2, 3), (1, 0)))[level]
        return [(a * per + w, b * per + w) for a, b in moves for w in lanes]

    def pick(slots, candidates, ties=()):
        return pl.pallas_call(
            functools.partial(pick_kernel, slots, len(candidates)),
            in_specs=[smem] + [any_spec] * (len(candidates) + len(ties)),
            out_specs=[vmem] * len(slots),
            out_shape=[chunk_type] * len(slots),
            scratch_shapes=[pltpu.SemaphoreType.DMA((len(slots),))],
            compiler_params=params(12),
            cost_estimate=cost(ROWS * step, 4 * ROWS * step),
            name="pick",
        )(flags, *candidates, *ties)

    unit_bounds = [blocks * p // 4 for p in range(5)]
    units, inverses = [], []

    def make_units(part, tie):
        low, high = unit_bounds[part], unit_bounds[part + 1]
        if high == low:
            return []
        rows = (high - low) * BLOCK
        made = pl.pallas_call(
            functools.partial(units_kernel, low, high - low),
            in_specs=[pinned, any_spec],
            out_specs=[vmem, vmem],
            out_shape=[
                jax.ShapeDtypeStruct((rows, width), jnp.bfloat16),
                jax.ShapeDtypeStruct((rows, 128), jnp.float32),
            ],
            scratch_shapes=[
                pltpu.VMEM((2, BLOCK, width), jnp.bfloat16),
                pltpu.SemaphoreType.DMA((2,)),
            ],
            compiler_params=params((46, 44, 40, 36)[part]),
            cost_estimate=cost(4 * rows * width, 4 * rows * width),
            name="units",
        )(decoder, tie)
        units.append(made[0])
        inverses.append(made[1])
        return [made[1]]

    mine, first, second, third, held = ([None] * PAIRS for _ in range(5))
    across = [send(own[2 * k + 1], each([(0, 2)])) for k in range(PAIRS)]
    done = make_units(0, own[0])
    for k in range(PAIRS):
        [mine[k]] = pick([TAKES], [own[2 * k], across[k]], () if k else done)
        first[k] = send(mine[k], hop(0, (0, 2)))
    done = make_units(1, mine[PAIRS - 1])
    for k in range(PAIRS):
        [going] = pick([WAITS], [mine[k], first[k]], () if k else done)
        second[k] = send(going, hop(1, (0, 2)))
    for k in range(PAIRS):
        [going] = pick([WAITS], [mine[k], second[k]], done if k else ())
        third[k] = send(going, hop(2, (0, 2)))
        if k == 0:
            done = make_units(2, going)
    for k in range(PAIRS):
        [held[k]] = pick([REACHED], [mine[k], first[k], second[k], third[k]])
    done = make_units(3, held[PAIRS - 1])
    chosen = []
    for k in range(PAIRS):
        other = send(held[k], each([(0, 2), (2, 0)]))
        core_held = send(held[k], each([(0, 1), (2, 3)]))
        core_other = send(other, each([(0, 1), (2, 3)]))
        pair = pick(
            [LOW, HIGH], [held[k], core_held, other, core_other], () if k else done
        )
        for n in range(len(fresh)):
            moves = each([(w, w + (4 << n)) for w in range(4 << n)])
            pair = [pick([FRESH + n], [value, send(value, moves)])[0] for value in pair]
        chosen += pair

    delta = jnp.reshape(index * shard - start, (1,)).astype(jnp.int32)
    whole_chunk = pl.BlockSpec((ROWS, step), lambda i: (0, 0))
    half_flops = ROWS * shard * width
    parts = len(units)
    partial = pl.pallas_call(
        functools.partial(partial_kernel, 0, parts),
        in_specs=[vmem] * (2 + parts),
        out_specs=vmem,
        out_shape=jax.ShapeDtypeStruct((shard, ROWS), jnp.float32),
        compiler_params=params(16),
        cost_estimate=cost(half_flops, shard * width),
        name="part_cosines",
    )(chosen[0], chosen[1], *units)
    by_col, by_row, factors, local_penalty = pl.pallas_call(
        functools.partial(weight_kernel, 1, parts),
        in_specs=[smem] + [vmem] * (3 + 2 * parts),
        out_specs=[vmem] * 4,
        out_shape=[
            jax.ShapeDtypeStruct((shard, ROWS), jnp.bfloat16),
            jax.ShapeDtypeStruct((ROWS, shard), jnp.bfloat16),
            jax.ShapeDtypeStruct((shard, 128), jnp.float32),
            jax.ShapeDtypeStruct((8, 128), jnp.float32),
        ],
        compiler_params=params(16),
        cost_estimate=cost(half_flops, shard * width),
        name="weights",
    )(delta, chosen[2], chosen[3], partial, *units, *inverses)

    core_side = within % 2
    plane_x = jnp.reshape((within // 2) % 2, (1,)).astype(jnp.int32)
    tall = ROWS + 8
    coded_type = jax.ShapeDtypeStruct((CODED_ROWS, piece // 2), jnp.int32)
    piece_type = jax.ShapeDtypeStruct((ROWS, piece), jnp.float32)
    tile_type = jax.ShapeDtypeStruct((8, 128), jnp.float32)
    merge_cost = cost(20 * ROWS * piece, 12 * ROWS * piece)

    def row_part(k, side):
        return pl.pallas_call(
            functools.partial(row_kernel, k, parts),
            in_specs=[smem] + [vmem] * (2 + parts),
            out_specs=vmem,
            out_shape=jax.ShapeDtypeStruct((tall, step), jnp.float32),
            compiler_params=params(24),
            cost_estimate=cost(half_flops // 2, shard * width // 2),
            name="row_part",
        )(jnp.reshape(side, (1,)).astype(jnp.int32), by_row, local_penalty, *units)

    def merge(kept, arrived, keep, ties=()):
        tiles = [piece_type, tile_type, coded_type] if keep else [coded_type]
        result = pl.pallas_call(
            functools.partial(merge_kernel, len(arrived), keep),
            in_specs=[vmem] * (2 + len(arrived)) + [any_spec] * len(ties),
            out_specs=[vmem] * len(tiles),
            out_shape=tiles,
            compiler_params=params(24),
            cost_estimate=merge_cost,
            name="merge",
        )(*kept, *arrived, *ties)
        return (tuple(result[:2]), result[2]) if keep else result[0]

    kept, msg = [None] * PAIRS, [None] * PAIRS
    for k in range(PAIRS):
        away, near = row_part(k, 1 - core_side), row_part(k, core_side)
        far = per // 2
        while far >= 4:
            moves = each([(w + far, w) for w in range(far)])
            away, near = away + send(away, moves), near + send(near, moves)
            far //= 2
        rest, tile, msg[k] = pl.pallas_call(
            split_kernel,
            in_specs=[smem, vmem, vmem],
            out_specs=[vmem, vmem, vmem],
            out_shape=[piece_type, tile_type, coded_type],
            compiler_params=params(24),
            cost_estimate=merge_cost,
            name="split",
        )(plane_x, near, send(away, across_core))
        kept[k] = (rest, tile)

    out_type = jax.ShapeDtypeStruct((shard, width), jnp.float32)
    mark_type = jax.ShapeDtypeStruct((8, 128), jnp.float32)
    mark_spec = pl.BlockSpec((8, 128), lambda i: (0, 0))
    bounds = [1 + (blocks - 1) * p // 7 for p in (0, 2, 4, 5, 5, 7)]
    grad = None

    def finish(part, tie):
        nonlocal grad
        low, high = bounds[part], bounds[part + 1]
        if high == low:
            return []
        operands = [by_col, decoder, factors, *chosen]
        specs = [
            pl.BlockSpec((BLOCK, ROWS), lambda i: (i + low, 0)),
            pl.BlockSpec((BLOCK, width), lambda i: (i + low, 0)),
            pl.BlockSpec((BLOCK, 128), lambda i: (i + low, 0)),
        ] + [whole_chunk] * COUNT
        operands.append(tie)
        specs.append(any_spec)
        aliases = {}
        if grad is not None:
            aliases = {len(operands): 0}
            operands.append(grad)
            specs.append(any_spec)
        rows = (high - low) * BLOCK
        grad, mark = pl.pallas_call(
            finish_kernel,
            grid=(high - low,),
            in_specs=specs,
            out_specs=[pl.BlockSpec((BLOCK, width), lambda i: (i + low, 0)), mark_spec],
            out_shape=[out_type, mark_type],
            input_output_aliases=aliases,
            compiler_params=params(50),
            cost_estimate=cost(2 * ROWS * rows * width, 6 * rows * width),
            name="finish",
        )(*operands)
        return [mark]

    lanes = range(4)
    across = [send(msg[k], across_x) for k in range(PAIRS)]
    ties = finish(0, msg[PAIRS - 1])
    for k in range(PAIRS):
        kept[k], msg[k] = merge(kept[k], [across[k]], True, () if k else ties)
    arrivals = [[] for _ in range(PAIRS)]
    for level in range(3):
        for k in range(PAIRS):
            arrivals[k].append(send(msg[k], hop(level, lanes)))
        ties = finish(level + 1, msg[PAIRS - 1])
        for k in range(PAIRS):
            tied = () if k else ties
            if level < 2:
                msg[k] = merge(kept[k], arrivals[k][-1:], False, tied)
            else:
                kept[k], msg[k] = merge(kept[k], arrivals[k], True, tied)

    tile = kept[0][1]
    far = 4
    while far < per:
        moves = each([(w, w + far) for w in range(far)])
        fresh = (within >= far) & (within < 2 * far)
        tile = jnp.where(fresh, send(tile, moves), tile)
        far *= 2

    finish(4, msg[PAIRS - 1])
    sums, row_specs = [], []
    narrow = BLOCK // 2
    for k in range(PAIRS):
        sums.append(kept[k][0])
        row_specs.append(pl.BlockSpec((narrow, piece), lambda i: (i, 0)))
        arrivals = [send(msg[k], each([(source, 0)])) for source in (2, 3, 1)]
        for arrived in (arrivals[0], arrivals[2], arrivals[1]):
            sums += [arrived, arrived]
            row_specs += [
                pl.BlockSpec((narrow, piece // 2), lambda i: (i, 0)),
                pl.BlockSpec((8, piece // 2), lambda i: (ROWS // 8, 0)),
            ]

    owner = jnp.reshape(here & (within == 0), (1,)).astype(jnp.int32)
    operands = [owner, by_col, decoder, factors, tile, *chosen, *sums]
    specs = [
        smem,
        pl.BlockSpec((narrow, ROWS), lambda i: (i, 0)),
        pl.BlockSpec((narrow, width), lambda i: (i, 0)),
        pl.BlockSpec((narrow, 128), lambda i: (i, 0)),
        pl.BlockSpec((8, 128), lambda i: (0, 0)),
    ]
    specs += [whole_chunk] * COUNT
    specs += row_specs
    aliases = {}
    if grad is not None:
        aliases = {len(operands): 0}
        operands.append(grad)
        specs.append(any_spec)
    decoder_grad, penalty = pl.pallas_call(
        functools.partial(last_kernel, DW / (ROWS * latents)),
        grid=(2,),
        in_specs=specs,
        out_specs=[pl.BlockSpec((narrow, width), lambda i: (i, 0)), smem],
        out_shape=[out_type, jax.ShapeDtypeStruct((1,), jnp.float32)],
        scratch_shapes=[pltpu.VMEM((narrow, width), jnp.float32)],
        input_output_aliases=aliases,
        compiler_params=params(50),
        name="finish_rows",
    )(*operands)

    return (penalty, decoder_grad)


def solution(mesh):
    in_specs = (P(("groups", "row"), None), P("groups"))
    out_specs = (P("groups"), P(("groups", "row"), None))
    return jax.shard_map(
        on_device, mesh=mesh, in_specs=in_specs, out_specs=out_specs, check_vma=False
    )
```

```python
import functools
import math

import jax
import jax.numpy as jnp
from jax import lax
from jax.experimental import pallas as pl
from jax.experimental.pallas import tpu as pltpu
from jax.sharding import PartitionSpec as P

DW = 4096
ROWS = 256
BLOCK = 256
WIDE = 512
PAIRS = 2
COUNT = 2 * PAIRS
MIB = 1024 * 1024
NT = (((1,), (1,)), ((), ()))


def params(mib):
    return pltpu.CompilerParams(vmem_limit_bytes=mib * MIB)


def cost(flops, moved):
    return pl.CostEstimate(flops=flops, bytes_accessed=moved, transcendentals=0)


def strip_inverse(ref, rows):
    width = ref.shape[1]
    total = None
    for t in range(0, width, 128):
        v = ref[rows, t : t + 128].astype(jnp.float32)
        total = v * v if total is None else total + v * v
    return 1.0 / jnp.sqrt(jnp.sum(total, axis=1, keepdims=True) + 1e-06)


def head_kernel(flags_ref, decoder_ref, *refs):
    chunk_refs, (held, sems) = refs[:COUNT], refs[COUNT:]
    step = chunk_refs[0].shape[1]
    strip = ROWS // 4

    def fetch(j):
        rows = pl.ds(j * strip, strip)
        return pltpu.make_async_copy(decoder_ref.at[rows, :], held.at[rows, :], sems.at[j])

    for j in range(4):
        fetch(j).start()
    for j in range(4):
        fetch(j).wait()
        rows = slice(j * strip, (j + 1) * strip)
        inverse = strip_inverse(held, rows)
        for k, ref in enumerate(chunk_refs):
            for t in range(0, step, 128):
                v = held[rows, k * step + t : k * step + t + 128].astype(jnp.float32)
                ref[rows, t : t + 128] = (v * inverse).astype(jnp.bfloat16)


def units_kernel(low, count, decoder_ref, *refs):
    units_ref, inverse_ref, held, sems = refs[-4:]
    strip = 64

    def fetch(j):
        return pltpu.make_async_copy(
            decoder_ref.at[pl.ds((low + j) * BLOCK, BLOCK), :], held.at[j % 2], sems.at[j % 2]
        )

    fetch(0).start()
    for j in range(count):
        if j + 1 < count:
            fetch(j + 1).start()
        fetch(j).wait()
        block = held.at[j % 2]
        for base in range(0, BLOCK, strip):
            rows = slice(base, base + strip)
            to = slice(j * BLOCK + base, j * BLOCK + base + strip)
            inverse = strip_inverse(block, rows)
            inverse_ref[to, :] = jnp.broadcast_to(inverse, (strip, 128))
            for t in range(0, block.shape[1], 128):
                v = block[rows, t : t + 128].astype(jnp.float32)
                units_ref[to, t : t + 128] = (v * inverse).astype(jnp.bfloat16)


def pair_cosines(k, units_ref, rows, low_ref, high_ref):
    step = low_ref.shape[1]
    base = 2 * k * step
    low = lax.dot_general(
        units_ref[rows, base : base + step],
        low_ref[...],
        NT,
        preferred_element_type=jnp.float32,
    )
    high = lax.dot_general(
        units_ref[rows, base + step : base + 2 * step],
        high_ref[...],
        NT,
        preferred_element_type=jnp.float32,
    )
    return low + high


def pick_kernel(slots, count, flags_ref, *refs):
    out_refs, sems = refs[-len(slots) - 1 : -1], refs[-1]
    for n, (slot, out_ref) in enumerate(zip(slots, out_refs)):
        for c in range(count):

            @pl.when(flags_ref[slot] == c)
            def _(out_ref=out_ref, c=c, n=n):
                pltpu.make_async_copy(refs[c], out_ref, sems.at[n]).start()

    for n, out_ref in enumerate(out_refs):
        pltpu.make_async_copy(refs[0], out_ref, sems.at[n]).wait()


def partial_kernel(k, parts, low_ref, high_ref, *refs):
    out_ref = refs[-1]
    base = 0
    for units_ref in refs[:parts]:
        count = units_ref.shape[0]
        size = min(WIDE, count)

        def body(j, carry, units_ref=units_ref, size=size, base=base):
            rows = pl.ds(pl.multiple_of(j * size, size), size)
            to = pl.ds(pl.multiple_of(base + j * size, size), size)
            out_ref[to, :] = pair_cosines(k, units_ref, rows, low_ref, high_ref)
            return carry

        lax.fori_loop(0, count // size, body, 0)
        base += count


def weight_kernel(k, parts, delta_ref, low_ref, high_ref, partial_ref, *refs):
    col_ref, row_ref, factor_ref, penalty_ref = refs[-4:]
    penalty_ref[...] = jnp.zeros_like(penalty_ref)
    base = 0
    for units_ref, inverse_ref in zip(refs[:parts], refs[parts : 2 * parts]):
        count = units_ref.shape[0]
        size = min(WIDE, count)

        def body(j, carry, units_ref=units_ref, inverse_ref=inverse_ref, size=size, base=base):
            here = pl.ds(pl.multiple_of(j * size, size), size)
            first = base + j * size
            span = pl.ds(pl.multiple_of(first, size), size)
            cosines = partial_ref[span, :] + pair_cosines(k, units_ref, here, low_ref, high_ref)
            latents = lax.broadcasted_iota(jnp.int32, (size, ROWS), 0) + (delta_ref[0] + first)
            rows = lax.broadcasted_iota(jnp.int32, (size, ROWS), 1)
            inside = (latents >= 0) & (latents < ROWS)
            weight = jnp.where(latents == rows, 0.0, jnp.where(inside, 0.5, 1.0))
            products = weight * cosines
            weighted = products.astype(jnp.bfloat16)
            col_ref[span, :] = weighted
            row_ref[:, span] = products.T.astype(jnp.bfloat16)
            along = jnp.sum(weighted.astype(jnp.float32) * cosines, axis=1, keepdims=True)
            inverse = inverse_ref[here, :]
            lanes = lax.broadcasted_iota(jnp.int32, (size, 128), 1)
            factor_ref[span, :] = jnp.where(lanes < 64, inverse, along * inverse)
            squares = products * cosines
            squares = squares[:, :128] + squares[:, 128:]
            penalty_ref[...] += jnp.sum(squares.reshape(size // 8, 8, 128), axis=0)
            return carry

        lax.fori_loop(0, count // size, body, 0)
        base += count


def row_kernel(k, parts, side_ref, row_ref, penalty_ref, *refs):
    out_ref = refs[-1]
    tile = out_ref.shape[1] // 2
    first = (2 * k + side_ref[0]) * out_ref.shape[1]
    for i in range(2):
        span = pl.ds(pl.multiple_of(first + i * tile, tile), tile)
        total, base = None, 0
        for units_ref in refs[:parts]:
            count = units_ref.shape[0]
            part = jnp.dot(
                row_ref[:, base : base + count],
                units_ref[:, span],
                preferred_element_type=jnp.float32,
            )
            total = part if total is None else total + part
            base += count
        out_ref[:ROWS, i * tile : (i + 1) * tile] = total
    out_ref[ROWS:, :] = jnp.concatenate([penalty_ref[...]] * (out_ref.shape[1] // 128), axis=1)


def finish_kernel(col_ref, decoder_ref, factor_ref, *refs):
    chunks = refs[:COUNT]
    out_ref, mark_ref = refs[-2:]
    step = chunks[0].shape[1]
    scale = (2.0 * math.sqrt(DW)) * factor_ref[:, :1]
    back = scale * factor_ref[:, 64:65]
    for k in range(COUNT):
        span = slice(k * step, (k + 1) * step)
        part = jnp.dot(col_ref[...], chunks[k][...], preferred_element_type=jnp.float32)
        out_ref[:, span] = scale * part - back * decoder_ref[:, span].astype(jnp.float32)
    mark_ref[...] = jnp.zeros_like(mark_ref)


STEPS = 32000.0
CODED_ROWS = ROWS + 16
PENALTY_STEPS = float(1 << 23)


def pack(coded):
    half = coded.shape[1] // 2
    return (coded[:, :half] << 16) | (coded[:, half:] & 0xFFFF)


def unpack(words):
    both = jnp.concatenate([words >> 16, (words << 16) >> 16], axis=1)
    return both.astype(jnp.float32)


def encode(value, penalty, msg_ref):
    top = jnp.max(jnp.abs(value), axis=0, keepdims=True)
    power = jnp.ceil(jnp.log2(jnp.maximum(top, 1e-35)) * 8.0)
    ratio = value * jnp.exp2(power * -0.125)
    coded = ratio * lax.rsqrt(jnp.maximum(jnp.abs(ratio), 1e-30))
    msg_ref[:ROWS, :] = pack(jnp.round(coded * STEPS).astype(jnp.int32))
    power = pack(power.astype(jnp.int32))
    msg_ref[ROWS : ROWS + 8, :] = jnp.broadcast_to(power, (8, power.shape[1]))
    top = jnp.max(jnp.max(penalty, axis=1, keepdims=True), axis=0, keepdims=True)
    power = jnp.ceil(jnp.log2(jnp.maximum(top, 1e-35)))
    coded = jnp.round(penalty * (jnp.exp2(-power) * PENALTY_STEPS)).astype(jnp.int32)
    msg_ref[ROWS + 8 :, :128] = coded
    msg_ref[ROWS + 8 :, 128:] = jnp.broadcast_to(power.astype(jnp.int32), (8, 128))


def decode(words, powers):
    coded = unpack(words)
    scale = jnp.exp2(unpack(powers)[:1, :] * 0.125) * (1.0 / (STEPS * STEPS))
    return coded * jnp.abs(coded) * scale


def decode_at(msg_ref):
    value = decode(msg_ref[:ROWS, :], msg_ref[ROWS : ROWS + 8, :])
    power = msg_ref[ROWS + 8 :, 128:].astype(jnp.float32)
    penalty = msg_ref[ROWS + 8 :, :128].astype(jnp.float32) * (jnp.exp2(power) / PENALTY_STEPS)
    return value, penalty


def split_kernel(odd_ref, mine_ref, theirs_ref, kept_ref, penalty_ref, msg_ref):
    piece = kept_ref.shape[1]
    penalty = mine_ref[ROWS:, :128] + theirs_ref[ROWS:, :128]
    penalty_ref[...] = penalty
    low, high = slice(0, piece), slice(piece, 2 * piece)

    def divide(keep, away):
        kept_ref[...] = mine_ref[:ROWS, keep] + theirs_ref[:ROWS, keep]
        encode(mine_ref[:ROWS, away] + theirs_ref[:ROWS, away], penalty, msg_ref)

    @pl.when(odd_ref[0] == 0)
    def _():
        divide(low, high)

    @pl.when(odd_ref[0] == 1)
    def _():
        divide(high, low)


def merge_kernel(arrived, keep, kept_ref, penalty_ref, *refs):
    value, penalty = kept_ref[...], penalty_ref[...]
    for msg_ref in refs[:arrived]:
        more, more_penalty = decode_at(msg_ref)
        value, penalty = value + more, penalty + more_penalty
    if keep:
        refs[-3][...] = value
        refs[-2][...] = penalty
    encode(value, penalty, refs[-1])


def last_kernel(share, owner_ref, col_ref, decoder_ref, factor_ref, tile_ref, *refs):
    chunks, sums = refs[:COUNT], refs[COUNT : COUNT + 7 * PAIRS]
    out_ref, penalty_ref, column = refs[-3:]
    penalty_ref[0] = jnp.sum(tile_ref[...]) * share
    step = chunks[0].shape[1]
    piece = step // 2
    owner = owner_ref[0] == 1
    total = jnp.zeros((col_ref.shape[0], 128), jnp.float32)
    for k in range(COUNT):
        span = slice(k * step, (k + 1) * step)
        part = jnp.dot(col_ref[...], chunks[k][...], preferred_element_type=jnp.float32)
        own, *coded = sums[7 * (k // 2) : 7 * (k // 2) + 7]
        pieces = [own[...]] + [
            decode(coded[2 * p][...], coded[2 * p + 1][...]) for p in range(3)
        ]
        row_sum = jnp.concatenate(pieces[2 * (k % 2) : 2 * (k % 2) + 2], axis=1)
        part = part + jnp.where(owner, row_sum, 0.0)
        column[:, span] = part
        along = part * decoder_ref[:, span].astype(jnp.float32)
        for t in range(0, step, 128):
            total = total + along[:, t : t + 128]
    inverse = factor_ref[:, :1]
    scale = (2.0 * math.sqrt(DW)) * inverse
    back = scale * (jnp.sum(total, axis=1, keepdims=True) * inverse * inverse)
    for k in range(COUNT):
        span = slice(k * step, (k + 1) * step)
        out_ref[:, span] = scale * column[:, span] - back * decoder_ref[:, span].astype(
            jnp.float32
        )


def on_device(decoder, quarter):
    shard, width = decoder.shape
    devices = lax.axis_size("row")
    index = lax.axis_index("row")
    per = devices // 4
    latents = shard * devices
    blocks = shard // BLOCK
    step = width // COUNT
    chosen_quarter = quarter[0]
    start = chosen_quarter * (latents // 4)
    place = index // per
    within = index % per
    here = place == chosen_quarter
    even_chip = (within // 2) % 2 == 0
    smem = pl.BlockSpec(memory_space=pltpu.SMEM)

    def send(value, pairs):
        return lax.ppermute(value, "row", pairs)

    def each(moves):
        return [(z * per + a, z * per + b) for z in range(4) for a, b in moves]

    near = jnp.where(place == 1, chosen_quarter == 0, chosen_quarter == 3)
    middle = (place == 1) | (place == 2)
    reached = jnp.where(here, 0, jnp.where(middle, jnp.where(near, 1, 2), 3))
    core_index = within % 2
    fresh = [(within >= 4 << n) & (within < 8 << n) for n in range((per // 4).bit_length() - 1)]
    TAKES, WAITS, REACHED, LOW, HIGH, FRESH = range(6)
    flags = jnp.stack(
        [
            jnp.where(within == 2, 1, 0),
            jnp.where(here, 0, 1),
            reached,
            jnp.where(even_chip, 0, 2) + core_index,
            jnp.where(even_chip, 2, 0) + core_index,
        ]
        + [jnp.where(value, 1, 0) for value in fresh]
    ).astype(jnp.int32)

    pinned = pl.BlockSpec(memory_space=pl.ANY)
    any_spec = pinned
    vmem = pl.BlockSpec(memory_space=pltpu.VMEM)
    chunk_type = jax.ShapeDtypeStruct((ROWS, step), jnp.bfloat16)
    own = pl.pallas_call(
        head_kernel,
        in_specs=[smem, pinned],
        out_specs=[vmem] * COUNT,
        out_shape=[chunk_type] * COUNT,
        scratch_shapes=[
            pltpu.VMEM((ROWS, width), jnp.bfloat16),
            pltpu.SemaphoreType.DMA((4,)),
        ],
        compiler_params=params(44),
        cost_estimate=cost(4 * ROWS * width, 4 * ROWS * width),
        name="head_units",
    )(flags, decoder)

    across_x = each([(0, 2), (2, 0), (1, 3), (3, 1)])
    across_core = each([(0, 1), (1, 0), (2, 3), (3, 2)])
    piece = step // 2

    def hop(level, lanes):
        moves = (((0, 1), (3, 2)), ((1, 2), (2, 1)), ((2, 3), (1, 0)))[level]
        return [(a * per + w, b * per + w) for a, b in moves for w in lanes]

    def pick(slots, candidates, ties=()):
        return pl.pallas_call(
            functools.partial(pick_kernel, slots, len(candidates)),
            in_specs=[smem] + [any_spec] * (len(candidates) + len(ties)),
            out_specs=[vmem] * len(slots),
            out_shape=[chunk_type] * len(slots),
            scratch_shapes=[pltpu.SemaphoreType.DMA((len(slots),))],
            compiler_params=params(12),
            cost_estimate=cost(ROWS * step, 4 * ROWS * step),
            name="pick",
        )(flags, *candidates, *ties)

    unit_bounds = [blocks * p // 4 for p in range(5)]
    units, inverses = [], []

    def make_units(part, tie):
        low, high = unit_bounds[part], unit_bounds[part + 1]
        if high == low:
            return []
        rows = (high - low) * BLOCK
        made = pl.pallas_call(
            functools.partial(units_kernel, low, high - low),
            in_specs=[pinned, any_spec],
            out_specs=[vmem, vmem],
            out_shape=[
                jax.ShapeDtypeStruct((rows, width), jnp.bfloat16),
                jax.ShapeDtypeStruct((rows, 128), jnp.float32),
            ],
            scratch_shapes=[
                pltpu.VMEM((2, BLOCK, width), jnp.bfloat16),
                pltpu.SemaphoreType.DMA((2,)),
            ],
            compiler_params=params((43, 40, 37, 34)[part]),
            cost_estimate=cost(4 * rows * width, 4 * rows * width),
            name="units",
        )(decoder, tie)
        units.append(made[0])
        inverses.append(made[1])
        return [made[1]]

    mine, first, second, third, held = ([None] * PAIRS for _ in range(5))
    across = [send(own[2 * k + 1], each([(0, 2)])) for k in range(PAIRS)]
    done = make_units(0, own[0])
    for k in range(PAIRS):
        [mine[k]] = pick([TAKES], [own[2 * k], across[k]], () if k else done)
        first[k] = send(mine[k], hop(0, (0, 2)))
    done = make_units(1, mine[PAIRS - 1])
    for k in range(PAIRS):
        [going] = pick([WAITS], [mine[k], first[k]], () if k else done)
        second[k] = send(going, hop(1, (0, 2)))
    for k in range(PAIRS):
        [going] = pick([WAITS], [mine[k], second[k]], done if k else ())
        third[k] = send(going, hop(2, (0, 2)))
        if k == 0:
            done = make_units(2, going)
    for k in range(PAIRS):
        [held[k]] = pick([REACHED], [mine[k], first[k], second[k], third[k]])
    done = make_units(3, held[PAIRS - 1])
    chosen = []
    for k in range(PAIRS):
        other = send(held[k], each([(0, 2), (2, 0)]))
        core_held = send(held[k], each([(0, 1), (2, 3)]))
        core_other = send(other, each([(0, 1), (2, 3)]))
        pair = pick(
            [LOW, HIGH], [held[k], core_held, other, core_other], () if k else done
        )
        for n in range(len(fresh)):
            moves = each([(w, w + (4 << n)) for w in range(4 << n)])
            pair = [pick([FRESH + n], [value, send(value, moves)])[0] for value in pair]
        chosen += pair

    delta = jnp.reshape(index * shard - start, (1,)).astype(jnp.int32)
    whole_chunk = pl.BlockSpec((ROWS, step), lambda i: (0, 0))
    half_flops = ROWS * shard * width
    parts = len(units)
    partial = pl.pallas_call(
        functools.partial(partial_kernel, 0, parts),
        in_specs=[vmem] * (2 + parts),
        out_specs=vmem,
        out_shape=jax.ShapeDtypeStruct((shard, ROWS), jnp.float32),
        compiler_params=params(16),
        cost_estimate=cost(half_flops, shard * width),
        name="part_cosines",
    )(chosen[0], chosen[1], *units)
    by_col, by_row, factors, local_penalty = pl.pallas_call(
        functools.partial(weight_kernel, 1, parts),
        in_specs=[smem] + [vmem] * (3 + 2 * parts),
        out_specs=[vmem] * 4,
        out_shape=[
            jax.ShapeDtypeStruct((shard, ROWS), jnp.bfloat16),
            jax.ShapeDtypeStruct((ROWS, shard), jnp.bfloat16),
            jax.ShapeDtypeStruct((shard, 128), jnp.float32),
            jax.ShapeDtypeStruct((8, 128), jnp.float32),
        ],
        compiler_params=params(16),
        cost_estimate=cost(half_flops, shard * width),
        name="weights",
    )(delta, chosen[2], chosen[3], partial, *units, *inverses)

    core_side = within % 2
    plane_x = jnp.reshape((within // 2) % 2, (1,)).astype(jnp.int32)
    tall = ROWS + 8
    coded_type = jax.ShapeDtypeStruct((CODED_ROWS, piece // 2), jnp.int32)
    piece_type = jax.ShapeDtypeStruct((ROWS, piece), jnp.float32)
    tile_type = jax.ShapeDtypeStruct((8, 128), jnp.float32)
    merge_cost = cost(20 * ROWS * piece, 12 * ROWS * piece)

    def row_part(k, side):
        return pl.pallas_call(
            functools.partial(row_kernel, k, parts),
            in_specs=[smem] + [vmem] * (2 + parts),
            out_specs=vmem,
            out_shape=jax.ShapeDtypeStruct((tall, step), jnp.float32),
            compiler_params=params(24),
            cost_estimate=cost(half_flops // 2, shard * width // 2),
            name="row_part",
        )(jnp.reshape(side, (1,)).astype(jnp.int32), by_row, local_penalty, *units)

    def merge(kept, arrived, keep, ties=()):
        tiles = [piece_type, tile_type, coded_type] if keep else [coded_type]
        result = pl.pallas_call(
            functools.partial(merge_kernel, len(arrived), keep),
            in_specs=[vmem] * (2 + len(arrived)) + [any_spec] * len(ties),
            out_specs=[vmem] * len(tiles),
            out_shape=tiles,
            compiler_params=params(24),
            cost_estimate=merge_cost,
            name="merge",
        )(*kept, *arrived, *ties)
        return (tuple(result[:2]), result[2]) if keep else result[0]

    kept, msg = [None] * PAIRS, [None] * PAIRS
    for k in range(PAIRS):
        away, near = row_part(k, 1 - core_side), row_part(k, core_side)
        far = per // 2
        while far >= 4:
            moves = each([(w + far, w) for w in range(far)])
            away, near = away + send(away, moves), near + send(near, moves)
            far //= 2
        rest, tile, msg[k] = pl.pallas_call(
            split_kernel,
            in_specs=[smem, vmem, vmem],
            out_specs=[vmem, vmem, vmem],
            out_shape=[piece_type, tile_type, coded_type],
            compiler_params=params(24),
            cost_estimate=merge_cost,
            name="split",
        )(plane_x, near, send(away, across_core))
        kept[k] = (rest, tile)

    out_type = jax.ShapeDtypeStruct((shard, width), jnp.float32)
    mark_type = jax.ShapeDtypeStruct((8, 128), jnp.float32)
    mark_spec = pl.BlockSpec((8, 128), lambda i: (0, 0))
    bounds = [1 + (blocks - 1) * p // 7 for p in (0, 2, 4, 5, 5, 7)]
    grad = None

    def finish(part, ties):
        nonlocal grad
        low, high = bounds[part], bounds[part + 1]
        if high == low:
            return []
        operands = [by_col, decoder, factors, *chosen]
        specs = [
            pl.BlockSpec((BLOCK, ROWS), lambda i: (i + low, 0)),
            pl.BlockSpec((BLOCK, width), lambda i: (i + low, 0)),
            pl.BlockSpec((BLOCK, 128), lambda i: (i + low, 0)),
        ] + [whole_chunk] * COUNT
        operands += ties
        specs += [any_spec] * len(ties)
        aliases = {}
        if grad is not None:
            aliases = {len(operands): 0}
            operands.append(grad)
            specs.append(any_spec)
        rows = (high - low) * BLOCK
        grad, mark = pl.pallas_call(
            finish_kernel,
            grid=(high - low,),
            in_specs=specs,
            out_specs=[pl.BlockSpec((BLOCK, width), lambda i: (i + low, 0)), mark_spec],
            out_shape=[out_type, mark_type],
            input_output_aliases=aliases,
            compiler_params=params(44),
            cost_estimate=cost(2 * ROWS * rows * width, 6 * rows * width),
            name="finish",
        )(*operands)
        return [mark]

    lanes = range(4)
    across = [send(msg[k], across_x) for k in range(PAIRS)]
    ties = finish(0, msg)
    for k in range(PAIRS):
        kept[k], msg[k] = merge(kept[k], [across[k]], True, ties)
    arrivals = [[] for _ in range(PAIRS)]
    for level in range(3):
        for k in range(PAIRS):
            arrivals[k].append(send(msg[k], hop(level, lanes)))
        ties = finish(level + 1, msg)
        for k in range(PAIRS):
            if level < 2:
                msg[k] = merge(kept[k], arrivals[k][-1:], False, ties)
            else:
                kept[k], msg[k] = merge(kept[k], arrivals[k], True, ties)

    tile = kept[0][1]
    far = 4
    while far < per:
        moves = each([(w, w + far) for w in range(far)])
        fresh = (within >= far) & (within < 2 * far)
        tile = jnp.where(fresh, send(tile, moves), tile)
        far *= 2

    finish(4, msg)
    sums, row_specs = [], []
    narrow = BLOCK // 2
    for k in range(PAIRS):
        sums.append(kept[k][0])
        row_specs.append(pl.BlockSpec((narrow, piece), lambda i: (i, 0)))
        arrivals = [send(msg[k], each([(source, 0)])) for source in (2, 3, 1)]
        for arrived in (arrivals[0], arrivals[2], arrivals[1]):
            sums += [arrived, arrived]
            row_specs += [
                pl.BlockSpec((narrow, piece // 2), lambda i: (i, 0)),
                pl.BlockSpec((8, piece // 2), lambda i: (ROWS // 8, 0)),
            ]

    owner = jnp.reshape(here & (within == 0), (1,)).astype(jnp.int32)
    operands = [owner, by_col, decoder, factors, tile, *chosen, *sums]
    specs = [
        smem,
        pl.BlockSpec((narrow, ROWS), lambda i: (i, 0)),
        pl.BlockSpec((narrow, width), lambda i: (i, 0)),
        pl.BlockSpec((narrow, 128), lambda i: (i, 0)),
        pl.BlockSpec((8, 128), lambda i: (0, 0)),
    ]
    specs += [whole_chunk] * COUNT
    specs += row_specs
    aliases = {}
    if grad is not None:
        aliases = {len(operands): 0}
        operands.append(grad)
        specs.append(any_spec)
    decoder_grad, penalty = pl.pallas_call(
        functools.partial(last_kernel, DW / (ROWS * latents)),
        grid=(2,),
        in_specs=specs,
        out_specs=[pl.BlockSpec((narrow, width), lambda i: (i, 0)), smem],
        out_shape=[out_type, jax.ShapeDtypeStruct((1,), jnp.float32)],
        scratch_shapes=[pltpu.VMEM((narrow, width), jnp.float32)],
        input_output_aliases=aliases,
        compiler_params=params(44),
        name="finish_rows",
    )(*operands)

    return (penalty, decoder_grad)


def solution(mesh):
    in_specs = (P(("groups", "row"), None), P("groups"))
    out_specs = (P("groups"), P(("groups", "row"), None))
    return jax.shard_map(
        on_device, mesh=mesh, in_specs=in_specs, out_specs=out_specs, check_vma=False
    )
```

```python
import functools
import math

import jax
import jax.numpy as jnp
from jax import lax
from jax.experimental import pallas as pl
from jax.experimental.pallas import tpu as pltpu
from jax.sharding import PartitionSpec as P

DW = 4096
ROWS = 256
BLOCK = 256
WIDE = 512
PAIRS = 2
COUNT = 2 * PAIRS
MIB = 1024 * 1024
NT = (((1,), (1,)), ((), ()))


def params(mib):
    return pltpu.CompilerParams(vmem_limit_bytes=mib * MIB)


def cost(flops, moved):
    return pl.CostEstimate(flops=flops, bytes_accessed=moved, transcendentals=0)


def strip_inverse(ref, rows):
    width = ref.shape[1]
    total = None
    for t in range(0, width, 128):
        v = ref[rows, t : t + 128].astype(jnp.float32)
        total = v * v if total is None else total + v * v
    return 1.0 / jnp.sqrt(jnp.sum(total, axis=1, keepdims=True) + 1e-06)


def head_kernel(flags_ref, decoder_ref, *refs):
    chunk_refs, (held, sems) = refs[:COUNT], refs[COUNT:]
    step = chunk_refs[0].shape[1]
    strip = ROWS // 4

    def fetch(j):
        rows = pl.ds(j * strip, strip)
        return pltpu.make_async_copy(decoder_ref.at[rows, :], held.at[rows, :], sems.at[j])

    for j in range(4):
        fetch(j).start()
    for j in range(4):
        fetch(j).wait()
        rows = slice(j * strip, (j + 1) * strip)
        inverse = strip_inverse(held, rows)
        for k, ref in enumerate(chunk_refs):
            for t in range(0, step, 128):
                v = held[rows, k * step + t : k * step + t + 128].astype(jnp.float32)
                ref[rows, t : t + 128] = (v * inverse).astype(jnp.bfloat16)


def units_kernel(low, count, decoder_ref, *refs):
    units_ref, inverse_ref, held, sems = refs[-4:]
    strip = 64

    def fetch(j):
        return pltpu.make_async_copy(
            decoder_ref.at[pl.ds((low + j) * BLOCK, BLOCK), :], held.at[j % 2], sems.at[j % 2]
        )

    fetch(0).start()
    for j in range(count):
        if j + 1 < count:
            fetch(j + 1).start()
        fetch(j).wait()
        block = held.at[j % 2]
        for base in range(0, BLOCK, strip):
            rows = slice(base, base + strip)
            to = slice(j * BLOCK + base, j * BLOCK + base + strip)
            inverse = strip_inverse(block, rows)
            inverse_ref[to, :] = jnp.broadcast_to(inverse, (strip, 128))
            for t in range(0, block.shape[1], 128):
                v = block[rows, t : t + 128].astype(jnp.float32)
                units_ref[to, t : t + 128] = (v * inverse).astype(jnp.bfloat16)


def pair_cosines(k, units_ref, rows, low_ref, high_ref):
    step = low_ref.shape[1]
    base = 2 * k * step
    low = lax.dot_general(
        units_ref[rows, base : base + step],
        low_ref[...],
        NT,
        preferred_element_type=jnp.float32,
    )
    high = lax.dot_general(
        units_ref[rows, base + step : base + 2 * step],
        high_ref[...],
        NT,
        preferred_element_type=jnp.float32,
    )
    return low + high


def pick_kernel(slots, count, flags_ref, *refs):
    out_refs, sems = refs[-len(slots) - 1 : -1], refs[-1]
    for n, (slot, out_ref) in enumerate(zip(slots, out_refs)):
        for c in range(count):

            @pl.when(flags_ref[slot] == c)
            def _(out_ref=out_ref, c=c, n=n):
                pltpu.make_async_copy(refs[c], out_ref, sems.at[n]).start()

    for n, out_ref in enumerate(out_refs):
        pltpu.make_async_copy(refs[0], out_ref, sems.at[n]).wait()


def partial_kernel(k, parts, low_ref, high_ref, *refs):
    out_ref = refs[-1]
    base = 0
    for units_ref in refs[:parts]:
        count = units_ref.shape[0]
        size = min(WIDE, count)

        def body(j, carry, units_ref=units_ref, size=size, base=base):
            rows = pl.ds(pl.multiple_of(j * size, size), size)
            to = pl.ds(pl.multiple_of(base + j * size, size), size)
            out_ref[to, :] = pair_cosines(k, units_ref, rows, low_ref, high_ref)
            return carry

        lax.fori_loop(0, count // size, body, 0)
        base += count


def weight_kernel(k, parts, delta_ref, low_ref, high_ref, partial_ref, *refs):
    col_ref, row_ref, factor_ref, penalty_ref = refs[-4:]
    penalty_ref[...] = jnp.zeros_like(penalty_ref)
    base = 0
    for units_ref, inverse_ref in zip(refs[:parts], refs[parts : 2 * parts]):
        count = units_ref.shape[0]
        size = min(WIDE, count)

        def body(j, carry, units_ref=units_ref, inverse_ref=inverse_ref, size=size, base=base):
            here = pl.ds(pl.multiple_of(j * size, size), size)
            first = base + j * size
            span = pl.ds(pl.multiple_of(first, size), size)
            cosines = partial_ref[span, :] + pair_cosines(k, units_ref, here, low_ref, high_ref)
            latents = lax.broadcasted_iota(jnp.int32, (size, ROWS), 0) + (delta_ref[0] + first)
            rows = lax.broadcasted_iota(jnp.int32, (size, ROWS), 1)
            inside = (latents >= 0) & (latents < ROWS)
            weight = jnp.where(latents == rows, 0.0, jnp.where(inside, 0.5, 1.0))
            products = weight * cosines
            weighted = products.astype(jnp.bfloat16)
            col_ref[span, :] = weighted
            row_ref[:, span] = products.T.astype(jnp.bfloat16)
            along = jnp.sum(weighted.astype(jnp.float32) * cosines, axis=1, keepdims=True)
            inverse = inverse_ref[here, :]
            lanes = lax.broadcasted_iota(jnp.int32, (size, 128), 1)
            factor_ref[span, :] = jnp.where(lanes < 64, inverse, along * inverse)
            squares = products * cosines
            squares = squares[:, :128] + squares[:, 128:]
            penalty_ref[...] += jnp.sum(squares.reshape(size // 8, 8, 128), axis=0)
            return carry

        lax.fori_loop(0, count // size, body, 0)
        base += count


def row_kernel(k, parts, side_ref, row_ref, penalty_ref, *refs):
    out_ref = refs[-1]
    tile = out_ref.shape[1] // 2
    first = (2 * k + side_ref[0]) * out_ref.shape[1]
    for i in range(2):
        span = pl.ds(pl.multiple_of(first + i * tile, tile), tile)
        total, base = None, 0
        for units_ref in refs[:parts]:
            count = units_ref.shape[0]
            part = jnp.dot(
                row_ref[:, base : base + count],
                units_ref[:, span],
                preferred_element_type=jnp.float32,
            )
            total = part if total is None else total + part
            base += count
        out_ref[:ROWS, i * tile : (i + 1) * tile] = total
    out_ref[ROWS:, :] = jnp.concatenate([penalty_ref[...]] * (out_ref.shape[1] // 128), axis=1)


def finish_kernel(col_ref, decoder_ref, factor_ref, *refs):
    chunks = refs[:COUNT]
    out_ref, mark_ref = refs[-2:]
    step = chunks[0].shape[1]
    scale = (2.0 * math.sqrt(DW)) * factor_ref[:, :1]
    back = scale * factor_ref[:, 64:65]
    for k in range(COUNT):
        span = slice(k * step, (k + 1) * step)
        part = jnp.dot(col_ref[...], chunks[k][...], preferred_element_type=jnp.float32)
        out_ref[:, span] = scale * part - back * decoder_ref[:, span].astype(jnp.float32)
    mark_ref[...] = jnp.zeros_like(mark_ref)


STEPS = 32000.0
CODED_ROWS = ROWS + 16
PENALTY_STEPS = float(1 << 23)


def pack(coded):
    half = coded.shape[1] // 2
    return (coded[:, :half] << 16) | (coded[:, half:] & 0xFFFF)


def unpack(words):
    both = jnp.concatenate([words >> 16, (words << 16) >> 16], axis=1)
    return both.astype(jnp.float32)


def encode(value, penalty, msg_ref):
    top = jnp.max(jnp.abs(value), axis=0, keepdims=True)
    power = jnp.ceil(jnp.log2(jnp.maximum(top, 1e-35)) * 8.0)
    ratio = value * jnp.exp2(power * -0.125)
    coded = ratio * lax.rsqrt(jnp.maximum(jnp.abs(ratio), 1e-30))
    msg_ref[:ROWS, :] = pack(jnp.round(coded * STEPS).astype(jnp.int32))
    power = pack(power.astype(jnp.int32))
    msg_ref[ROWS : ROWS + 8, :] = jnp.broadcast_to(power, (8, power.shape[1]))
    top = jnp.max(jnp.max(penalty, axis=1, keepdims=True), axis=0, keepdims=True)
    power = jnp.ceil(jnp.log2(jnp.maximum(top, 1e-35)))
    coded = jnp.round(penalty * (jnp.exp2(-power) * PENALTY_STEPS)).astype(jnp.int32)
    msg_ref[ROWS + 8 :, :128] = coded
    msg_ref[ROWS + 8 :, 128:] = jnp.broadcast_to(power.astype(jnp.int32), (8, 128))


def decode(words, powers):
    coded = unpack(words)
    scale = jnp.exp2(unpack(powers)[:1, :] * 0.125) * (1.0 / (STEPS * STEPS))
    return coded * jnp.abs(coded) * scale


def decode_at(msg_ref):
    value = decode(msg_ref[:ROWS, :], msg_ref[ROWS : ROWS + 8, :])
    power = msg_ref[ROWS + 8 :, 128:].astype(jnp.float32)
    penalty = msg_ref[ROWS + 8 :, :128].astype(jnp.float32) * (jnp.exp2(power) / PENALTY_STEPS)
    return value, penalty


def split_kernel(odd_ref, mine_ref, theirs_ref, kept_ref, penalty_ref, msg_ref):
    piece = kept_ref.shape[1]
    penalty = mine_ref[ROWS:, :128] + theirs_ref[ROWS:, :128]
    penalty_ref[...] = penalty
    low, high = slice(0, piece), slice(piece, 2 * piece)

    def divide(keep, away):
        kept_ref[...] = mine_ref[:ROWS, keep] + theirs_ref[:ROWS, keep]
        encode(mine_ref[:ROWS, away] + theirs_ref[:ROWS, away], penalty, msg_ref)

    @pl.when(odd_ref[0] == 0)
    def _():
        divide(low, high)

    @pl.when(odd_ref[0] == 1)
    def _():
        divide(high, low)


def merge_kernel(arrived, keep, kept_ref, penalty_ref, *refs):
    value, penalty = kept_ref[...], penalty_ref[...]
    for msg_ref in refs[:arrived]:
        more, more_penalty = decode_at(msg_ref)
        value, penalty = value + more, penalty + more_penalty
    if keep:
        refs[-3][...] = value
        refs[-2][...] = penalty
    encode(value, penalty, refs[-1])


def last_kernel(share, owner_ref, col_ref, decoder_ref, factor_ref, tile_ref, *refs):
    chunks, sums = refs[:COUNT], refs[COUNT : COUNT + 7 * PAIRS]
    out_ref, penalty_ref, column = refs[-3:]
    penalty_ref[0] = jnp.sum(tile_ref[...]) * share
    step = chunks[0].shape[1]
    piece = step // 2
    owner = owner_ref[0] == 1
    total = jnp.zeros((col_ref.shape[0], 128), jnp.float32)
    for k in range(COUNT):
        span = slice(k * step, (k + 1) * step)
        part = jnp.dot(col_ref[...], chunks[k][...], preferred_element_type=jnp.float32)
        own, *coded = sums[7 * (k // 2) : 7 * (k // 2) + 7]
        pieces = [own[...]] + [
            decode(coded[2 * p][...], coded[2 * p + 1][...]) for p in range(3)
        ]
        row_sum = jnp.concatenate(pieces[2 * (k % 2) : 2 * (k % 2) + 2], axis=1)
        part = part + jnp.where(owner, row_sum, 0.0)
        column[:, span] = part
        along = part * decoder_ref[:, span].astype(jnp.float32)
        for t in range(0, step, 128):
            total = total + along[:, t : t + 128]
    inverse = factor_ref[:, :1]
    scale = (2.0 * math.sqrt(DW)) * inverse
    back = scale * (jnp.sum(total, axis=1, keepdims=True) * inverse * inverse)
    for k in range(COUNT):
        span = slice(k * step, (k + 1) * step)
        out_ref[:, span] = scale * column[:, span] - back * decoder_ref[:, span].astype(
            jnp.float32
        )


def on_device(decoder, quarter):
    shard, width = decoder.shape
    devices = lax.axis_size("row")
    index = lax.axis_index("row")
    per = devices // 4
    latents = shard * devices
    blocks = shard // BLOCK
    step = width // COUNT
    chosen_quarter = quarter[0]
    start = chosen_quarter * (latents // 4)
    place = index // per
    within = index % per
    here = place == chosen_quarter
    even_chip = (within // 2) % 2 == 0
    smem = pl.BlockSpec(memory_space=pltpu.SMEM)

    def send(value, pairs):
        return lax.ppermute(value, "row", pairs)

    def each(moves):
        return [(z * per + a, z * per + b) for z in range(4) for a, b in moves]

    near = jnp.where(place == 1, chosen_quarter == 0, chosen_quarter == 3)
    middle = (place == 1) | (place == 2)
    reached = jnp.where(here, 0, jnp.where(middle, jnp.where(near, 1, 2), 3))
    core_index = within % 2
    fresh = [(within >= 4 << n) & (within < 8 << n) for n in range((per // 4).bit_length() - 1)]
    TAKES, WAITS, REACHED, LOW, HIGH, FRESH = range(6)
    flags = jnp.stack(
        [
            jnp.where(within == 2, 1, 0),
            jnp.where(here, 0, 1),
            reached,
            jnp.where(even_chip, 0, 2) + core_index,
            jnp.where(even_chip, 2, 0) + core_index,
        ]
        + [jnp.where(value, 1, 0) for value in fresh]
    ).astype(jnp.int32)

    pinned = pl.BlockSpec(memory_space=pl.ANY)
    any_spec = pinned
    vmem = pl.BlockSpec(memory_space=pltpu.VMEM)
    chunk_type = jax.ShapeDtypeStruct((ROWS, step), jnp.bfloat16)
    own = pl.pallas_call(
        head_kernel,
        in_specs=[smem, pinned],
        out_specs=[vmem] * COUNT,
        out_shape=[chunk_type] * COUNT,
        scratch_shapes=[
            pltpu.VMEM((ROWS, width), jnp.bfloat16),
            pltpu.SemaphoreType.DMA((4,)),
        ],
        compiler_params=params(50),
        cost_estimate=cost(4 * ROWS * width, 4 * ROWS * width),
        name="head_units",
    )(flags, decoder)

    across_x = each([(0, 2), (2, 0), (1, 3), (3, 1)])
    across_core = each([(0, 1), (1, 0), (2, 3), (3, 2)])
    piece = step // 2

    def hop(level, lanes):
        moves = (((0, 1), (3, 2)), ((1, 2), (2, 1)), ((2, 3), (1, 0)))[level]
        return [(a * per + w, b * per + w) for a, b in moves for w in lanes]

    def pick(slots, candidates, ties=()):
        return pl.pallas_call(
            functools.partial(pick_kernel, slots, len(candidates)),
            in_specs=[smem] + [any_spec] * (len(candidates) + len(ties)),
            out_specs=[vmem] * len(slots),
            out_shape=[chunk_type] * len(slots),
            scratch_shapes=[pltpu.SemaphoreType.DMA((len(slots),))],
            compiler_params=params(12),
            cost_estimate=cost(ROWS * step, 4 * ROWS * step),
            name="pick",
        )(flags, *candidates, *ties)

    unit_bounds = [blocks * p // 4 for p in range(5)]
    units, inverses = [], []

    def make_units(part, tie):
        low, high = unit_bounds[part], unit_bounds[part + 1]
        if high == low:
            return []
        rows = (high - low) * BLOCK
        made = pl.pallas_call(
            functools.partial(units_kernel, low, high - low),
            in_specs=[pinned, any_spec],
            out_specs=[vmem, vmem],
            out_shape=[
                jax.ShapeDtypeStruct((rows, width), jnp.bfloat16),
                jax.ShapeDtypeStruct((rows, 128), jnp.float32),
            ],
            scratch_shapes=[
                pltpu.VMEM((2, BLOCK, width), jnp.bfloat16),
                pltpu.SemaphoreType.DMA((2,)),
            ],
            compiler_params=params((37, 33, 29, 25)[part]),
            cost_estimate=cost(4 * rows * width, 4 * rows * width),
            name="units",
        )(decoder, tie)
        units.append(made[0])
        inverses.append(made[1])
        return [made[1]]

    mine, first, second, third, held = ([None] * PAIRS for _ in range(5))
    across = [send(own[2 * k + 1], each([(0, 2)])) for k in range(PAIRS)]
    done = make_units(0, own[0])
    for k in range(PAIRS):
        [mine[k]] = pick([TAKES], [own[2 * k], across[k]], () if k else done)
        first[k] = send(mine[k], hop(0, (0, 2)))
    done = make_units(1, mine[PAIRS - 1])
    for k in range(PAIRS):
        [going] = pick([WAITS], [mine[k], first[k]], () if k else done)
        second[k] = send(going, hop(1, (0, 2)))
    for k in range(PAIRS):
        [going] = pick([WAITS], [mine[k], second[k]], done if k else ())
        third[k] = send(going, hop(2, (0, 2)))
        if k == 0:
            done = make_units(2, going)
    for k in range(PAIRS):
        [held[k]] = pick([REACHED], [mine[k], first[k], second[k], third[k]])
    done = make_units(3, held[PAIRS - 1])
    chosen = []
    for k in range(PAIRS):
        other = send(held[k], each([(0, 2), (2, 0)]))
        core_held = send(held[k], each([(0, 1), (2, 3)]))
        core_other = send(other, each([(0, 1), (2, 3)]))
        pair = pick(
            [LOW, HIGH], [held[k], core_held, other, core_other], () if k else done
        )
        for n in range(len(fresh)):
            moves = each([(w, w + (4 << n)) for w in range(4 << n)])
            pair = [pick([FRESH + n], [value, send(value, moves)])[0] for value in pair]
        chosen += pair

    delta = jnp.reshape(index * shard - start, (1,)).astype(jnp.int32)
    whole_chunk = pl.BlockSpec((ROWS, step), lambda i: (0, 0))
    half_flops = ROWS * shard * width
    parts = len(units)
    partial = pl.pallas_call(
        functools.partial(partial_kernel, 0, parts),
        in_specs=[vmem] * (2 + parts),
        out_specs=vmem,
        out_shape=jax.ShapeDtypeStruct((shard, ROWS), jnp.float32),
        compiler_params=params(16),
        cost_estimate=cost(half_flops, shard * width),
        name="part_cosines",
    )(chosen[0], chosen[1], *units)
    by_col, by_row, factors, local_penalty = pl.pallas_call(
        functools.partial(weight_kernel, 1, parts),
        in_specs=[smem] + [vmem] * (3 + 2 * parts),
        out_specs=[vmem] * 4,
        out_shape=[
            jax.ShapeDtypeStruct((shard, ROWS), jnp.bfloat16),
            jax.ShapeDtypeStruct((ROWS, shard), jnp.bfloat16),
            jax.ShapeDtypeStruct((shard, 128), jnp.float32),
            jax.ShapeDtypeStruct((8, 128), jnp.float32),
        ],
        compiler_params=params(16),
        cost_estimate=cost(half_flops, shard * width),
        name="weights",
    )(delta, chosen[2], chosen[3], partial, *units, *inverses)

    core_side = within % 2
    plane_x = jnp.reshape((within // 2) % 2, (1,)).astype(jnp.int32)
    tall = ROWS + 8
    coded_type = jax.ShapeDtypeStruct((CODED_ROWS, piece // 2), jnp.int32)
    piece_type = jax.ShapeDtypeStruct((ROWS, piece), jnp.float32)
    tile_type = jax.ShapeDtypeStruct((8, 128), jnp.float32)
    merge_cost = cost(20 * ROWS * piece, 12 * ROWS * piece)

    def row_part(k, side):
        return pl.pallas_call(
            functools.partial(row_kernel, k, parts),
            in_specs=[smem] + [vmem] * (2 + parts),
            out_specs=vmem,
            out_shape=jax.ShapeDtypeStruct((tall, step), jnp.float32),
            compiler_params=params(24),
            cost_estimate=cost(half_flops // 2, shard * width // 2),
            name="row_part",
        )(jnp.reshape(side, (1,)).astype(jnp.int32), by_row, local_penalty, *units)

    def merge(kept, arrived, keep, ties=()):
        tiles = [piece_type, tile_type, coded_type] if keep else [coded_type]
        result = pl.pallas_call(
            functools.partial(merge_kernel, len(arrived), keep),
            in_specs=[vmem] * (2 + len(arrived)) + [any_spec] * len(ties),
            out_specs=[vmem] * len(tiles),
            out_shape=tiles,
            compiler_params=params(24),
            cost_estimate=merge_cost,
            name="merge",
        )(*kept, *arrived, *ties)
        return (tuple(result[:2]), result[2]) if keep else result[0]

    kept, msg = [None] * PAIRS, [None] * PAIRS
    for k in range(PAIRS):
        away, near = row_part(k, 1 - core_side), row_part(k, core_side)
        far = per // 2
        while far >= 4:
            moves = each([(w + far, w) for w in range(far)])
            away, near = away + send(away, moves), near + send(near, moves)
            far //= 2
        rest, tile, msg[k] = pl.pallas_call(
            split_kernel,
            in_specs=[smem, vmem, vmem],
            out_specs=[vmem, vmem, vmem],
            out_shape=[piece_type, tile_type, coded_type],
            compiler_params=params(24),
            cost_estimate=merge_cost,
            name="split",
        )(plane_x, near, send(away, across_core))
        kept[k] = (rest, tile)

    out_type = jax.ShapeDtypeStruct((shard, width), jnp.float32)
    mark_type = jax.ShapeDtypeStruct((8, 128), jnp.float32)
    mark_spec = pl.BlockSpec((8, 128), lambda i: (0, 0))
    bounds = [1 + (blocks - 1) * p // 7 for p in (0, 2, 4, 5, 5, 7)]
    grad = None

    def finish(part, tie):
        nonlocal grad
        low, high = bounds[part], bounds[part + 1]
        if high == low:
            return []
        operands = [by_col, decoder, factors, *chosen]
        specs = [
            pl.BlockSpec((BLOCK, ROWS), lambda i: (i + low, 0)),
            pl.BlockSpec((BLOCK, width), lambda i: (i + low, 0)),
            pl.BlockSpec((BLOCK, 128), lambda i: (i + low, 0)),
        ] + [whole_chunk] * COUNT
        operands.append(tie)
        specs.append(any_spec)
        aliases = {}
        if grad is not None:
            aliases = {len(operands): 0}
            operands.append(grad)
            specs.append(any_spec)
        rows = (high - low) * BLOCK
        grad, mark = pl.pallas_call(
            finish_kernel,
            grid=(high - low,),
            in_specs=specs,
            out_specs=[pl.BlockSpec((BLOCK, width), lambda i: (i + low, 0)), mark_spec],
            out_shape=[out_type, mark_type],
            input_output_aliases=aliases,
            compiler_params=params(50),
            cost_estimate=cost(2 * ROWS * rows * width, 6 * rows * width),
            name="finish",
        )(*operands)
        return [mark]

    lanes = range(4)
    across = [send(msg[k], across_x) for k in range(PAIRS)]
    ties = finish(0, msg[PAIRS - 1])
    for k in range(PAIRS):
        kept[k], msg[k] = merge(kept[k], [across[k]], True, () if k else ties)
    arrivals = [[] for _ in range(PAIRS)]
    for level in range(3):
        for k in range(PAIRS):
            arrivals[k].append(send(msg[k], hop(level, lanes)))
        ties = finish(level + 1, msg[PAIRS - 1])
        for k in range(PAIRS):
            tied = () if k else ties
            if level < 2:
                msg[k] = merge(kept[k], arrivals[k][-1:], False, tied)
            else:
                kept[k], msg[k] = merge(kept[k], arrivals[k], True, tied)

    tile = kept[0][1]
    far = 4
    while far < per:
        moves = each([(w, w + far) for w in range(far)])
        fresh = (within >= far) & (within < 2 * far)
        tile = jnp.where(fresh, send(tile, moves), tile)
        far *= 2

    finish(4, msg[PAIRS - 1])
    sums, row_specs = [], []
    narrow = BLOCK // 2
    for k in range(PAIRS):
        sums.append(kept[k][0])
        row_specs.append(pl.BlockSpec((narrow, piece), lambda i: (i, 0)))
        arrivals = [send(msg[k], each([(source, 0)])) for source in (2, 3, 1)]
        for arrived in (arrivals[0], arrivals[2], arrivals[1]):
            sums += [arrived, arrived]
            row_specs += [
                pl.BlockSpec((narrow, piece // 2), lambda i: (i, 0)),
                pl.BlockSpec((8, piece // 2), lambda i: (ROWS // 8, 0)),
            ]

    owner = jnp.reshape(here & (within == 0), (1,)).astype(jnp.int32)
    operands = [owner, by_col, decoder, factors, tile, *chosen, *sums]
    specs = [
        smem,
        pl.BlockSpec((narrow, ROWS), lambda i: (i, 0)),
        pl.BlockSpec((narrow, width), lambda i: (i, 0)),
        pl.BlockSpec((narrow, 128), lambda i: (i, 0)),
        pl.BlockSpec((8, 128), lambda i: (0, 0)),
    ]
    specs += [whole_chunk] * COUNT
    specs += row_specs
    aliases = {}
    if grad is not None:
        aliases = {len(operands): 0}
        operands.append(grad)
        specs.append(any_spec)
    decoder_grad, penalty = pl.pallas_call(
        functools.partial(last_kernel, DW / (ROWS * latents)),
        grid=(2,),
        in_specs=specs,
        out_specs=[pl.BlockSpec((narrow, width), lambda i: (i, 0)), smem],
        out_shape=[out_type, jax.ShapeDtypeStruct((1,), jnp.float32)],
        scratch_shapes=[pltpu.VMEM((narrow, width), jnp.float32)],
        input_output_aliases=aliases,
        compiler_params=params(50),
        name="finish_rows",
    )(*operands)

    return (penalty, decoder_grad)


def solution(mesh):
    in_specs = (P(("groups", "row"), None), P("groups"))
    out_specs = (P("groups"), P(("groups", "row"), None))
    return jax.shard_map(
        on_device, mesh=mesh, in_specs=in_specs, out_specs=out_specs, check_vma=False
    )
```

```python
import functools
import math

import jax
import jax.numpy as jnp
from jax import lax
from jax.experimental import pallas as pl
from jax.experimental.pallas import tpu as pltpu
from jax.sharding import PartitionSpec as P

DW = 4096
ROWS = 256
BLOCK = 256
WIDE = 512
PAIRS = 2
COUNT = 2 * PAIRS
MIB = 1024 * 1024
NT = (((1,), (1,)), ((), ()))


def params(mib):
    return pltpu.CompilerParams(vmem_limit_bytes=mib * MIB)


def cost(flops, moved):
    return pl.CostEstimate(flops=flops, bytes_accessed=moved, transcendentals=0)


def strip_inverse(ref, rows):
    width = ref.shape[1]
    total = None
    for t in range(0, width, 128):
        v = ref[rows, t : t + 128].astype(jnp.float32)
        total = v * v if total is None else total + v * v
    return 1.0 / jnp.sqrt(jnp.sum(total, axis=1, keepdims=True) + 1e-06)


def head_kernel(flags_ref, decoder_ref, *refs):
    chunk_refs, (held, sems) = refs[:COUNT], refs[COUNT:]
    step = chunk_refs[0].shape[1]
    strip = ROWS // 4

    def fetch(j):
        rows = pl.ds(j * strip, strip)
        return pltpu.make_async_copy(decoder_ref.at[rows, :], held.at[rows, :], sems.at[j])

    for j in range(4):
        fetch(j).start()
    for j in range(4):
        fetch(j).wait()
        rows = slice(j * strip, (j + 1) * strip)
        inverse = strip_inverse(held, rows)
        for k, ref in enumerate(chunk_refs):
            for t in range(0, step, 128):
                v = held[rows, k * step + t : k * step + t + 128].astype(jnp.float32)
                ref[rows, t : t + 128] = (v * inverse).astype(jnp.bfloat16)


def units_kernel(low, count, away, decoder_ref, *refs):
    strip = 64
    if away:
        _, target_ref, inverse_ref, held, sems, units_ref, out_sems = refs
    else:
        _, units_ref, inverse_ref, held, sems = refs

    def leave(j):
        rows = pl.ds(j * BLOCK, BLOCK)
        return pltpu.make_async_copy(
            units_ref.at[rows, :], target_ref.at[rows, :], out_sems.at[j]
        )

    def fetch(j):
        return pltpu.make_async_copy(
            decoder_ref.at[pl.ds((low + j) * BLOCK, BLOCK), :], held.at[j % 2], sems.at[j % 2]
        )

    fetch(0).start()
    for j in range(count):
        if j + 1 < count:
            fetch(j + 1).start()
        fetch(j).wait()
        block = held.at[j % 2]
        for base in range(0, BLOCK, strip):
            rows = slice(base, base + strip)
            to = slice(j * BLOCK + base, j * BLOCK + base + strip)
            inverse = strip_inverse(block, rows)
            inverse_ref[to, :] = jnp.broadcast_to(inverse, (strip, 128))
            for t in range(0, block.shape[1], 128):
                v = block[rows, t : t + 128].astype(jnp.float32)
                units_ref[to, t : t + 128] = (v * inverse).astype(jnp.bfloat16)
        if away:
            leave(j).start()
    if away:
        for j in range(count):
            leave(j).wait()


def pair_cosines(k, units_ref, rows, low_ref, high_ref):
    step = low_ref.shape[1]
    base = 2 * k * step
    low = lax.dot_general(
        units_ref[rows, base : base + step],
        low_ref[...],
        NT,
        preferred_element_type=jnp.float32,
    )
    high = lax.dot_general(
        units_ref[rows, base + step : base + 2 * step],
        high_ref[...],
        NT,
        preferred_element_type=jnp.float32,
    )
    return low + high


def pick_kernel(slots, count, flags_ref, *refs):
    out_refs, sems = refs[-len(slots) - 1 : -1], refs[-1]
    for n, (slot, out_ref) in enumerate(zip(slots, out_refs)):
        for c in range(count):

            @pl.when(flags_ref[slot] == c)
            def _(out_ref=out_ref, c=c, n=n):
                pltpu.make_async_copy(refs[c], out_ref, sems.at[n]).start()

    for n, out_ref in enumerate(out_refs):
        pltpu.make_async_copy(refs[0], out_ref, sems.at[n]).wait()


def partial_kernel(k, parts, low_ref, high_ref, *refs):
    out_ref = refs[-1]
    base = 0
    for units_ref in refs[:parts]:
        count = units_ref.shape[0]
        size = min(WIDE, count)

        def body(j, carry, units_ref=units_ref, size=size, base=base):
            rows = pl.ds(pl.multiple_of(j * size, size), size)
            to = pl.ds(pl.multiple_of(base + j * size, size), size)
            out_ref[to, :] = pair_cosines(k, units_ref, rows, low_ref, high_ref)
            return carry

        lax.fori_loop(0, count // size, body, 0)
        base += count


def weight_kernel(k, parts, delta_ref, low_ref, high_ref, partial_ref, *refs):
    col_ref, row_ref, factor_ref, penalty_ref = refs[-4:]
    penalty_ref[...] = jnp.zeros_like(penalty_ref)
    base = 0
    for units_ref, inverse_ref in zip(refs[:parts], refs[parts : 2 * parts]):
        count = units_ref.shape[0]
        size = min(WIDE, count)

        def body(j, carry, units_ref=units_ref, inverse_ref=inverse_ref, size=size, base=base):
            here = pl.ds(pl.multiple_of(j * size, size), size)
            first = base + j * size
            span = pl.ds(pl.multiple_of(first, size), size)
            cosines = partial_ref[span, :] + pair_cosines(k, units_ref, here, low_ref, high_ref)
            latents = lax.broadcasted_iota(jnp.int32, (size, ROWS), 0) + (delta_ref[0] + first)
            rows = lax.broadcasted_iota(jnp.int32, (size, ROWS), 1)
            inside = (latents >= 0) & (latents < ROWS)
            weight = jnp.where(latents == rows, 0.0, jnp.where(inside, 0.5, 1.0))
            products = weight * cosines
            weighted = products.astype(jnp.bfloat16)
            col_ref[span, :] = weighted
            row_ref[:, span] = products.T.astype(jnp.bfloat16)
            along = jnp.sum(weighted.astype(jnp.float32) * cosines, axis=1, keepdims=True)
            inverse = inverse_ref[here, :]
            lanes = lax.broadcasted_iota(jnp.int32, (size, 128), 1)
            factor_ref[span, :] = jnp.where(lanes < 64, inverse, along * inverse)
            squares = products * cosines
            squares = squares[:, :128] + squares[:, 128:]
            penalty_ref[...] += jnp.sum(squares.reshape(size // 8, 8, 128), axis=0)
            return carry

        lax.fori_loop(0, count // size, body, 0)
        base += count


def row_kernel(k, parts, side_ref, row_ref, penalty_ref, *refs):
    out_ref = refs[-1]
    tile = out_ref.shape[1] // 2
    first = (2 * k + side_ref[0]) * out_ref.shape[1]
    for i in range(2):
        span = pl.ds(pl.multiple_of(first + i * tile, tile), tile)
        total, base = None, 0
        for units_ref in refs[:parts]:
            count = units_ref.shape[0]
            part = jnp.dot(
                row_ref[:, base : base + count],
                units_ref[:, span],
                preferred_element_type=jnp.float32,
            )
            total = part if total is None else total + part
            base += count
        out_ref[:ROWS, i * tile : (i + 1) * tile] = total
    out_ref[ROWS:, :] = jnp.concatenate([penalty_ref[...]] * (out_ref.shape[1] // 128), axis=1)


def finish_kernel(col_ref, decoder_ref, factor_ref, *refs):
    chunks = refs[:COUNT]
    out_ref, mark_ref = refs[-2:]
    step = chunks[0].shape[1]
    scale = (2.0 * math.sqrt(DW)) * factor_ref[:, :1]
    back = scale * factor_ref[:, 64:65]
    for k in range(COUNT):
        span = slice(k * step, (k + 1) * step)
        part = jnp.dot(col_ref[...], chunks[k][...], preferred_element_type=jnp.float32)
        out_ref[:, span] = scale * part - back * decoder_ref[:, span].astype(jnp.float32)
    mark_ref[...] = jnp.zeros_like(mark_ref)


STEPS = 32000.0
CODED_ROWS = ROWS + 16
PENALTY_STEPS = float(1 << 23)


def pack(coded):
    half = coded.shape[1] // 2
    return (coded[:, :half] << 16) | (coded[:, half:] & 0xFFFF)


def unpack(words):
    both = jnp.concatenate([words >> 16, (words << 16) >> 16], axis=1)
    return both.astype(jnp.float32)


def encode(value, penalty, msg_ref):
    top = jnp.max(jnp.abs(value), axis=0, keepdims=True)
    power = jnp.ceil(jnp.log2(jnp.maximum(top, 1e-35)) * 8.0)
    ratio = value * jnp.exp2(power * -0.125)
    coded = ratio * lax.rsqrt(jnp.maximum(jnp.abs(ratio), 1e-30))
    msg_ref[:ROWS, :] = pack(jnp.round(coded * STEPS).astype(jnp.int32))
    power = pack(power.astype(jnp.int32))
    msg_ref[ROWS : ROWS + 8, :] = jnp.broadcast_to(power, (8, power.shape[1]))
    top = jnp.max(jnp.max(penalty, axis=1, keepdims=True), axis=0, keepdims=True)
    power = jnp.ceil(jnp.log2(jnp.maximum(top, 1e-35)))
    coded = jnp.round(penalty * (jnp.exp2(-power) * PENALTY_STEPS)).astype(jnp.int32)
    msg_ref[ROWS + 8 :, :128] = coded
    msg_ref[ROWS + 8 :, 128:] = jnp.broadcast_to(power.astype(jnp.int32), (8, 128))


def decode(words, powers):
    coded = unpack(words)
    scale = jnp.exp2(unpack(powers)[:1, :] * 0.125) * (1.0 / (STEPS * STEPS))
    return coded * jnp.abs(coded) * scale


def decode_at(msg_ref):
    value = decode(msg_ref[:ROWS, :], msg_ref[ROWS : ROWS + 8, :])
    power = msg_ref[ROWS + 8 :, 128:].astype(jnp.float32)
    penalty = msg_ref[ROWS + 8 :, :128].astype(jnp.float32) * (jnp.exp2(power) / PENALTY_STEPS)
    return value, penalty


def split_kernel(odd_ref, mine_ref, theirs_ref, kept_ref, penalty_ref, msg_ref):
    piece = kept_ref.shape[1]
    penalty = mine_ref[ROWS:, :128] + theirs_ref[ROWS:, :128]
    penalty_ref[...] = penalty
    low, high = slice(0, piece), slice(piece, 2 * piece)

    def divide(keep, away):
        kept_ref[...] = mine_ref[:ROWS, keep] + theirs_ref[:ROWS, keep]
        encode(mine_ref[:ROWS, away] + theirs_ref[:ROWS, away], penalty, msg_ref)

    @pl.when(odd_ref[0] == 0)
    def _():
        divide(low, high)

    @pl.when(odd_ref[0] == 1)
    def _():
        divide(high, low)


def merge_kernel(arrived, keep, kept_ref, penalty_ref, *refs):
    value, penalty = kept_ref[...], penalty_ref[...]
    for msg_ref in refs[:arrived]:
        more, more_penalty = decode_at(msg_ref)
        value, penalty = value + more, penalty + more_penalty
    if keep:
        refs[-3][...] = value
        refs[-2][...] = penalty
    encode(value, penalty, refs[-1])


def last_kernel(share, owner_ref, col_ref, decoder_ref, factor_ref, tile_ref, *refs):
    chunks, sums = refs[:COUNT], refs[COUNT : COUNT + 7 * PAIRS]
    out_ref, penalty_ref, column = refs[-3:]
    penalty_ref[0] = jnp.sum(tile_ref[...]) * share
    step = chunks[0].shape[1]
    piece = step // 2
    owner = owner_ref[0] == 1
    total = jnp.zeros((col_ref.shape[0], 128), jnp.float32)
    for k in range(COUNT):
        span = slice(k * step, (k + 1) * step)
        part = jnp.dot(col_ref[...], chunks[k][...], preferred_element_type=jnp.float32)
        own, *coded = sums[7 * (k // 2) : 7 * (k // 2) + 7]
        pieces = [own[...]] + [
            decode(coded[2 * p][...], coded[2 * p + 1][...]) for p in range(3)
        ]
        row_sum = jnp.concatenate(pieces[2 * (k % 2) : 2 * (k % 2) + 2], axis=1)
        part = part + jnp.where(owner, row_sum, 0.0)
        column[:, span] = part
        along = part * decoder_ref[:, span].astype(jnp.float32)
        for t in range(0, step, 128):
            total = total + along[:, t : t + 128]
    inverse = factor_ref[:, :1]
    scale = (2.0 * math.sqrt(DW)) * inverse
    back = scale * (jnp.sum(total, axis=1, keepdims=True) * inverse * inverse)
    for k in range(COUNT):
        span = slice(k * step, (k + 1) * step)
        out_ref[:, span] = scale * column[:, span] - back * decoder_ref[:, span].astype(
            jnp.float32
        )


def on_device(decoder, quarter):
    shard, width = decoder.shape
    devices = lax.axis_size("row")
    index = lax.axis_index("row")
    per = devices // 4
    latents = shard * devices
    blocks = shard // BLOCK
    step = width // COUNT
    chosen_quarter = quarter[0]
    start = chosen_quarter * (latents // 4)
    place = index // per
    within = index % per
    here = place == chosen_quarter
    even_chip = (within // 2) % 2 == 0
    smem = pl.BlockSpec(memory_space=pltpu.SMEM)

    def send(value, pairs):
        return lax.ppermute(value, "row", pairs)

    def each(moves):
        return [(z * per + a, z * per + b) for z in range(4) for a, b in moves]

    near = jnp.where(place == 1, chosen_quarter == 0, chosen_quarter == 3)
    middle = (place == 1) | (place == 2)
    reached = jnp.where(here, 0, jnp.where(middle, jnp.where(near, 1, 2), 3))
    core_index = within % 2
    fresh = [(within >= 4 << n) & (within < 8 << n) for n in range((per // 4).bit_length() - 1)]
    TAKES, WAITS, REACHED, LOW, HIGH, FRESH = range(6)
    flags = jnp.stack(
        [
            jnp.where(within == 2, 1, 0),
            jnp.where(here, 0, 1),
            reached,
            jnp.where(even_chip, 0, 2) + core_index,
            jnp.where(even_chip, 2, 0) + core_index,
        ]
        + [jnp.where(value, 1, 0) for value in fresh]
    ).astype(jnp.int32)

    pinned = pl.BlockSpec(memory_space=pl.ANY)
    any_spec = pinned
    vmem = pl.BlockSpec(memory_space=pltpu.VMEM)
    chunk_type = jax.ShapeDtypeStruct((ROWS, step), jnp.bfloat16)
    own = pl.pallas_call(
        head_kernel,
        in_specs=[smem, pinned],
        out_specs=[vmem] * COUNT,
        out_shape=[chunk_type] * COUNT,
        scratch_shapes=[
            pltpu.VMEM((ROWS, width), jnp.bfloat16),
            pltpu.SemaphoreType.DMA((4,)),
        ],
        compiler_params=params(50),
        cost_estimate=cost(4 * ROWS * width, 4 * ROWS * width),
        name="head_units",
    )(flags, decoder)

    across_x = each([(0, 2), (2, 0), (1, 3), (3, 1)])
    across_core = each([(0, 1), (1, 0), (2, 3), (3, 2)])
    piece = step // 2

    def hop(level, lanes):
        moves = (((0, 1), (3, 2)), ((1, 2), (2, 1)), ((2, 3), (1, 0)))[level]
        return [(a * per + w, b * per + w) for a, b in moves for w in lanes]

    def pick(slots, candidates, ties=()):
        return pl.pallas_call(
            functools.partial(pick_kernel, slots, len(candidates)),
            in_specs=[smem] + [any_spec] * (len(candidates) + len(ties)),
            out_specs=[vmem] * len(slots),
            out_shape=[chunk_type] * len(slots),
            scratch_shapes=[pltpu.SemaphoreType.DMA((len(slots),))],
            compiler_params=params(12),
            cost_estimate=cost(ROWS * step, 4 * ROWS * step),
            name="pick",
        )(flags, *candidates, *ties)

    unit_bounds = [blocks * p // 4 for p in range(5)]
    units, inverses = [], []

    def make_units(part, tie):
        low, high = unit_bounds[part], unit_bounds[part + 1]
        if high == low:
            return []
        rows = (high - low) * BLOCK
        away = part < 3
        extra = [
            pltpu.VMEM((rows, width), jnp.bfloat16),
            pltpu.SemaphoreType.DMA((high - low,)),
        ]
        made = pl.pallas_call(
            functools.partial(units_kernel, low, high - low, away),
            in_specs=[pinned, any_spec],
            out_specs=[pl.BlockSpec(memory_space=pltpu.HBM) if away else vmem, vmem],
            out_shape=[
                jax.ShapeDtypeStruct((rows, width), jnp.bfloat16),
                jax.ShapeDtypeStruct((rows, 128), jnp.float32),
            ],
            scratch_shapes=[
                pltpu.VMEM((2, BLOCK, width), jnp.bfloat16),
                pltpu.SemaphoreType.DMA((2,)),
            ]
            + (extra if away else []),
            compiler_params=params((50, 50, 50, 36)[part]),
            cost_estimate=cost(4 * rows * width, 4 * rows * width),
            name="units",
        )(decoder, tie)
        units.append(made[0])
        inverses.append(made[1])
        return [made[1]]

    mine, first, second, third, held = ([None] * PAIRS for _ in range(5))
    across = [send(own[2 * k + 1], each([(0, 2)])) for k in range(PAIRS)]
    done = make_units(0, own[0])
    for k in range(PAIRS):
        [mine[k]] = pick([TAKES], [own[2 * k], across[k]], () if k else done)
        first[k] = send(mine[k], hop(0, (0, 2)))
    done = make_units(1, mine[PAIRS - 1])
    for k in range(PAIRS):
        [going] = pick([WAITS], [mine[k], first[k]], () if k else done)
        second[k] = send(going, hop(1, (0, 2)))
    for k in range(PAIRS):
        [going] = pick([WAITS], [mine[k], second[k]], done if k else ())
        third[k] = send(going, hop(2, (0, 2)))
        if k == 0:
            done = make_units(2, going)
    for k in range(PAIRS):
        [held[k]] = pick([REACHED], [mine[k], first[k], second[k], third[k]])
    done = make_units(3, held[PAIRS - 1])
    chosen = []
    for k in range(PAIRS):
        other = send(held[k], each([(0, 2), (2, 0)]))
        core_held = send(held[k], each([(0, 1), (2, 3)]))
        core_other = send(other, each([(0, 1), (2, 3)]))
        pair = pick(
            [LOW, HIGH], [held[k], core_held, other, core_other], () if k else done
        )
        for n in range(len(fresh)):
            moves = each([(w, w + (4 << n)) for w in range(4 << n)])
            pair = [pick([FRESH + n], [value, send(value, moves)])[0] for value in pair]
        chosen += pair

    delta = jnp.reshape(index * shard - start, (1,)).astype(jnp.int32)
    whole_chunk = pl.BlockSpec((ROWS, step), lambda i: (0, 0))
    half_flops = ROWS * shard * width
    parts = len(units)
    partial = pl.pallas_call(
        functools.partial(partial_kernel, 0, parts),
        in_specs=[vmem] * (2 + parts),
        out_specs=vmem,
        out_shape=jax.ShapeDtypeStruct((shard, ROWS), jnp.float32),
        compiler_params=params(16),
        cost_estimate=cost(half_flops, shard * width),
        name="part_cosines",
    )(chosen[0], chosen[1], *units)
    by_col, by_row, factors, local_penalty = pl.pallas_call(
        functools.partial(weight_kernel, 1, parts),
        in_specs=[smem] + [vmem] * (3 + 2 * parts),
        out_specs=[vmem] * 4,
        out_shape=[
            jax.ShapeDtypeStruct((shard, ROWS), jnp.bfloat16),
            jax.ShapeDtypeStruct((ROWS, shard), jnp.bfloat16),
            jax.ShapeDtypeStruct((shard, 128), jnp.float32),
            jax.ShapeDtypeStruct((8, 128), jnp.float32),
        ],
        compiler_params=params(16),
        cost_estimate=cost(half_flops, shard * width),
        name="weights",
    )(delta, chosen[2], chosen[3], partial, *units, *inverses)

    core_side = within % 2
    plane_x = jnp.reshape((within // 2) % 2, (1,)).astype(jnp.int32)
    tall = ROWS + 8
    coded_type = jax.ShapeDtypeStruct((CODED_ROWS, piece // 2), jnp.int32)
    piece_type = jax.ShapeDtypeStruct((ROWS, piece), jnp.float32)
    tile_type = jax.ShapeDtypeStruct((8, 128), jnp.float32)
    merge_cost = cost(20 * ROWS * piece, 12 * ROWS * piece)

    def row_part(k, side):
        return pl.pallas_call(
            functools.partial(row_kernel, k, parts),
            in_specs=[smem] + [vmem] * (2 + parts),
            out_specs=vmem,
            out_shape=jax.ShapeDtypeStruct((tall, step), jnp.float32),
            compiler_params=params(24),
            cost_estimate=cost(half_flops // 2, shard * width // 2),
            name="row_part",
        )(jnp.reshape(side, (1,)).astype(jnp.int32), by_row, local_penalty, *units)

    def merge(kept, arrived, keep, ties=()):
        tiles = [piece_type, tile_type, coded_type] if keep else [coded_type]
        result = pl.pallas_call(
            functools.partial(merge_kernel, len(arrived), keep),
            in_specs=[vmem] * (2 + len(arrived)) + [any_spec] * len(ties),
            out_specs=[vmem] * len(tiles),
            out_shape=tiles,
            compiler_params=params(24),
            cost_estimate=merge_cost,
            name="merge",
        )(*kept, *arrived, *ties)
        return (tuple(result[:2]), result[2]) if keep else result[0]

    kept, msg = [None] * PAIRS, [None] * PAIRS
    for k in range(PAIRS):
        away, near = row_part(k, 1 - core_side), row_part(k, core_side)
        far = per // 2
        while far >= 4:
            moves = each([(w + far, w) for w in range(far)])
            away, near = away + send(away, moves), near + send(near, moves)
            far //= 2
        rest, tile, msg[k] = pl.pallas_call(
            split_kernel,
            in_specs=[smem, vmem, vmem],
            out_specs=[vmem, vmem, vmem],
            out_shape=[piece_type, tile_type, coded_type],
            compiler_params=params(24),
            cost_estimate=merge_cost,
            name="split",
        )(plane_x, near, send(away, across_core))
        kept[k] = (rest, tile)

    out_type = jax.ShapeDtypeStruct((shard, width), jnp.float32)
    mark_type = jax.ShapeDtypeStruct((8, 128), jnp.float32)
    mark_spec = pl.BlockSpec((8, 128), lambda i: (0, 0))
    bounds = [1 + (blocks - 1) * p // 7 for p in (0, 2, 4, 5, 5, 7)]
    grad = None

    def finish(part, tie):
        nonlocal grad
        low, high = bounds[part], bounds[part + 1]
        if high == low:
            return []
        operands = [by_col, decoder, factors, *chosen]
        specs = [
            pl.BlockSpec((BLOCK, ROWS), lambda i: (i + low, 0)),
            pl.BlockSpec((BLOCK, width), lambda i: (i + low, 0)),
            pl.BlockSpec((BLOCK, 128), lambda i: (i + low, 0)),
        ] + [whole_chunk] * COUNT
        operands.append(tie)
        specs.append(any_spec)
        aliases = {}
        if grad is not None:
            aliases = {len(operands): 0}
            operands.append(grad)
            specs.append(any_spec)
        rows = (high - low) * BLOCK
        grad, mark = pl.pallas_call(
            finish_kernel,
            grid=(high - low,),
            in_specs=specs,
            out_specs=[pl.BlockSpec((BLOCK, width), lambda i: (i + low, 0)), mark_spec],
            out_shape=[out_type, mark_type],
            input_output_aliases=aliases,
            compiler_params=params(50),
            cost_estimate=cost(2 * ROWS * rows * width, 6 * rows * width),
            name="finish",
        )(*operands)
        return [mark]

    lanes = range(4)
    across = [send(msg[k], across_x) for k in range(PAIRS)]
    ties = finish(0, msg[PAIRS - 1])
    for k in range(PAIRS):
        kept[k], msg[k] = merge(kept[k], [across[k]], True, () if k else ties)
    arrivals = [[] for _ in range(PAIRS)]
    for level in range(3):
        for k in range(PAIRS):
            arrivals[k].append(send(msg[k], hop(level, lanes)))
        ties = finish(level + 1, msg[PAIRS - 1])
        for k in range(PAIRS):
            tied = () if k else ties
            if level < 2:
                msg[k] = merge(kept[k], arrivals[k][-1:], False, tied)
            else:
                kept[k], msg[k] = merge(kept[k], arrivals[k], True, tied)

    tile = kept[0][1]
    far = 4
    while far < per:
        moves = each([(w, w + far) for w in range(far)])
        fresh = (within >= far) & (within < 2 * far)
        tile = jnp.where(fresh, send(tile, moves), tile)
        far *= 2

    finish(4, msg[PAIRS - 1])
    sums, row_specs = [], []
    narrow = BLOCK // 2
    for k in range(PAIRS):
        sums.append(kept[k][0])
        row_specs.append(pl.BlockSpec((narrow, piece), lambda i: (i, 0)))
        arrivals = [send(msg[k], each([(source, 0)])) for source in (2, 3, 1)]
        for arrived in (arrivals[0], arrivals[2], arrivals[1]):
            sums += [arrived, arrived]
            row_specs += [
                pl.BlockSpec((narrow, piece // 2), lambda i: (i, 0)),
                pl.BlockSpec((8, piece // 2), lambda i: (ROWS // 8, 0)),
            ]

    owner = jnp.reshape(here & (within == 0), (1,)).astype(jnp.int32)
    operands = [owner, by_col, decoder, factors, tile, *chosen, *sums]
    specs = [
        smem,
        pl.BlockSpec((narrow, ROWS), lambda i: (i, 0)),
        pl.BlockSpec((narrow, width), lambda i: (i, 0)),
        pl.BlockSpec((narrow, 128), lambda i: (i, 0)),
        pl.BlockSpec((8, 128), lambda i: (0, 0)),
    ]
    specs += [whole_chunk] * COUNT
    specs += row_specs
    aliases = {}
    if grad is not None:
        aliases = {len(operands): 0}
        operands.append(grad)
        specs.append(any_spec)
    decoder_grad, penalty = pl.pallas_call(
        functools.partial(last_kernel, DW / (ROWS * latents)),
        grid=(2,),
        in_specs=specs,
        out_specs=[pl.BlockSpec((narrow, width), lambda i: (i, 0)), smem],
        out_shape=[out_type, jax.ShapeDtypeStruct((1,), jnp.float32)],
        scratch_shapes=[pltpu.VMEM((narrow, width), jnp.float32)],
        input_output_aliases=aliases,
        compiler_params=params(50),
        name="finish_rows",
    )(*operands)

    return (penalty, decoder_grad)


def solution(mesh):
    in_specs = (P(("groups", "row"), None), P("groups"))
    out_specs = (P("groups"), P(("groups", "row"), None))
    return jax.shard_map(
        on_device, mesh=mesh, in_specs=in_specs, out_specs=out_specs, check_vma=False
    )
```

```python
import functools
import math

import jax
import jax.numpy as jnp
from jax import lax
from jax.experimental import pallas as pl
from jax.experimental.pallas import tpu as pltpu
from jax.sharding import PartitionSpec as P

DW = 4096
ROWS = 256
BLOCK = 256
WIDE = 512
PAIRS = 2
COUNT = 2 * PAIRS
MIB = 1024 * 1024
NT = (((1,), (1,)), ((), ()))


def params(mib):
    return pltpu.CompilerParams(vmem_limit_bytes=mib * MIB)


def cost(flops, moved):
    return pl.CostEstimate(flops=flops, bytes_accessed=moved, transcendentals=0)


def strip_inverse(ref, rows):
    width = ref.shape[1]
    total = None
    for t in range(0, width, 128):
        v = ref[rows, t : t + 128].astype(jnp.float32)
        total = v * v if total is None else total + v * v
    return 1.0 / jnp.sqrt(jnp.sum(total, axis=1, keepdims=True) + 1e-06)


def head_kernel(flags_ref, decoder_ref, *refs):
    chunk_refs, (held, sems) = refs[:COUNT], refs[COUNT:]
    step = chunk_refs[0].shape[1]
    strip = ROWS // 4

    def fetch(j):
        rows = pl.ds(j * strip, strip)
        return pltpu.make_async_copy(decoder_ref.at[rows, :], held.at[rows, :], sems.at[j])

    for j in range(4):
        fetch(j).start()
    for j in range(4):
        fetch(j).wait()
        rows = slice(j * strip, (j + 1) * strip)
        inverse = strip_inverse(held, rows)
        for k, ref in enumerate(chunk_refs):
            for t in range(0, step, 128):
                v = held[rows, k * step + t : k * step + t + 128].astype(jnp.float32)
                ref[rows, t : t + 128] = (v * inverse).astype(jnp.bfloat16)


def units_kernel(low, count, away, decoder_ref, *refs):
    strip = 64
    if away:
        _, target_ref, inverse_ref, held, sems, units_ref, out_sems = refs
    else:
        _, units_ref, inverse_ref, held, sems = refs

    def leave(j):
        rows = pl.ds(j * BLOCK, BLOCK)
        return pltpu.make_async_copy(
            units_ref.at[rows, :], target_ref.at[rows, :], out_sems.at[j]
        )

    def fetch(j):
        return pltpu.make_async_copy(
            decoder_ref.at[pl.ds((low + j) * BLOCK, BLOCK), :], held.at[j % 2], sems.at[j % 2]
        )

    fetch(0).start()
    for j in range(count):
        if j + 1 < count:
            fetch(j + 1).start()
        fetch(j).wait()
        block = held.at[j % 2]
        for base in range(0, BLOCK, strip):
            rows = slice(base, base + strip)
            to = slice(j * BLOCK + base, j * BLOCK + base + strip)
            inverse = strip_inverse(block, rows)
            inverse_ref[to, :] = jnp.broadcast_to(inverse, (strip, 128))
            for t in range(0, block.shape[1], 128):
                v = block[rows, t : t + 128].astype(jnp.float32)
                units_ref[to, t : t + 128] = (v * inverse).astype(jnp.bfloat16)
        if away:
            leave(j).start()
    if away:
        for j in range(count):
            leave(j).wait()


def pair_cosines(k, units_ref, rows, low_ref, high_ref):
    step = low_ref.shape[1]
    base = 2 * k * step
    low = lax.dot_general(
        units_ref[rows, base : base + step],
        low_ref[...],
        NT,
        preferred_element_type=jnp.float32,
    )
    high = lax.dot_general(
        units_ref[rows, base + step : base + 2 * step],
        high_ref[...],
        NT,
        preferred_element_type=jnp.float32,
    )
    return low + high


def pick_kernel(slots, count, flags_ref, *refs):
    out_refs, sems = refs[-len(slots) - 1 : -1], refs[-1]
    for n, (slot, out_ref) in enumerate(zip(slots, out_refs)):
        for c in range(count):

            @pl.when(flags_ref[slot] == c)
            def _(out_ref=out_ref, c=c, n=n):
                pltpu.make_async_copy(refs[c], out_ref, sems.at[n]).start()

    for n, out_ref in enumerate(out_refs):
        pltpu.make_async_copy(refs[0], out_ref, sems.at[n]).wait()


def partial_kernel(k, parts, low_ref, high_ref, *refs):
    out_ref = refs[-1]
    base = 0
    for units_ref in refs[:parts]:
        count = units_ref.shape[0]
        size = min(WIDE, count)

        def body(j, carry, units_ref=units_ref, size=size, base=base):
            rows = pl.ds(pl.multiple_of(j * size, size), size)
            to = pl.ds(pl.multiple_of(base + j * size, size), size)
            out_ref[to, :] = pair_cosines(k, units_ref, rows, low_ref, high_ref)
            return carry

        lax.fori_loop(0, count // size, body, 0)
        base += count


def weight_kernel(k, parts, delta_ref, low_ref, high_ref, partial_ref, *refs):
    col_ref, row_ref, factor_ref, penalty_ref = refs[-4:]
    penalty_ref[...] = jnp.zeros_like(penalty_ref)
    base = 0
    for units_ref, inverse_ref in zip(refs[:parts], refs[parts : 2 * parts]):
        count = units_ref.shape[0]
        size = min(WIDE, count)

        def body(j, carry, units_ref=units_ref, inverse_ref=inverse_ref, size=size, base=base):
            here = pl.ds(pl.multiple_of(j * size, size), size)
            first = base + j * size
            span = pl.ds(pl.multiple_of(first, size), size)
            cosines = partial_ref[span, :] + pair_cosines(k, units_ref, here, low_ref, high_ref)
            latents = lax.broadcasted_iota(jnp.int32, (size, ROWS), 0) + (delta_ref[0] + first)
            rows = lax.broadcasted_iota(jnp.int32, (size, ROWS), 1)
            inside = (latents >= 0) & (latents < ROWS)
            weight = jnp.where(latents == rows, 0.0, jnp.where(inside, 0.5, 1.0))
            products = weight * cosines
            weighted = products.astype(jnp.bfloat16)
            col_ref[span, :] = weighted
            row_ref[:, span] = products.T.astype(jnp.bfloat16)
            along = jnp.sum(weighted.astype(jnp.float32) * cosines, axis=1, keepdims=True)
            inverse = inverse_ref[here, :]
            lanes = lax.broadcasted_iota(jnp.int32, (size, 128), 1)
            factor_ref[span, :] = jnp.where(lanes < 64, inverse, along * inverse)
            squares = products * cosines
            squares = squares[:, :128] + squares[:, 128:]
            penalty_ref[...] += jnp.sum(squares.reshape(size // 8, 8, 128), axis=0)
            return carry

        lax.fori_loop(0, count // size, body, 0)
        base += count


def row_kernel(k, parts, side_ref, row_ref, penalty_ref, *refs):
    out_ref = refs[-1]
    tile = out_ref.shape[1] // 2
    first = (2 * k + side_ref[0]) * out_ref.shape[1]
    for i in range(2):
        span = pl.ds(pl.multiple_of(first + i * tile, tile), tile)
        total, base = None, 0
        for units_ref in refs[:parts]:
            count = units_ref.shape[0]
            part = jnp.dot(
                row_ref[:, base : base + count],
                units_ref[:, span],
                preferred_element_type=jnp.float32,
            )
            total = part if total is None else total + part
            base += count
        out_ref[:ROWS, i * tile : (i + 1) * tile] = total
    out_ref[ROWS:, :] = jnp.concatenate([penalty_ref[...]] * (out_ref.shape[1] // 128), axis=1)


def finish_kernel(col_ref, decoder_ref, factor_ref, *refs):
    chunks = refs[:COUNT]
    out_ref, mark_ref = refs[-2:]
    step = chunks[0].shape[1]
    scale = (2.0 * math.sqrt(DW)) * factor_ref[:, :1]
    back = scale * factor_ref[:, 64:65]
    for k in range(COUNT):
        span = slice(k * step, (k + 1) * step)
        part = jnp.dot(col_ref[...], chunks[k][...], preferred_element_type=jnp.float32)
        out_ref[:, span] = scale * part - back * decoder_ref[:, span].astype(jnp.float32)
    mark_ref[...] = jnp.zeros_like(mark_ref)


STEPS = 32000.0
CODED_ROWS = ROWS + 16
PENALTY_STEPS = float(1 << 23)


def pack(coded):
    half = coded.shape[1] // 2
    return (coded[:, :half] << 16) | (coded[:, half:] & 0xFFFF)


def unpack(words):
    both = jnp.concatenate([words >> 16, (words << 16) >> 16], axis=1)
    return both.astype(jnp.float32)


def encode(value, penalty, msg_ref):
    top = jnp.max(jnp.abs(value), axis=0, keepdims=True)
    power = jnp.ceil(jnp.log2(jnp.maximum(top, 1e-35)) * 8.0)
    ratio = value * jnp.exp2(power * -0.125)
    coded = ratio * lax.rsqrt(jnp.maximum(jnp.abs(ratio), 1e-30))
    msg_ref[:ROWS, :] = pack(jnp.round(coded * STEPS).astype(jnp.int32))
    power = pack(power.astype(jnp.int32))
    msg_ref[ROWS : ROWS + 8, :] = jnp.broadcast_to(power, (8, power.shape[1]))
    top = jnp.max(jnp.max(penalty, axis=1, keepdims=True), axis=0, keepdims=True)
    power = jnp.ceil(jnp.log2(jnp.maximum(top, 1e-35)))
    coded = jnp.round(penalty * (jnp.exp2(-power) * PENALTY_STEPS)).astype(jnp.int32)
    msg_ref[ROWS + 8 :, :128] = coded
    msg_ref[ROWS + 8 :, 128:] = jnp.broadcast_to(power.astype(jnp.int32), (8, 128))


def decode(words, powers):
    coded = unpack(words)
    scale = jnp.exp2(unpack(powers)[:1, :] * 0.125) * (1.0 / (STEPS * STEPS))
    return coded * jnp.abs(coded) * scale


def decode_at(msg_ref):
    value = decode(msg_ref[:ROWS, :], msg_ref[ROWS : ROWS + 8, :])
    power = msg_ref[ROWS + 8 :, 128:].astype(jnp.float32)
    penalty = msg_ref[ROWS + 8 :, :128].astype(jnp.float32) * (jnp.exp2(power) / PENALTY_STEPS)
    return value, penalty


def split_kernel(odd_ref, mine_ref, theirs_ref, kept_ref, penalty_ref, msg_ref):
    piece = kept_ref.shape[1]
    penalty = mine_ref[ROWS:, :128] + theirs_ref[ROWS:, :128]
    penalty_ref[...] = penalty
    low, high = slice(0, piece), slice(piece, 2 * piece)

    def divide(keep, away):
        kept_ref[...] = mine_ref[:ROWS, keep] + theirs_ref[:ROWS, keep]
        encode(mine_ref[:ROWS, away] + theirs_ref[:ROWS, away], penalty, msg_ref)

    @pl.when(odd_ref[0] == 0)
    def _():
        divide(low, high)

    @pl.when(odd_ref[0] == 1)
    def _():
        divide(high, low)


def merge_kernel(arrived, keep, kept_ref, penalty_ref, *refs):
    value, penalty = kept_ref[...], penalty_ref[...]
    for msg_ref in refs[:arrived]:
        more, more_penalty = decode_at(msg_ref)
        value, penalty = value + more, penalty + more_penalty
    if keep:
        refs[-3][...] = value
        refs[-2][...] = penalty
    encode(value, penalty, refs[-1])


def last_kernel(share, owner_ref, col_ref, decoder_ref, factor_ref, tile_ref, *refs):
    chunks, sums = refs[:COUNT], refs[COUNT : COUNT + 7 * PAIRS]
    out_ref, penalty_ref, column = refs[-3:]
    penalty_ref[0] = jnp.sum(tile_ref[...]) * share
    step = chunks[0].shape[1]
    piece = step // 2
    owner = owner_ref[0] == 1
    total = jnp.zeros((col_ref.shape[0], 128), jnp.float32)
    for k in range(COUNT):
        span = slice(k * step, (k + 1) * step)
        part = jnp.dot(col_ref[...], chunks[k][...], preferred_element_type=jnp.float32)
        own, *coded = sums[7 * (k // 2) : 7 * (k // 2) + 7]
        pieces = [own[...]] + [
            decode(coded[2 * p][...], coded[2 * p + 1][...]) for p in range(3)
        ]
        row_sum = jnp.concatenate(pieces[2 * (k % 2) : 2 * (k % 2) + 2], axis=1)
        part = part + jnp.where(owner, row_sum, 0.0)
        column[:, span] = part
        along = part * decoder_ref[:, span].astype(jnp.float32)
        for t in range(0, step, 128):
            total = total + along[:, t : t + 128]
    inverse = factor_ref[:, :1]
    scale = (2.0 * math.sqrt(DW)) * inverse
    back = scale * (jnp.sum(total, axis=1, keepdims=True) * inverse * inverse)
    for k in range(COUNT):
        span = slice(k * step, (k + 1) * step)
        out_ref[:, span] = scale * column[:, span] - back * decoder_ref[:, span].astype(
            jnp.float32
        )


def on_device(decoder, quarter):
    shard, width = decoder.shape
    devices = lax.axis_size("row")
    index = lax.axis_index("row")
    per = devices // 4
    latents = shard * devices
    blocks = shard // BLOCK
    step = width // COUNT
    chosen_quarter = quarter[0]
    start = chosen_quarter * (latents // 4)
    place = index // per
    within = index % per
    here = place == chosen_quarter
    even_chip = (within // 2) % 2 == 0
    smem = pl.BlockSpec(memory_space=pltpu.SMEM)

    def send(value, pairs):
        return lax.ppermute(value, "row", pairs)

    def each(moves):
        return [(z * per + a, z * per + b) for z in range(4) for a, b in moves]

    near = jnp.where(place == 1, chosen_quarter == 0, chosen_quarter == 3)
    middle = (place == 1) | (place == 2)
    reached = jnp.where(here, 0, jnp.where(middle, jnp.where(near, 1, 2), 3))
    core_index = within % 2
    fresh = [(within >= 4 << n) & (within < 8 << n) for n in range((per // 4).bit_length() - 1)]
    TAKES, WAITS, REACHED, LOW, HIGH, FRESH = range(6)
    flags = jnp.stack(
        [
            jnp.where(within == 2, 1, 0),
            jnp.where(here, 0, 1),
            reached,
            jnp.where(even_chip, 0, 2) + core_index,
            jnp.where(even_chip, 2, 0) + core_index,
        ]
        + [jnp.where(value, 1, 0) for value in fresh]
    ).astype(jnp.int32)

    pinned = pl.BlockSpec(memory_space=pl.ANY)
    any_spec = pinned
    vmem = pl.BlockSpec(memory_space=pltpu.VMEM)
    chunk_type = jax.ShapeDtypeStruct((ROWS, step), jnp.bfloat16)
    own = pl.pallas_call(
        head_kernel,
        in_specs=[smem, pinned],
        out_specs=[vmem] * COUNT,
        out_shape=[chunk_type] * COUNT,
        scratch_shapes=[
            pltpu.VMEM((ROWS, width), jnp.bfloat16),
            pltpu.SemaphoreType.DMA((4,)),
        ],
        compiler_params=params(50),
        cost_estimate=cost(4 * ROWS * width, 4 * ROWS * width),
        name="head_units",
    )(flags, decoder)

    across_x = each([(0, 2), (2, 0), (1, 3), (3, 1)])
    across_core = each([(0, 1), (1, 0), (2, 3), (3, 2)])
    piece = step // 2

    def hop(level, lanes):
        moves = (((0, 1), (3, 2)), ((1, 2), (2, 1)), ((2, 3), (1, 0)))[level]
        return [(a * per + w, b * per + w) for a, b in moves for w in lanes]

    def pick(slots, candidates, ties=()):
        return pl.pallas_call(
            functools.partial(pick_kernel, slots, len(candidates)),
            in_specs=[smem] + [any_spec] * (len(candidates) + len(ties)),
            out_specs=[vmem] * len(slots),
            out_shape=[chunk_type] * len(slots),
            scratch_shapes=[pltpu.SemaphoreType.DMA((len(slots),))],
            compiler_params=params(12),
            cost_estimate=cost(ROWS * step, 4 * ROWS * step),
            name="pick",
        )(flags, *candidates, *ties)

    unit_bounds = [blocks * p // 4 for p in range(5)]
    units, inverses = [], []

    def make_units(part, tie):
        low, high = unit_bounds[part], unit_bounds[part + 1]
        if high == low:
            return []
        rows = (high - low) * BLOCK
        away = part < 4
        extra = [
            pltpu.VMEM((rows, width), jnp.bfloat16),
            pltpu.SemaphoreType.DMA((high - low,)),
        ]
        made = pl.pallas_call(
            functools.partial(units_kernel, low, high - low, away),
            in_specs=[pinned, any_spec],
            out_specs=[pl.BlockSpec(memory_space=pltpu.HBM) if away else vmem, vmem],
            out_shape=[
                jax.ShapeDtypeStruct((rows, width), jnp.bfloat16),
                jax.ShapeDtypeStruct((rows, 128), jnp.float32),
            ],
            scratch_shapes=[
                pltpu.VMEM((2, BLOCK, width), jnp.bfloat16),
                pltpu.SemaphoreType.DMA((2,)),
            ]
            + (extra if away else []),
            compiler_params=params(50),
            cost_estimate=cost(4 * rows * width, 4 * rows * width),
            name="units",
        )(decoder, tie)
        units.append(made[0])
        inverses.append(made[1])
        return [made[1]]

    mine, first, second, third, held = ([None] * PAIRS for _ in range(5))
    across = [send(own[2 * k + 1], each([(0, 2)])) for k in range(PAIRS)]
    done = make_units(0, own[0])
    for k in range(PAIRS):
        [mine[k]] = pick([TAKES], [own[2 * k], across[k]], () if k else done)
        first[k] = send(mine[k], hop(0, (0, 2)))
    done = make_units(1, mine[PAIRS - 1])
    for k in range(PAIRS):
        [going] = pick([WAITS], [mine[k], first[k]], () if k else done)
        second[k] = send(going, hop(1, (0, 2)))
    for k in range(PAIRS):
        [going] = pick([WAITS], [mine[k], second[k]], done if k else ())
        third[k] = send(going, hop(2, (0, 2)))
        if k == 0:
            done = make_units(2, going)
    for k in range(PAIRS):
        [held[k]] = pick([REACHED], [mine[k], first[k], second[k], third[k]])
    done = make_units(3, held[PAIRS - 1])
    chosen = []
    for k in range(PAIRS):
        other = send(held[k], each([(0, 2), (2, 0)]))
        core_held = send(held[k], each([(0, 1), (2, 3)]))
        core_other = send(other, each([(0, 1), (2, 3)]))
        pair = pick(
            [LOW, HIGH], [held[k], core_held, other, core_other], () if k else done
        )
        for n in range(len(fresh)):
            moves = each([(w, w + (4 << n)) for w in range(4 << n)])
            pair = [pick([FRESH + n], [value, send(value, moves)])[0] for value in pair]
        chosen += pair

    delta = jnp.reshape(index * shard - start, (1,)).astype(jnp.int32)
    whole_chunk = pl.BlockSpec((ROWS, step), lambda i: (0, 0))
    half_flops = ROWS * shard * width
    parts = len(units)
    partial = pl.pallas_call(
        functools.partial(partial_kernel, 0, parts),
        in_specs=[vmem] * (2 + parts),
        out_specs=vmem,
        out_shape=jax.ShapeDtypeStruct((shard, ROWS), jnp.float32),
        compiler_params=params(16),
        cost_estimate=cost(half_flops, shard * width),
        name="part_cosines",
    )(chosen[0], chosen[1], *units)
    by_col, by_row, factors, local_penalty = pl.pallas_call(
        functools.partial(weight_kernel, 1, parts),
        in_specs=[smem] + [vmem] * (3 + 2 * parts),
        out_specs=[vmem] * 4,
        out_shape=[
            jax.ShapeDtypeStruct((shard, ROWS), jnp.bfloat16),
            jax.ShapeDtypeStruct((ROWS, shard), jnp.bfloat16),
            jax.ShapeDtypeStruct((shard, 128), jnp.float32),
            jax.ShapeDtypeStruct((8, 128), jnp.float32),
        ],
        compiler_params=params(16),
        cost_estimate=cost(half_flops, shard * width),
        name="weights",
    )(delta, chosen[2], chosen[3], partial, *units, *inverses)

    core_side = within % 2
    plane_x = jnp.reshape((within // 2) % 2, (1,)).astype(jnp.int32)
    tall = ROWS + 8
    coded_type = jax.ShapeDtypeStruct((CODED_ROWS, piece // 2), jnp.int32)
    piece_type = jax.ShapeDtypeStruct((ROWS, piece), jnp.float32)
    tile_type = jax.ShapeDtypeStruct((8, 128), jnp.float32)
    merge_cost = cost(20 * ROWS * piece, 12 * ROWS * piece)

    def row_part(k, side):
        return pl.pallas_call(
            functools.partial(row_kernel, k, parts),
            in_specs=[smem] + [vmem] * (2 + parts),
            out_specs=vmem,
            out_shape=jax.ShapeDtypeStruct((tall, step), jnp.float32),
            compiler_params=params(24),
            cost_estimate=cost(half_flops // 2, shard * width // 2),
            name="row_part",
        )(jnp.reshape(side, (1,)).astype(jnp.int32), by_row, local_penalty, *units)

    def merge(kept, arrived, keep, ties=()):
        tiles = [piece_type, tile_type, coded_type] if keep else [coded_type]
        result = pl.pallas_call(
            functools.partial(merge_kernel, len(arrived), keep),
            in_specs=[vmem] * (2 + len(arrived)) + [any_spec] * len(ties),
            out_specs=[vmem] * len(tiles),
            out_shape=tiles,
            compiler_params=params(24),
            cost_estimate=merge_cost,
            name="merge",
        )(*kept, *arrived, *ties)
        return (tuple(result[:2]), result[2]) if keep else result[0]

    kept, msg = [None] * PAIRS, [None] * PAIRS
    for k in range(PAIRS):
        away, near = row_part(k, 1 - core_side), row_part(k, core_side)
        far = per // 2
        while far >= 4:
            moves = each([(w + far, w) for w in range(far)])
            away, near = away + send(away, moves), near + send(near, moves)
            far //= 2
        rest, tile, msg[k] = pl.pallas_call(
            split_kernel,
            in_specs=[smem, vmem, vmem],
            out_specs=[vmem, vmem, vmem],
            out_shape=[piece_type, tile_type, coded_type],
            compiler_params=params(24),
            cost_estimate=merge_cost,
            name="split",
        )(plane_x, near, send(away, across_core))
        kept[k] = (rest, tile)

    out_type = jax.ShapeDtypeStruct((shard, width), jnp.float32)
    mark_type = jax.ShapeDtypeStruct((8, 128), jnp.float32)
    mark_spec = pl.BlockSpec((8, 128), lambda i: (0, 0))
    bounds = [1 + (blocks - 1) * p // 7 for p in (0, 2, 4, 5, 5, 7)]
    grad = None

    def finish(part, tie):
        nonlocal grad
        low, high = bounds[part], bounds[part + 1]
        if high == low:
            return []
        operands = [by_col, decoder, factors, *chosen]
        specs = [
            pl.BlockSpec((BLOCK, ROWS), lambda i: (i + low, 0)),
            pl.BlockSpec((BLOCK, width), lambda i: (i + low, 0)),
            pl.BlockSpec((BLOCK, 128), lambda i: (i + low, 0)),
        ] + [whole_chunk] * COUNT
        operands.append(tie)
        specs.append(any_spec)
        aliases = {}
        if grad is not None:
            aliases = {len(operands): 0}
            operands.append(grad)
            specs.append(any_spec)
        rows = (high - low) * BLOCK
        grad, mark = pl.pallas_call(
            finish_kernel,
            grid=(high - low,),
            in_specs=specs,
            out_specs=[pl.BlockSpec((BLOCK, width), lambda i: (i + low, 0)), mark_spec],
            out_shape=[out_type, mark_type],
            input_output_aliases=aliases,
            compiler_params=params(50),
            cost_estimate=cost(2 * ROWS * rows * width, 6 * rows * width),
            name="finish",
        )(*operands)
        return [mark]

    lanes = range(4)
    across = [send(msg[k], across_x) for k in range(PAIRS)]
    ties = finish(0, msg[PAIRS - 1])
    for k in range(PAIRS):
        kept[k], msg[k] = merge(kept[k], [across[k]], True, () if k else ties)
    arrivals = [[] for _ in range(PAIRS)]
    for level in range(3):
        for k in range(PAIRS):
            arrivals[k].append(send(msg[k], hop(level, lanes)))
        ties = finish(level + 1, msg[PAIRS - 1])
        for k in range(PAIRS):
            tied = () if k else ties
            if level < 2:
                msg[k] = merge(kept[k], arrivals[k][-1:], False, tied)
            else:
                kept[k], msg[k] = merge(kept[k], arrivals[k], True, tied)

    tile = kept[0][1]
    far = 4
    while far < per:
        moves = each([(w, w + far) for w in range(far)])
        fresh = (within >= far) & (within < 2 * far)
        tile = jnp.where(fresh, send(tile, moves), tile)
        far *= 2

    finish(4, msg[PAIRS - 1])
    sums, row_specs = [], []
    narrow = BLOCK // 2
    for k in range(PAIRS):
        sums.append(kept[k][0])
        row_specs.append(pl.BlockSpec((narrow, piece), lambda i: (i, 0)))
        arrivals = [send(msg[k], each([(source, 0)])) for source in (2, 3, 1)]
        for arrived in (arrivals[0], arrivals[2], arrivals[1]):
            sums += [arrived, arrived]
            row_specs += [
                pl.BlockSpec((narrow, piece // 2), lambda i: (i, 0)),
                pl.BlockSpec((8, piece // 2), lambda i: (ROWS // 8, 0)),
            ]

    owner = jnp.reshape(here & (within == 0), (1,)).astype(jnp.int32)
    operands = [owner, by_col, decoder, factors, tile, *chosen, *sums]
    specs = [
        smem,
        pl.BlockSpec((narrow, ROWS), lambda i: (i, 0)),
        pl.BlockSpec((narrow, width), lambda i: (i, 0)),
        pl.BlockSpec((narrow, 128), lambda i: (i, 0)),
        pl.BlockSpec((8, 128), lambda i: (0, 0)),
    ]
    specs += [whole_chunk] * COUNT
    specs += row_specs
    aliases = {}
    if grad is not None:
        aliases = {len(operands): 0}
        operands.append(grad)
        specs.append(any_spec)
    decoder_grad, penalty = pl.pallas_call(
        functools.partial(last_kernel, DW / (ROWS * latents)),
        grid=(2,),
        in_specs=specs,
        out_specs=[pl.BlockSpec((narrow, width), lambda i: (i, 0)), smem],
        out_shape=[out_type, jax.ShapeDtypeStruct((1,), jnp.float32)],
        scratch_shapes=[pltpu.VMEM((narrow, width), jnp.float32)],
        input_output_aliases=aliases,
        compiler_params=params(50),
        name="finish_rows",
    )(*operands)

    return (penalty, decoder_grad)


def solution(mesh):
    in_specs = (P(("groups", "row"), None), P("groups"))
    out_specs = (P("groups"), P(("groups", "row"), None))
    return jax.shard_map(
        on_device, mesh=mesh, in_specs=in_specs, out_specs=out_specs, check_vma=False
    )
```
